32 devices in a mesh: section: 2 (over z_hi), context: 8 (over y, x, core), tensor: 2 (over z_lo).
Axes of the slice: x: 2, y: 2, z: 4 (z_hi: 2, z_lo: 2; z = z_hi * 2 + z_lo), core: 2. Of those that a mesh axis runs over, the one named last changes fastest.
Arguments:
- block_input: bfloat16 [4, 1024, 1536], P(None, 'context'), may hold values from -6 to 6
- norm_gain: float32 [2, 1536], P('section'), may hold values from 0.1 to 1.9
- w_gate: bfloat16 [2, 1536, 3072], P('section', 'context', 'tensor'), may hold values from -0.15625 to 0.15625
- w_value: bfloat16 [2, 1536, 3072], P('section', 'context', 'tensor'), may hold values from -0.15625 to 0.15625
- w_bc: bfloat16 [2, 1536, 256], P('section', 'context'), may hold values from -0.15625 to 0.15625
- w_dt: bfloat16 [2, 1536, 48], P('section', 'context', 'tensor'), may hold values from -0.15625 to 0.15625
- conv_value: float32 [2, 4, 3072], P('section', None, 'tensor'), may hold values from -3 to 3
- conv_bc: float32 [2, 4, 256], P('section'), may hold values from -3 to 3
- conv_value_bias: float32 [2, 3072], P('section', 'tensor'), may hold values from -3 to 3
- conv_bc_bias: float32 [2, 256], P('section'), may hold values from -3 to 3
- dt_bias: float32 [2, 48], P('section', 'tensor'), may hold values from -5 to -3
- decay_log: float32 [2, 48], P('section', 'tensor'), may hold values from -5.3 to 0.7
- skip: float32 [2, 48], P('section', 'tensor'), may hold values from 0.5 to 2
- gate_gain: float32 [2, 3072], P('section', 'tensor'), may hold values from 0.1 to 1.9
- w_out: bfloat16 [2, 3072, 1536], P('section', 'tensor', 'context'), may hold values from -0.109375 to 0.109375
- cotangent: bfloat16 [4, 1024, 1536], P(None, 'context'), may hold values from -6 to 6
Outputs:
- section_outputs: bfloat16 [2, 4, 1024, 1536], P('section', None, 'context')
- section_input_grads: float32 [2, 4, 1024, 1536], P('section', None, 'context')
- norm_gain_grad: float32 [2, 1536], P('section')
- w_gate_grad: float32 [2, 1536, 3072], P('section', 'context', 'tensor')
- w_value_grad: float32 [2, 1536, 3072], P('section', 'context', 'tensor')
- w_bc_grad: float32 [2, 1536, 256], P('section', 'context')
- w_dt_grad: float32 [2, 1536, 48], P('section', 'context', 'tensor')
- conv_value_grad: float32 [2, 4, 3072], P('section', None, 'tensor')
- conv_bc_grad: float32 [2, 4, 256], P('section')
- conv_value_bias_grad: float32 [2, 3072], P('section', 'tensor')
- conv_bc_bias_grad: float32 [2, 256], P('section')
- dt_bias_grad: float32 [2, 48], P('section', 'tensor')
- decay_log_grad: float32 [2, 48], P('section', 'tensor')
- skip_grad: float32 [2, 48], P('section', 'tensor')
- gate_gain_grad: float32 [2, 3072], P('section', 'tensor')
- w_out_grad: float32 [2, 3072, 1536], P('section', 'tensor', 'context')
The draws below stay inside these ranges and needn't reach their ends.
All inputs are finite; a program needn't handle non-finite values.
Results may differ from the reference program's by a relative error of at most 0.019.
Values may be sent and summed in bfloat16 or wider, within the bound.
No kernel may reach another device: no remote copies, remote signals or barrier semaphores. Data moves between devices by JAX's collectives and lax.ppermute only.
A program may use at most 256 MiB of HBM per device.

```python
import math
import jax
import jax.numpy as jnp
from jax import lax

D = 1536
HEADS = 48
HEAD_DIM = 64
STATE = 128
CONV = 4
MICRO = 4
INNER = 3072
LENGTH = 1024
N_SECTION = 2


def block_scale(key, dims, cuts, low, top_value):
    level, own = 1.0, jax.random.fold_in(key, 6)
    for position, shards_of in cuts:
        heights = jnp.exp(jax.random.uniform(jax.random.fold_in(own, position), (shards_of,), jnp.float32, low / len(cuts), top_value / len(cuts)))
        level = level * jnp.repeat(heights, dims[position] // shards_of).reshape([-1 if axis == position else 1 for axis in range(len(dims))])
    return level


def normal_values(own_key, extent, deviation, bound, split=(), kind=jnp.bfloat16):
    factor_of = block_scale(own_key, extent, split, -0.22, 0.18) if split else 1.0
    values = jax.random.normal(own_key, extent, jnp.float32) * deviation * factor_of
    return jnp.minimum(jnp.maximum(values, -bound), bound).astype(kind)


def setup_inputs(seed: int = 0) -> dict:
    splits = jax.random.split(jax.random.key(seed), 17)
    block_input = normal_values(splits[0], (MICRO, LENGTH, D), 1.0, 6.0, ((1, 8),))
    norm_gain = jnp.clip(1.0 + 0.18 * jax.random.normal(splits[1], (N_SECTION, D), jnp.float32), 0.1, 1.9)
    w_gate = normal_values(splits[2], (N_SECTION, D, INNER), D ** -0.5, 0.15625, ((0, 2), (1, 8), (2, 2)))
    w_value = normal_values(splits[3], (N_SECTION, D, INNER), D ** -0.5, 0.15625, ((0, 2), (1, 8), (2, 2)))
    w_bc = normal_values(splits[4], (N_SECTION, D, 2 * STATE), D ** -0.5, 0.15625, ((0, 2), (1, 8)))
    w_dt = normal_values(splits[5], (N_SECTION, D, HEADS), D ** -0.5, 0.15625, ((0, 2), (1, 8), (2, 2)))
    conv_value = normal_values(splits[6], (N_SECTION, CONV, INNER), CONV ** -0.5, 3.0, ((0, 2), (2, 2)), jnp.float32)
    conv_bc = normal_values(splits[7], (N_SECTION, CONV, 2 * STATE), CONV ** -0.5, 3.0, ((0, 2),), jnp.float32)
    conv_value_bias = normal_values(splits[8], (N_SECTION, INNER), 0.5, 3.0, ((0, 2), (1, 2)), jnp.float32)
    conv_bc_bias = normal_values(splits[9], (N_SECTION, 2 * STATE), 0.5, 3.0, ((0, 2),), jnp.float32)
    dt_bias = jnp.clip(-5.0 + 2.0 * jax.random.uniform(splits[10], (N_SECTION, HEADS), jnp.float32) ** block_scale(splits[10], (N_SECTION, HEADS), ((0, 2), (1, 2)), -0.2, 0.2), -5.0, -3.0)
    decay_log = jnp.clip(-5.3 + 6 * jax.random.uniform(splits[11], (N_SECTION, HEADS), jnp.float32) ** block_scale(splits[11], (N_SECTION, HEADS), ((0, 2), (1, 2)), -0.2, 0.2), -5.3, 0.7)
    skip = jnp.clip(0.5 + 1.5 * jax.random.uniform(splits[12], (N_SECTION, HEADS), jnp.float32) ** block_scale(splits[12], (N_SECTION, HEADS), ((0, 2), (1, 2)), -0.2, 0.2), 0.5, 2.0)
    gate_gain = jnp.clip(1.0 + 0.18 * jax.random.normal(splits[13], (N_SECTION, INNER), jnp.float32), 0.1, 1.9)
    w_out = normal_values(splits[14], (N_SECTION, INNER, D), INNER ** -0.5, 0.109375, ((0, 2), (1, 2), (2, 8)))
    cotangent = normal_values(splits[15], (MICRO, LENGTH, D), 1.0, 6.0, ((1, 8),))
    return dict(block_input=block_input, norm_gain=norm_gain, w_gate=w_gate, w_value=w_value, w_bc=w_bc, w_dt=w_dt, conv_value=conv_value, conv_bc=conv_bc, conv_value_bias=conv_value_bias, conv_bc_bias=conv_bc_bias, dt_bias=dt_bias, decay_log=decay_log, skip=skip, gate_gain=gate_gain, w_out=w_out, cotangent=cotangent)


@jax.custom_vjp
def low(v):
    return lax.optimization_barrier(v.astype(jnp.bfloat16)).astype(jnp.float32)

@jax.custom_vjp
def low_back(v):
    return v

def low_keep(v):
    return (low(v), None)

def low_pass(kept, grad):
    return (grad,)

def back_keep(v):
    return (v, None)

def back_low(kept, grad):
    return (low(grad),)
low.defvjp(low_keep, low_pass)
low_back.defvjp(back_keep, back_low)
epsilon = 1e-05
highest = lax.Precision.HIGHEST

def mult(left, right):
    return jnp.dot(left, right, precision=highest, preferred_element_type=jnp.float32)

def conv_apply(mixed_pre, border, kernel, kernel_bias):
    token_count = mixed_pre.shape[0]
    padded = jnp.concatenate([border, mixed_pre], axis=0)
    running = kernel_bias[None, :]
    for tap_index in range(CONV):
        running = running + kernel[tap_index][None, :] * padded[tap_index:tap_index + token_count]
    return jax.nn.silu(running)

def split_mixed(mixed, head_count):
    inner_width = head_count * HEAD_DIM
    token_count = mixed.shape[0]
    values = mixed[:, :inner_width].reshape(token_count, head_count, HEAD_DIM)
    return (values, mixed[:, inner_width:inner_width + STATE], mixed[:, inner_width + STATE:])

def decay_rates(step_pre, step_bias, decay_log):
    step_size = jax.nn.softplus(step_pre + step_bias[None, :])
    log_decay = jnp.cumsum(-jnp.exp(decay_log)[None, :] * step_size, axis=0)
    return (step_size, log_decay)

def summaries(values, input_map, step_size, log_decay):
    total_decay = jnp.exp(log_decay[-1])
    weight_rows = jnp.exp(log_decay[-1][None, :] - log_decay) * step_size
    end_state = jnp.einsum('th,thp,tn->hpn', weight_rows, values, input_map, precision=highest)
    return (total_decay, end_state)

def outputs(values, input_map, output_map, step_size, log_decay, skip_gain, state_in):
    token_count = log_decay.shape[0]
    positions = jnp.arange(token_count)
    causal = (positions[:, None] >= positions[None, :])[:, :, None]
    log_gap = log_decay[:, None, :] - log_decay[None, :, :]
    decay = jnp.where(causal, jnp.exp(jnp.where(causal, log_gap, 0.0)), 0.0)
    contact = jnp.einsum('tn,sn->ts', output_map, input_map, precision=highest)
    mixing = decay * contact[:, :, None] * step_size[None, :, :]
    inside = jnp.einsum('tsh,shp->thp', mixing, values, precision=highest)
    carried = jnp.exp(log_decay)[:, :, None] * jnp.einsum('tn,hpn->thp', output_map, state_in, precision=highest)
    result = inside + carried + skip_gain[None, :, None] * values
    return result.reshape(token_count, -1)

def scan_ssm(mixed, step_pre, step_bias, decay_log, skip_gain):
    token_count = mixed.shape[0]
    block_size = math.gcd(token_count, 256)
    block_count = token_count // block_size
    values, input_map, output_map = split_mixed(mixed, HEADS)

    def one_block(state, pieces):
        block_values, block_in, block_out, block_pre = pieces
        step_size, log_decay = decay_rates(block_pre, step_bias, decay_log)
        result = outputs(block_values, block_in, block_out, step_size, log_decay, skip_gain, state)
        total_decay, end_state = summaries(block_values, block_in, step_size, log_decay)
        return (total_decay[:, None, None] * state + end_state, result)
    pieces = (values.reshape(block_count, block_size, HEADS, HEAD_DIM), input_map.reshape(block_count, block_size, STATE), output_map.reshape(block_count, block_size, STATE), step_pre.reshape(block_count, block_size, HEADS))
    start = jnp.zeros((HEADS, HEAD_DIM, STATE), mixed.dtype)
    _, results = lax.scan(jax.checkpoint(one_block), start, pieces)
    return results.reshape(token_count, HEADS * HEAD_DIM)

def layer(residual, params):
    norm_in, gate_w, value_w, maps_w, step_w, conv_values, conv_maps, conv_values_bias, conv_maps_bias, step_bias, decay_log, skip_gain, gate_gain, out_w = params
    in_scale = lax.rsqrt(lax.optimization_barrier(jnp.mean(residual * residual, axis=1, keepdims=True)) + epsilon)
    normed_in = low(residual * in_scale * norm_in[None, :])
    gate_pre = low_back(mult(normed_in, gate_w))
    value_pre = low_back(mult(normed_in, value_w))
    maps_pre = low_back(mult(normed_in, maps_w))
    step_pre = low_back(mult(normed_in, step_w))
    mixed_pre = jnp.concatenate([value_pre, maps_pre], axis=1)
    kernel = jnp.concatenate([conv_values, conv_maps], axis=1)
    kernel_bias = jnp.concatenate([conv_values_bias, conv_maps_bias], axis=0)
    border = jnp.zeros((CONV - 1, mixed_pre.shape[1]), mixed_pre.dtype)
    mixed = conv_apply(mixed_pre, border, kernel, kernel_bias)
    ssm_out = scan_ssm(mixed, step_pre, step_bias, decay_log, skip_gain)
    gated = ssm_out * jax.nn.silu(gate_pre)
    gate_scale = lax.rsqrt(lax.optimization_barrier(jnp.mean(gated * gated, axis=1, keepdims=True)) + epsilon)
    gate_normed = low(gated * gate_scale * gate_gain[None, :])
    branch = low_back(mult(gate_normed, out_w))
    return residual + branch

def reference(block_input, norm_gain, w_gate, w_value, w_bc, w_dt, conv_value, conv_bc, conv_value_bias, conv_bc_bias, dt_bias, decay_log, skip, gate_gain, w_out, cotangent):
    weights = tuple((item.astype(jnp.float32) for item in (norm_gain, w_gate, w_value, w_bc, w_dt, conv_value, conv_bc, conv_value_bias, conv_bc_bias, dt_bias, decay_log, skip, gate_gain, w_out)))
    section_count = norm_gain.shape[0]
    totals = [tuple((jnp.zeros_like(item[section_index]) for item in weights)) for section_index in range(section_count)]
    section_rows = [[] for section_index in range(section_count)]
    grad_rows = [[] for section_index in range(section_count)]
    for micro_index in range(MICRO):
        residual = block_input[micro_index].astype(jnp.float32)
        pullbacks = []
        for section_index in range(section_count):
            params = tuple((item[section_index] for item in weights))
            result, pullback = jax.vjp(layer, residual, params)
            pullbacks.append(pullback)
            section_rows[section_index].append(result.astype(jnp.bfloat16))
            residual = low(result)
        out_grad = cotangent[micro_index].astype(jnp.float32)
        for section_index in reversed(range(section_count)):
            grad_in, grad_params = pullbacks[section_index](out_grad)
            grad_rows[section_index].append(grad_in)
            totals[section_index] = jax.tree.map(jnp.add, totals[section_index], grad_params)
            out_grad = low(grad_in)
    section_outputs = jnp.stack([jnp.stack(rows) for rows in section_rows])
    input_grads = jnp.stack([jnp.stack(rows) for rows in grad_rows])
    grads = [jnp.stack([totals[section_index][field] for section_index in range(section_count)]) for field in range(len(weights))]
    return (section_outputs, input_grads, grads[0], grads[1], grads[2], grads[3], grads[4], grads[5], grads[6], grads[7], grads[8], grads[9], grads[10], grads[11], grads[12], grads[13])
```

```python
import functools

import jax
import jax.numpy as jnp
from jax import lax
from jax.experimental import pallas as pl
from jax.experimental.pallas import tpu as pltpu
from jax.sharding import PartitionSpec as P

HEAD_DIM = 64
STATE = 128
CONV = 4
MAPS = 2 * STATE
CHUNK = 128
LANES = 128
PIECES = 2

epsilon = 1e-05
bf16 = jnp.bfloat16
f32 = jnp.float32


def low_dot(a, b, contract):
    return lax.dot_general(
        a.astype(bf16), b.astype(bf16), ((contract[0], contract[1]), ((), ())), preferred_element_type=f32
    )


def mm(a, b):
    return low_dot(a, b, ((1,), (0,)))


def mm_nt(a, b):
    return low_dot(a, b, ((1,), (1,)))


def mm_tn(a, b):
    return low_dot(a, b, ((0,), (0,)))


def softplus(v):
    return jnp.maximum(v, 0.0) + jnp.log(1.0 + jnp.exp(-jnp.abs(v)))


def groups_of(width):
    return [
        (at, min(LANES, width - at), at // HEAD_DIM, min(LANES, width - at) // HEAD_DIM)
        for at in range(0, width, LANES)
    ]


def head_rows(width):
    return -(-(width // HEAD_DIM) // 16) * 16


def column(cols, head):
    return jnp.broadcast_to(cols[:, head : head + 1], (cols.shape[0], LANES))


def choose(first, second, lanes):
    if second is None:
        return first[:, :lanes]
    lane = lax.broadcasted_iota(jnp.int32, (first.shape[0], lanes), 1)
    return jnp.where(lane < HEAD_DIM, first, second)


def only(value, which, count):
    if count == 1:
        return value
    lane = lax.broadcasted_iota(jnp.int32, value.shape, 1)
    return jnp.where((lane < HEAD_DIM) == (which == 0), value, jnp.zeros_like(value))


def pieces_of(value, count):
    terms = []
    for _ in range(count):
        term = value.astype(bf16)
        terms.append(term)
        value = value - term.astype(f32)
    return terms


def mm3(a, b):
    (a_hi, a_lo), (b_hi, b_lo) = pieces_of(a, 2), pieces_of(b, 2)
    return mm(jnp.concatenate([a_hi, a_lo, a_hi], axis=1), jnp.concatenate([b_hi, b_hi, b_lo], axis=0))


def mm3_nt(a, b):
    (a_hi, a_lo), (b_hi, b_lo) = pieces_of(a, 2), pieces_of(b, 2)
    return mm_nt(jnp.concatenate([a_hi, a_lo, a_hi], axis=1), jnp.concatenate([b_hi, b_hi, b_lo], axis=1))


def sum_dot(value, zero_one, count):
    return sum(mm(term, zero_one) for term in pieces_of(value, count))


def iotas():
    row = lax.broadcasted_iota(jnp.int32, (CHUNK, CHUNK), 0)
    col = lax.broadcasted_iota(jnp.int32, (CHUNK, CHUNK), 1)
    return row, col


def conv_rows(pad, taps_ref, at, lanes):
    here = slice(at, at + lanes)
    pre = taps_ref[CONV : CONV + 1, here] + taps_ref[CONV - 1 : CONV, here] * pad[8 : 8 + CHUNK, here]
    for k in range(CONV - 1):
        first = 8 - (CONV - 1) + k
        pre = pre + taps_ref[k : k + 1, here] * pad[first : first + CHUNK, here]
    return pre


def decay_terms(dt_pre, heads_ref, rows, row, col):
    wide = dt_pre.T[:rows] + heads_ref[0:rows, :]
    dt = softplus(wide)
    log_decay = sum_dot(-heads_ref[rows : 2 * rows, :] * dt, (row <= col).astype(bf16), 3)
    cols = jnp.concatenate([log_decay, dt, jnp.zeros((CHUNK - 2 * rows, CHUNK), f32)], axis=0).T
    return wide, dt, log_decay, cols


def as_row(value):
    return jnp.sum(value.T, axis=0, keepdims=True)


def filled(value):
    rows, lanes = value.shape
    if lanes == LANES:
        return value
    return jnp.concatenate([value, jnp.zeros((rows, LANES - lanes), f32)], axis=1)


def as_column(row):
    return jnp.broadcast_to(row, (CHUNK, LANES)).T


def deal(part, parts, first, count, total, own_ref, send_ref):
    def one(c, _):
        index = first + c
        distance = (index % parts) ^ part
        rows = total[pl.ds(pl.multiple_of(c * CHUNK, CHUNK), CHUNK), :]

        @pl.when(distance == 0)
        def _():
            own_ref[index // parts] = rows

        @pl.when(distance != 0)
        def _():
            send_ref[jnp.maximum(distance - 1, 0), index // parts] = rows.astype(send_ref.dtype)

        return 0

    lax.fori_loop(0, count, one, 0)


def forward_kernel(keep, width, parts, per_step, part_ref, h_ref, w1_ref, wg_ref, wo_ref, norm_ref, taps_ref, heads_ref, inner_ref, s0_ref, tail0_ref, *rest):
    if keep:
        dn_ref, own_ref, send_ref, sums_ref, st_ref, tail_ref, xn_ref, vbd_ref, z_ref, y_ref, sin_ref, pad, gg, total = rest
    else:
        g_ref, sums_ref, st_ref, tail_ref, xn_ref, vbd_ref, z_ref, pad = rest
    mixed = width + MAPS
    rows = head_rows(width)
    step = pl.program_id(0)

    @pl.when(step == 0)
    def _():
        st_ref[...] = s0_ref[...]
        tail_ref[...] = tail0_ref[...]

    def norm(c, _):
        here = pl.ds(pl.multiple_of(c * 64, 64), 64)
        hf = h_ref[here, :].astype(f32)
        scale = lax.rsqrt(jnp.mean(hf * hf, axis=1, keepdims=True) + epsilon)
        xn_ref[here, :] = (hf * scale * norm_ref[...]).astype(bf16)
        return 0

    lax.fori_loop(0, per_step * 2, norm, 0)
    vbd_ref[...] = jnp.dot(xn_ref[...], w1_ref[...], preferred_element_type=f32)
    z_ref[...] = jnp.dot(xn_ref[...], wg_ref[...], preferred_element_type=f32)
    row, col = iotas()

    def chunk(c, _):
        here = pl.ds(pl.multiple_of(c * CHUNK, CHUNK), CHUNK)
        pad[0:8, :] = tail_ref[...]
        pad[8 : 8 + CHUNK, :] = vbd_ref[here, :mixed]
        tail_ref[...] = pad[CHUNK : CHUNK + 8, :]
        pre = conv_rows(pad, taps_ref, width, MAPS)
        maps = pre * jax.nn.sigmoid(pre)
        b, c_map = maps[:, :STATE], maps[:, STATE:]
        b_rows = b.T
        _, _, log_row, cols = decay_terms(vbd_ref[here, mixed:], heads_ref, rows, row, col)
        contact = jnp.where(row >= col, mm3(c_map, b_rows), 0.0)
        if keep:
            sin_ref[c] = st_ref[...]
        carried = mm3(c_map, st_ref[...])
        squares = jnp.zeros((CHUNK, LANES), f32)
        pulls = jnp.zeros((CHUNK, LANES), f32)
        for at, lanes, head, count in groups_of(width):
            span = slice(at, at + lanes)
            pre = conv_rows(pad, taps_ref, at, lanes)
            own = pre * jax.nn.sigmoid(pre)
            logs = [column(cols, head + j) for j in range(count)]
            steps = [column(cols, rows + head + j) for j in range(count)]
            log_x = choose(logs[0], logs[-1] if count == 2 else None, lanes)
            step_x = choose(steps[0], steps[-1] if count == 2 else None, lanes)
            last_x = log_x[CHUNK - 1 : CHUNK, :]
            xd = own * step_x
            mixing = [
                jnp.exp(jnp.minimum(logs[j] - log_row[head + j : head + j + 1, :], 0.0)) * contact
                for j in range(count)
            ]
            inside = mm3(
                jnp.concatenate(mixing, axis=1),
                jnp.concatenate([only(xd, j, count) for j in range(count)], axis=0),
            )
            y = inside + jnp.exp(log_x) * carried[:, span] + inner_ref[0:1, span] * own
            st_ref[:, span] = jnp.exp(last_x) * st_ref[:, span] + mm3(b_rows, jnp.exp(last_x - log_x) * xd)
            z = z_ref[here, span]
            g = y * (z * jax.nn.sigmoid(z))
            if keep:
                gg[here, span] = (g * inner_ref[1:2, span]).astype(bf16)
                y_ref[here, span] = y
            else:
                g_ref[here, span] = g
            squares = squares + filled(g * g)
            if keep:
                pulls = pulls + filled(dn_ref[here, span] * inner_ref[1:2, span] * g)
        sums_ref[0, c] = as_row(squares)
        if keep:
            sums_ref[1, c] = as_row(pulls)
        return 0

    lax.fori_loop(0, per_step, chunk, 0)
    if keep:
        total[...] = lax.dot_general(
            gg[...], wo_ref[...], (((1,), (1,)), ((), ())), preferred_element_type=f32
        )
        deal(part_ref[0], parts, step * per_step, per_step, total, own_ref, send_ref)


def out_kernel(parts, per_step, part_ref, g_ref, q_ref, inner_ref, wo_ref, own_ref, send_ref, n, total):
    def chunk(c, _):
        here = pl.ds(pl.multiple_of(c * CHUNK, CHUNK), CHUNK)
        q = as_column(q_ref[c])
        for at, lanes, _, _ in groups_of(n.shape[1]):
            span = slice(at, at + lanes)
            n[here, span] = (g_ref[here, span] * q[:, :lanes] * inner_ref[1:2, span]).astype(bf16)
        return 0

    lax.fori_loop(0, per_step, chunk, 0)
    total[...] = lax.dot_general(n[...], wo_ref[...], (((1,), (1,)), ((), ())), preferred_element_type=f32)
    deal(part_ref[0], parts, pl.program_id(0) * per_step, per_step, total, own_ref, send_ref)


def out_call(place, g, q, weights, inner):
    wo = weights[2]
    tokens, width = g.shape
    depth = wo.shape[0]
    chunks = tokens // CHUNK
    per_step = min(STEP, chunks)
    steps = chunks // per_step
    count = per_step * CHUNK
    blocks = chunks // place.parts
    shapes = [(blocks, CHUNK, depth), (place.parts - 1, blocks, CHUNK, depth)]
    return pl.pallas_call(
        functools.partial(out_kernel, place.parts, per_step),
        grid_spec=pltpu.PrefetchScalarGridSpec(
            num_scalar_prefetch=1,
            grid=(steps,),
            in_specs=[
                block(steps, (count, width), lambda i, _: (i, 0)),
                block(steps, (per_step, 1, LANES), lambda i, _: (i, 0, 0)),
                once(inner.shape),
                once(wo.shape),
            ],
            out_specs=[once(shape) for shape in shapes],
            scratch_shapes=[pltpu.VMEM((count, width), bf16), pltpu.VMEM((count, depth), f32)],
        ),
        out_shape=[jax.ShapeDtypeStruct(shape, f32) for shape in shapes],
        compiler_params=kernel_params(steps, 8),
        cost_estimate=pl.CostEstimate(
            flops=tokens * width * 6000, bytes_accessed=tokens * depth * 8, transcendentals=0
        ),
        name="out_forward",
    )(place.part.reshape(1), g, q[:, None], inner, wo)


STEP = 4
GAIN_ROW = CONV + 1
HEAD_ROW = CONV + 2


def kernel_params(steps, megabytes):
    return pltpu.CompilerParams(vmem_limit_bytes=(megabytes if steps == 1 else 40) * 1024 * 1024)


def once(shape):
    return pl.BlockSpec(memory_space=pltpu.VMEM)


def block(steps, shape, index_map):
    return once(shape) if steps == 1 else pl.BlockSpec(shape, index_map)


def forward_call(place, h, weights, small, s0, tail0, dn=None):
    w1, wg, wo = weights
    norm_gain, taps, heads, inner = small
    keep = dn is not None
    tokens, depth = h.shape
    width = inner.shape[1]
    mixed = width + MAPS
    chunks = tokens // CHUNK
    per_step = min(STEP, chunks)
    steps = chunks // per_step
    count = per_step * CHUNK
    blocks = chunks // place.parts
    rows = lambda lanes: block(steps, (count, lanes), lambda i, _: (i, 0))
    if keep:
        shapes = [((blocks, CHUNK, depth), f32), ((place.parts - 1, blocks, CHUNK, depth), bf16)]
        out_shape = [jax.ShapeDtypeStruct(*item) for item in shapes]
        out_specs = [once(shape) for shape, _ in shapes]
    else:
        out_shape = [jax.ShapeDtypeStruct((tokens, width), f32)]
        out_specs = [rows(width)]
    out_shape += [
        jax.ShapeDtypeStruct((2, chunks, 1, LANES), f32),
        jax.ShapeDtypeStruct((STATE, width), f32),
        jax.ShapeDtypeStruct((8, mixed), f32),
    ]
    out_specs += [
        block(steps, (2, per_step, 1, LANES), lambda i, _: (0, i, 0, 0)),
        once((STATE, width)),
        once((8, mixed)),
    ]
    in_specs = [
        rows(depth),
        once(w1.shape),
        once(wg.shape),
        once(wo.shape),
        once((1, depth)),
        once(taps.shape),
        once(heads.shape),
        once(inner.shape),
        once(s0.shape),
        once(tail0.shape),
    ]
    args = [h, w1, wg, wo, norm_gain[None], taps, heads, inner, s0, tail0]
    held = [((tokens, depth), bf16), ((tokens, w1.shape[1]), f32), ((tokens, width), f32)]
    scratch = []
    if keep:
        in_specs.append(rows(width))
        args.append(dn)
        held.append(((tokens, width), f32))
        out_shape += [jax.ShapeDtypeStruct(*item) for item in held]
        out_specs += [rows(shape[1]) for shape, _ in held]
        out_shape.append(jax.ShapeDtypeStruct((chunks, STATE, width), f32))
        out_specs.append(block(steps, (per_step, STATE, width), lambda i, _: (i, 0, 0)))
    else:
        scratch = [pltpu.VMEM((count, shape[1]), kind) for shape, kind in held]
    scratch.append(pltpu.VMEM((CHUNK + 8, mixed), f32))
    if keep:
        scratch += [pltpu.VMEM((count, width), bf16), pltpu.VMEM((count, depth), f32)]
    return pl.pallas_call(
        functools.partial(forward_kernel, keep, width, place.parts, per_step),
        grid_spec=pltpu.PrefetchScalarGridSpec(
            num_scalar_prefetch=1, grid=(steps,), in_specs=in_specs, out_specs=out_specs, scratch_shapes=scratch
        ),
        out_shape=out_shape,
        compiler_params=kernel_params(steps, 10 if keep else 11),
        cost_estimate=pl.CostEstimate(
            flops=tokens * width * 40000, bytes_accessed=tokens * depth * 16, transcendentals=0
        ),
        name="section_forward",
    )(place.part.reshape(1), *args)


def normal_kernel(full, width, per_step, e_ref, wo_ref, z_ref, y_ref, q_ref, inner_ref, dn_ref, pull_ref, n_ref, gain_ref, gains):
    dn_ref[...] = jnp.dot(e_ref[...], wo_ref[...], preferred_element_type=f32)

    @pl.when(pl.program_id(0) == 0)
    def _():
        gains[...] = jnp.zeros_like(gains)

    def chunk(c, _):
        here = pl.ds(pl.multiple_of(c * CHUNK, CHUNK), CHUNK)
        q = as_column(q_ref[c])
        pulls = jnp.zeros((CHUNK, LANES), f32)
        for at, lanes, _, _ in groups_of(width):
            span = slice(at, at + lanes)
            z, dn_x, gain = z_ref[here, span], dn_ref[here, span], inner_ref[1:2, span]
            g = y_ref[here, span] * (z * jax.nn.sigmoid(z))
            gq = g * q[:, :lanes]
            pulls = pulls + filled(dn_x * gain * g)
            n_ref[here, span] = (gq * gain).astype(bf16)
            gains[:, span] += fold(dn_x * gq)
        pull_ref[c] = as_row(pulls)
        return 0

    lax.fori_loop(0, per_step, chunk, 0)
    gain_ref[...] = jnp.broadcast_to(jnp.sum(gains[...], axis=0, keepdims=True), gains.shape)


def gate_kernel(width, per_step, total, dn_ref, z_ref, y_ref, q_ref, pull_ref, inner_ref, dy_ref, dz_ref):
    def chunk(c, _):
        here = pl.ds(pl.multiple_of(c * CHUNK, CHUNK), CHUNK)
        q = as_column(q_ref[c])
        pull = as_column(pull_ref[c]) * (q * q * q) * (1.0 / total)
        for at, lanes, _, _ in groups_of(width):
            span = slice(at, at + lanes)
            z, y = z_ref[here, span], y_ref[here, span]
            sig = jax.nn.sigmoid(z)
            silu = z * sig
            dg = q[:, :lanes] * (dn_ref[here, span] * inner_ref[1:2, span]) - y * silu * pull[:, :lanes]
            dy_ref[here, span] = dg * silu
            dz_ref[here, span] = (dg * y * (sig + silu * (1.0 - sig))).astype(bf16)
        return 0

    lax.fori_loop(0, per_step, chunk, 0)


def normal_call(e, weights, z, y, q, inner):
    wo = weights[2]
    tokens, depth = e.shape
    width = inner.shape[1]
    chunks = tokens // CHUNK
    per_step = min(STEP, chunks)
    steps = chunks // per_step
    rows = lambda lanes: block(steps, (per_step * CHUNK, lanes), lambda i: (i, 0))
    lines = block(steps, (per_step, 1, LANES), lambda i: (i, 0, 0))
    return pl.pallas_call(
        functools.partial(normal_kernel, True, width, per_step),
        grid=(steps,),
        in_specs=[rows(depth), once(wo.shape), rows(width), rows(width), lines, once(inner.shape)],
        out_specs=[rows(width), lines, rows(width), once((8, width))],
        out_shape=[
            jax.ShapeDtypeStruct((tokens, width), f32),
            jax.ShapeDtypeStruct((chunks, 1, LANES), f32),
            jax.ShapeDtypeStruct((tokens, width), bf16),
            jax.ShapeDtypeStruct((8, width), f32),
        ],
        scratch_shapes=[pltpu.VMEM((8, width), f32)],
        compiler_params=kernel_params(steps, 4),
        cost_estimate=pl.CostEstimate(
            flops=tokens * width * 9000, bytes_accessed=tokens * depth * 16, transcendentals=0
        ),
        name="norm_backward",
    )(e, wo, z, y, q, inner)


def gate_call(place, dn, z, y, q, pull, inner):
    tokens, width = dn.shape
    chunks = tokens // CHUNK
    per_step = min(STEP, chunks)
    steps = chunks // per_step
    rows = lambda lanes: block(steps, (per_step * CHUNK, lanes), lambda i: (i, 0))
    lines = block(steps, (per_step, 1, LANES), lambda i: (i, 0, 0))
    return pl.pallas_call(
        functools.partial(gate_kernel, width, per_step, place.tensors * place.parts * width),
        grid=(steps,),
        in_specs=[rows(width), rows(width), rows(width), lines, lines, once(inner.shape)],
        out_specs=[rows(width), rows(width)],
        out_shape=[jax.ShapeDtypeStruct((tokens, width), f32), jax.ShapeDtypeStruct((tokens, width), bf16)],
        compiler_params=kernel_params(steps, 4),
        cost_estimate=pl.CostEstimate(
            flops=tokens * width * 6000, bytes_accessed=tokens * width * 16, transcendentals=0
        ),
        name="gate_backward",
    )(dn, z, y, q, pull, inner)


def fold(value):
    return jnp.sum(value.reshape(CHUNK // 8, 8, value.shape[1]), axis=0)


def backward_kernel(
    exact,
    width,
    parts,
    per_step,
    steps,
    part_ref,
    dy_ref,
    dz_ref,
    vbd_ref,
    before_ref,
    sin_ref,
    w1_ref,
    wg_ref,
    taps_ref,
    heads_ref,
    inner_ref,
    g0_ref,
    du0_ref,
    own_ref,
    send_ref,
    dvbd_ref,
    gt_ref,
    dut_ref,
    tapg_ref,
    pad,
    dpad,
    sums,
    y_in,
    dxd_out,
    dy_in_all,
    xd_out_all,
    total,
    taps_sum,
    headg_ref,
    skipg_ref,
    back_all,
):
    mixed = width + MAPS
    rows = head_rows(width)
    step = steps - 1 - pl.program_id(0)

    @pl.when(pl.program_id(0) == 0)
    def _():
        gt_ref[...] = g0_ref[...]
        dut_ref[...] = du0_ref[...]
        taps_sum[...] = jnp.zeros_like(taps_sum)
        headg_ref[...] = jnp.zeros_like(headg_ref)
        skipg_ref[...] = jnp.zeros_like(skipg_ref)

    row, col = iotas()
    causal = col >= row
    strict = col > row
    onward = (row >= col).astype(bf16)
    head_of = lax.broadcasted_iota(jnp.int32, (rows, width), 1) // HEAD_DIM
    ones = (head_of == lax.broadcasted_iota(jnp.int32, (rows, width), 0)).astype(bf16)

    def conv_back(here, at, lanes, du):
        span = slice(at, at + lanes)
        dpad[0:CHUNK, span] = du
        m = pad[8 : 8 + CHUNK, span]
        taps_sum[CONV * 8 : CONV * 8 + 8, span] += fold(du)
        taps_sum[CONV * 8 - 8 : CONV * 8, span] += fold(m * du)
        dm = taps_ref[CONV - 1 : CONV, span] * du
        for k in range(CONV - 1):
            first = CONV - 1 - k
            moved = dpad[first : first + CHUNK, span]
            dm = dm + taps_ref[k : k + 1, span] * moved
            taps_sum[k * 8 : k * 8 + 8, span] += fold(m * moved)
        dvbd_ref[here, span] = dm.astype(bf16)

    def chunk(reverse, _):
        c = per_step - 1 - reverse
        here = pl.ds(pl.multiple_of(c * CHUNK, CHUNK), CHUNK)
        dpad[CHUNK : CHUNK + 8, :] = dut_ref[...]
        pad[8 : 8 + CHUNK, :] = vbd_ref[here, :mixed]

        @pl.when(c == 0)
        def _():
            pad[0:8, :] = before_ref[0]

        @pl.when(c != 0)
        def _():
            pad[0:8, :] = vbd_ref[pl.ds(pl.multiple_of(jnp.maximum(c * CHUNK - 8, 0), 8), 8), :mixed]

        pre = conv_rows(pad, taps_ref, width, MAPS)
        sig = jax.nn.sigmoid(pre)
        maps = pre * sig
        maps_slope = sig + maps * (1.0 - sig)
        b_maps, c_maps = maps[:, :STATE], maps[:, STATE:]
        b_low, c_low = b_maps.astype(bf16), c_maps.astype(bf16)
        wide, dt, log_row, cols = decay_terms(vbd_ref[here, mixed:], heads_ref, rows, row, col)
        contact = jnp.where(causal, mm_nt(b_low, c_low), 0.0)
        back_low = gt_ref[...].astype(bf16)
        if exact:
            back_all[...] = gt_ref[...]
        c_rows = c_low.T
        y_in[...] = mm(c_low, sin_ref[c])
        dxd_out[...] = mm(b_low, back_low)
        dcontact = jnp.zeros((CHUNK, CHUNK), f32)
        log_rows, through = [], []
        for at, lanes, head, count in groups_of(width):
            span = slice(at, at + lanes)
            pre = conv_rows(pad, taps_ref, at, lanes)
            sig = jax.nn.sigmoid(pre)
            own = pre * sig
            slope = sig + own * (1.0 - sig)
            logs = [column(cols, head + j) for j in range(count)]
            steps_of = [column(cols, rows + head + j) for j in range(count)]
            log_x = choose(logs[0], logs[-1] if count == 2 else None, lanes)
            step_x = choose(steps_of[0], steps_of[-1] if count == 2 else None, lanes)
            last_x = log_x[CHUNK - 1 : CHUNK, :]
            dy = dy_ref[here, span]
            xd = own * step_x
            xd_low = xd.astype(bf16)
            dy_low = dy.astype(bf16)
            to_end = jnp.exp(last_x - log_x)
            dy_in = jnp.exp(log_x) * dy
            dy_in_low = dy_in.astype(bf16)
            if exact:
                dy_in_all[:, span] = dy_in
                xd_out_all[:, span] = to_end * xd
                dmix = mm3_nt(jnp.concatenate([only(xd, j, count) for j in range(count)], axis=0), dy)
            else:
                dy_in_all[:, span] = dy_in_low
                xd_out_all[:, span] = (to_end * xd).astype(bf16)
                dmix = mm_nt(jnp.concatenate([only(xd_low, j, count) for j in range(count)], axis=0), dy_low)
            mixing, products = [], []
            for j in range(count):
                decay = jnp.exp(jnp.minimum(log_row[head + j : head + j + 1, :] - logs[j], 0.0))
                one = decay * contact
                d_one = dmix[j * CHUNK : (j + 1) * CHUNK]
                dcontact = dcontact + decay * d_one
                mixing.append(one.astype(bf16))
                products.append((one * d_one).astype(bf16))
            dxd_in = mm(
                jnp.concatenate(mixing, axis=1),
                jnp.concatenate([only(dy_low, j, count) for j in range(count)], axis=0),
            )
            later = mm(jnp.concatenate(products, axis=0), onward)
            for j in range(count):
                log_rows.append(
                    jnp.sum(jnp.where(strict, later[j * CHUNK : (j + 1) * CHUNK], 0.0), axis=0, keepdims=True)
                )
            from_end = to_end * dxd_out[:, span]
            dxd = dxd_in + from_end
            sums[0:CHUNK, span] = (dy_in * y_in[:, span]).astype(bf16)
            sums[CHUNK : 2 * CHUNK, span] = (xd * from_end).astype(bf16)
            sums[2 * CHUNK : 3 * CHUNK, span] = (own * dxd).astype(bf16)
            carried = jnp.exp(last_x)
            back = gt_ref[:, span]
            through.append(
                jnp.sum(carried * sin_ref[c, :, span].astype(f32) * back, axis=0, keepdims=True)
            )
            skipg_ref[:, span] += fold(dy * own)
            gt_ref[:, span] = carried * back + mm(c_rows, dy_in_low)
            conv_back(here, at, lanes, (step_x * dxd + inner_ref[0:1, span] * dy) * slope)
        dcontact = jnp.where(causal, dcontact, 0.0)
        if exact:
            db = mm3_nt(xd_out_all[...], back_all[...]) + mm3(dcontact, c_maps)
            dc = mm3_nt(dy_in_all[...], sin_ref[c]) + mm3(dcontact.T, b_maps)
        else:
            db = mm_nt(xd_out_all[...], back_low) + mm(dcontact, c_low)
            dc = mm_nt(dy_in_all[...], sin_ref[c]) + mm_tn(dcontact, b_low)
        conv_back(here, width, STATE, db * maps_slope[:, :STATE])
        conv_back(here, width + STATE, STATE, dc * maps_slope[:, STATE:])
        dut_ref[...] = dpad[0:8, :]

        by_token = mm_nt(ones, sums[...])
        entering = by_token[:, :CHUNK]
        leaving = by_token[:, CHUNK : 2 * CHUNK]
        direct = by_token[:, 2 * CHUNK :]
        ends = jnp.broadcast_to(jnp.concatenate(through, axis=1), (CHUNK, width))
        ends = sum(mm_nt(ones, term) for term in pieces_of(ends, 2))
        inside = log_rows
        if rows > len(log_rows):
            inside = log_rows + [jnp.zeros((rows - len(log_rows), CHUNK), f32)]
        dlog = (
            jnp.concatenate(inside, axis=0)
            + sum_dot(entering, onward, 2)
            + sum_dot(leaving, (row < col).astype(bf16), 2)
            + ends
        )
        rate = heads_ref[rows : 2 * rows, :]
        ddt_pre = (direct - rate * dlog) * jax.nn.sigmoid(wide)
        headg_ref[0:rows, :] += ddt_pre
        headg_ref[rows : 2 * rows, :] += -rate * dt * dlog
        ddt_cols = jnp.concatenate([ddt_pre, jnp.zeros((CHUNK - rows, CHUNK), f32)], axis=0).T
        dvbd_ref[here, mixed:] = ddt_cols.astype(bf16)
        return 0

    lax.fori_loop(0, per_step, chunk, 0)
    nt = (((1,), (1,)), ((), ()))
    total[...] = lax.dot_general(dvbd_ref[...], w1_ref[...], nt, preferred_element_type=f32)
    total[...] += lax.dot_general(dz_ref[...], wg_ref[...], nt, preferred_element_type=f32)

    @pl.when(pl.program_id(0) == steps - 1)
    def _():
        tapg_ref[...] = jnp.zeros_like(tapg_ref)
        for k in range(CONV + 1):
            tapg_ref[k : k + 1, :] = jnp.sum(taps_sum[k * 8 : k * 8 + 8, :], axis=0, keepdims=True)
        skips = jnp.broadcast_to(jnp.sum(skipg_ref[...], axis=0, keepdims=True), (CHUNK, width))
        skips = sum(mm_nt(ones, term) for term in pieces_of(skips, 3))
        by_head = jnp.broadcast_to(jnp.sum(headg_ref[...], axis=1, keepdims=True), (2 * rows, LANES))
        columns = jnp.concatenate([by_head, skips, jnp.zeros((CHUNK - 3 * rows, LANES), f32)], axis=0)
        tapg_ref[HEAD_ROW : HEAD_ROW + 1, 0:LANES] = columns.T[0:1]

    deal(part_ref[0], parts, step * per_step, per_step, total, own_ref, send_ref)


def backward_call(place, exact, dy, dz, vbd, before, states, weights, small, g0, du0):
    w1, wg, _ = weights
    _, taps, heads, inner = small
    tokens, width = dy.shape
    depth = w1.shape[0]
    mixed = width + MAPS
    chunks = tokens // CHUNK
    per_step = min(STEP, chunks)
    steps = chunks // per_step
    count = per_step * CHUNK
    blocks = chunks // place.parts
    rows = lambda lanes: block(steps, (count, lanes), lambda i, _: (steps - 1 - i, 0))
    deep = lambda number, height, lanes: block(
        steps, (number, height, lanes), lambda i, _: (steps - 1 - i, 0, 0)
    )
    shapes = [
        ((STATE, width), f32),
        ((8, mixed), f32),
        ((8, mixed), f32),
    ]
    results = pl.pallas_call(
        functools.partial(backward_kernel, exact, width, place.parts, per_step, steps),
        grid_spec=pltpu.PrefetchScalarGridSpec(
            num_scalar_prefetch=1,
            grid=(steps,),
            in_specs=[
                rows(width),
                rows(width),
                rows(vbd.shape[1]),
                deep(1, 8, mixed),
                deep(per_step, STATE, width),
                once(w1.shape),
                once(wg.shape),
                once(taps.shape),
                once(heads.shape),
                once(inner.shape),
                once(g0.shape),
                once(du0.shape),
            ],
            out_specs=[
                once((blocks, CHUNK, depth)),
                once((place.parts - 1, blocks, CHUNK, depth)),
                rows(vbd.shape[1]),
            ]
            + [once(shape) for shape, _ in shapes],
            scratch_shapes=[
                pltpu.VMEM((CHUNK + 8, mixed), f32),
                pltpu.VMEM((CHUNK + 8, mixed), f32),
                pltpu.VMEM((3 * CHUNK, width), bf16),
                pltpu.VMEM((CHUNK, width), f32),
                pltpu.VMEM((CHUNK, width), f32),
                pltpu.VMEM((CHUNK, width), f32 if exact else bf16),
                pltpu.VMEM((CHUNK, width), f32 if exact else bf16),
                pltpu.VMEM((count, depth), f32),
                pltpu.VMEM((8 * (CONV + 1), mixed), f32),
                pltpu.VMEM((2 * head_rows(width), LANES), f32),
                pltpu.VMEM((8, width), f32),
                pltpu.VMEM((STATE, width), f32),
            ],
        ),
        out_shape=[
            jax.ShapeDtypeStruct((blocks, CHUNK, depth), f32),
            jax.ShapeDtypeStruct((place.parts - 1, blocks, CHUNK, depth), bf16),
            jax.ShapeDtypeStruct(vbd.shape, bf16),
        ]
        + [jax.ShapeDtypeStruct(*item) for item in shapes],
        compiler_params=kernel_params(steps, 12),
        cost_estimate=pl.CostEstimate(
            flops=tokens * width * 60000, bytes_accessed=tokens * depth * 16, transcendentals=0
        ),
        name="section_backward",
    )(place.part.reshape(1), dy, dz, vbd, before, states, w1, wg, taps, heads, inner, g0, du0)
    own, send, dvbd, gt, dut, sums = results
    return own, send, dvbd, gt, dut, sums


def unpack_kernel(parts, heads, rows, part_ref, both_ref, *refs):
    locals_ref, outs = refs[:parts], refs[parts:]
    wide_ref, bias_ref, gain_ref, maps_ref, maps_bias_ref, norm_ref, heads_ref = outs
    width = wide_ref.shape[1] // parts
    part = part_ref[0]
    lane = lax.broadcasted_iota(jnp.int32, (1, LANES), 1)
    by_head = [jnp.zeros((1, LANES), f32) for _ in range(3)]
    for d in range(parts):
        owner = part ^ d
        here = pl.ds(pl.multiple_of(owner * width, HEAD_DIM), width)
        ref = locals_ref[d]
        if width % LANES == 0:
            wide_ref[:, here] = ref[0:CONV, 0:width]
            bias_ref[:, here] = ref[CONV : CONV + 1, 0:width]
            gain_ref[:, here] = ref[GAIN_ROW : GAIN_ROW + 1, 0:width]
        else:
            for p in range(parts):

                @pl.when(owner == p)
                def _():
                    there = slice(p * width, (p + 1) * width)
                    wide_ref[:, there] = ref[0:CONV, 0:width]
                    bias_ref[:, there] = ref[CONV : CONV + 1, 0:width]
                    gain_ref[:, there] = ref[GAIN_ROW : GAIN_ROW + 1, 0:width]

        for k in range(3):
            values = ref[HEAD_ROW : HEAD_ROW + 1, 0:LANES]
            for p in range(parts):
                moved = pltpu.roll(values, (p * heads - k * rows) % LANES, 1)
                chosen = (owner == p) & (lane >= p * heads) & (lane < (p + 1) * heads)
                by_head[k] = jnp.where(chosen, moved, by_head[k])
    heads_ref[...] = jnp.concatenate(by_head + [jnp.zeros((5, LANES), f32)], axis=0)
    maps_ref[...] = both_ref[0:CONV, width : width + MAPS]
    maps_bias_ref[...] = both_ref[CONV : CONV + 1, width : width + MAPS]
    norm_ref[...] = both_ref[8:9, 0 : norm_ref.shape[1]]


def unpack(place, both, by_part, width, heads, depth):
    total = place.parts * width
    shapes = [(CONV, total), (1, total), (1, total), (CONV, MAPS), (1, MAPS), (1, depth), (8, LANES)]
    return pl.pallas_call(
        functools.partial(unpack_kernel, place.parts, heads, head_rows(width)),
        grid_spec=pltpu.PrefetchScalarGridSpec(
            num_scalar_prefetch=1,
            grid=(1,),
            in_specs=[once(both.shape)] * (1 + place.parts),
            out_specs=[once(shape) for shape in shapes],
        ),
        out_shape=[jax.ShapeDtypeStruct(shape, f32) for shape in shapes],
        compiler_params=pltpu.CompilerParams(vmem_limit_bytes=4 * 1024 * 1024),
        name="unpack_small",
    )(place.part.reshape(1), both, *by_part)


class Place:
    def __init__(self, micro_count):
        self.context = lax.axis_size("context")
        self.micros = micro_count
        self.parts = self.context // micro_count
        self.tensors = lax.axis_size("tensor")
        index = lax.axis_index("context")
        self.micro = index // self.parts
        self.part = index % self.parts
        self.tensor = lax.axis_index("tensor")

    def swap_part(self, block, mask):
        return lax.ppermute(block, "context", [(i, i ^ mask) for i in range(self.context)])

    def swap_micro(self, block, mask):
        return self.swap_part(block, mask * self.parts)

    def swap_tensor(self, block, mask):
        return lax.ppermute(block, "tensor", [(i, i ^ mask) for i in range(self.tensors)])

    def next_section(self, block, step, flip):
        count, tensors = lax.axis_size("section"), self.tensors
        return lax.ppermute(
            block,
            ("section", "tensor"),
            [
                (i * tensors + t, (i + step) * tensors + (t ^ flip))
                for i in range(count)
                if 0 <= i + step < count
                for t in range(tensors)
            ],
        )


def pick(array, index, axis):
    return lax.dynamic_index_in_dim(array, index, axis, False)


def tie(*items):
    return lax.optimization_barrier(items)


def bits_of(count):
    masks = []
    mask = 1
    while mask < count:
        masks.append(mask)
        mask *= 2
    return masks


def order(blocks, index, axis):
    count = len(blocks)
    shape = list(blocks[0].shape)
    shape.insert(axis, count)
    place = lax.broadcasted_iota(jnp.int32, shape, axis) ^ index
    result = jnp.expand_dims(blocks[0], axis)
    for d in range(1, count):
        result = jnp.where(place == d, jnp.expand_dims(blocks[d], axis), result)
    return jnp.broadcast_to(result, shape)


def beside(blocks, index):
    count = len(blocks)
    if count == 2:
        return jnp.where(
            index == 0, jnp.concatenate(blocks, axis=-1), jnp.concatenate(blocks[::-1], axis=-1)
        )
    return jnp.concatenate(
        [pick(order(blocks, index, 0), i, 0) for i in range(count)], axis=-1
    )


def sum_all(place, block, micro=True, part=True, tensor=True):
    if part:
        for mask in bits_of(place.parts):
            block = block + place.swap_part(block, mask)
    if tensor:
        for mask in bits_of(place.tensors):
            block = block + place.swap_tensor(block, mask)
    if micro:
        for mask in bits_of(place.micros):
            block = block + place.swap_micro(block, mask)
    return block


def lay_kernel(sizes, widths, places_ref, *refs):
    pieces, outs, sems = refs[: len(sizes)], refs[len(sizes) : -1], refs[-1]
    copies, number = [], 0
    for piece, size in zip(pieces, sizes):
        for row in range(size):
            at = 0
            for k, lanes in enumerate(widths):
                copies.append(
                    pltpu.make_async_copy(
                        piece.at[row, :, pl.ds(at, lanes)], outs[k].at[places_ref[number]], sems.at[number, k]
                    )
                )
                at += lanes
            number += 1
    for one in copies:
        one.start()
    for one in copies:
        one.wait()


def lay_rows(pieces, places, widths):
    rows = pieces[0].shape[1]
    sizes = [piece.shape[0] for piece in pieces]
    count = sum(sizes)
    if any(lanes % LANES for lanes in widths):
        whole = jnp.zeros((count,) + pieces[0].shape[1:], pieces[0].dtype)
        for i, row in enumerate(row for piece in pieces for row in piece):
            whole = lax.dynamic_update_index_in_dim(whole, row, places[i], 0)
        whole = whole.reshape(count * rows, -1)
        starts = [sum(widths[:k]) for k in range(len(widths))]
        return [whole[:, at : at + lanes] for at, lanes in zip(starts, widths)]
    results = pl.pallas_call(
        functools.partial(lay_kernel, sizes, widths),
        grid_spec=pltpu.PrefetchScalarGridSpec(
            num_scalar_prefetch=1,
            grid=(1,),
            in_specs=[pl.BlockSpec(memory_space=pl.ANY)] * len(pieces),
            out_specs=[pl.BlockSpec(memory_space=pltpu.VMEM)] * len(widths),
            scratch_shapes=[pltpu.SemaphoreType.DMA((count, len(widths)))],
        ),
        out_shape=[jax.ShapeDtypeStruct((count, rows, lanes), pieces[0].dtype) for lanes in widths],
        compiler_params=pltpu.CompilerParams(vmem_limit_bytes=4 * 1024 * 1024),
        name="lay_rows",
    )(jnp.stack(places).astype(jnp.int32), *pieces)
    return [result.reshape(count * rows, -1) for result in results]


def gather_weights(place, w_gate, w_value, w_bc, w_dt, w_out):
    parts = place.parts
    columns = w_gate.shape[1]
    width = columns // parts
    heads = w_dt.shape[1] // parts
    out_t = w_out.T

    def columns_of(part):
        steps = lax.dynamic_slice_in_dim(w_dt, part * heads, heads, 1)
        steps = jnp.pad(steps, ((0, 0), (0, LANES - heads)))
        cuts = [lax.dynamic_slice_in_dim(array, part * width, width, 1) for array in (w_value, w_gate, out_t)]
        return jnp.concatenate([cuts[0], w_bc, steps, cuts[1], cuts[2]], axis=1)[None]

    pieces, places = [], []
    for p in range(parts):
        block = columns_of(place.part ^ p)
        if p:
            block = place.swap_part(block, p)
        masks = bits_of(place.micros)
        if p % 2:
            masks = masks[::-1]
        found, distances = [block], [0]
        for mask in masks:
            whole = found[0] if len(found) == 1 else jnp.concatenate(found, axis=0)
            found.append(place.swap_micro(whole, mask))
            distances += [distance ^ mask for distance in distances]
        pieces += found
        places += [(place.micro ^ distance) * parts + (place.part ^ p) for distance in distances]
    return lay_rows(pieces, places, [width + MAPS + LANES, width, width])


def whole_tokens(place, rows):
    return [pick(rows, place.micro, 0)] + [
        place.swap_micro(pick(rows, place.micro ^ d, 0), d) for d in range(1, place.micros)
    ]


def lay_tokens(place, blocks):
    held = order(blocks, place.micro, 0)
    whole = order([held] + [place.swap_part(held, d) for d in range(1, place.parts)], place.part, 1)
    size = place.micros // PIECES
    return [whole[i * size : (i + 1) * size].reshape(-1, held.shape[-1]) for i in range(PIECES)]


def spread_tokens(place, rows):
    micros, count, width = rows.shape
    view = rows.reshape(micros, place.tensors, count // place.tensors, width)
    got = [
        place.swap_micro(pick(pick(view, place.micro ^ d, 0), place.tensor, 0), d) for d in range(1, micros)
    ]
    shares = jnp.stack(got)
    both = [shares] + [place.swap_tensor(shares, d) for d in range(1, place.tensors)]
    own = pick(rows, place.micro, 0)
    return lay_tokens(
        place,
        [own]
        + [
            order([part[d] for part in both], place.tensor, 0).reshape(count, width)
            for d in range(micros - 1)
        ],
    )


def blocks_of(place, array):
    return array.reshape(place.micros // PIECES, place.parts, place.tensors, -1, array.shape[-1])


def own_share(place, array, flip=0):
    return pick(pick(blocks_of(place, array), place.part, 1), place.tensor ^ flip, 1)


def cut(place, block):
    return block.reshape(block.shape[:-2] + (place.tensors, -1, block.shape[-1]))


class Reduction:
    def __init__(self, place, own, send, kind=bf16):
        self.place, self.kind = place, kind
        sends = [send.reshape(own.shape)] if place.parts == 2 else [send[d] for d in range(place.parts - 1)]
        self.came = [place.swap_part(cut(place, block), d + 1) for d, block in enumerate(sends)]
        self.own = cut(place, own)

    def launch(self, others=None):
        place = self.place

        def side(tensor):
            return pick(self.own, tensor, 1) + sum(pick(block, tensor, 1).astype(f32) for block in self.came)

        going = [side(place.tensor ^ d).astype(self.kind) for d in range(1, place.tensors)]
        going, others = tie(going, others)
        self.kept = side(place.tensor)
        self.sent = [place.swap_tensor(block, d + 1) for d, block in enumerate(going)]
        return others

    def land(self, others):
        self.sent, others = tie(self.sent, others)
        return others

    def result(self):
        return self.kept + sum(block.astype(f32) for block in self.sent)


class Gathering:
    def __init__(self, place, shares, flip=0):
        self.place, self.shares, self.flip = place, shares, flip
        self.came = None

    def launch(self):
        place = self.place
        self.came = [[place.swap_tensor(share, d) for share in self.shares] for d in range(1, place.tensors)]

    def result(self):
        place = self.place
        came = tie(self.came)[0]
        held = [order(list(group), place.tensor ^ self.flip, 1) for group in zip(self.shares, *came)]
        came = tie([[place.swap_part(block, d) for block in held] for d in range(1, place.parts)])[0]
        whole = [order(list(group), place.part, 1) for group in zip(held, *came)]
        return [block.reshape((-1,) + share.shape[2:]) for block, share in zip(whole, self.shares)]


def gather_shares(place, shares, flip=0):
    gathering = Gathering(place, shares, flip)
    gathering.launch()
    return gathering.result()


class Homing:
    def __init__(self, place, own):
        self.place = place
        self.own = pick(own, place.micro, 0)
        self.sends = [pick(own, place.micro ^ d, 0) for d in range(1, place.micros)]

    def launch(self):
        self.came = [self.place.swap_micro(block, d + 1) for d, block in enumerate(self.sends)]

    def turn(self, others=None):
        place = self.place
        self.rows, others = tie(order([self.own] + self.came, place.micro, 0), others)
        self.swapped = [place.swap_tensor(self.rows, d) for d in range(1, place.tensors)]
        return others

    def result(self):
        return order([self.rows] + self.swapped, self.place.tensor, 1)


def rows_dot(a, b):
    return jnp.dot(a, b, preferred_element_type=f32)


def columns_dot(a, b):
    return lax.dot_general(a, b, (((0,), (0,)), ((), ())), preferred_element_type=f32)


def forward_piece(place, h, weights, small, carry, dn=None):
    results = forward_call(place, h, weights, small, carry[0], carry[1], dn)
    if dn is None:
        return results[:2], (results[2], results[3])
    kept = (h, carry[1]) + tuple(results[5:])
    return results[:3], (results[3], results[4]), kept


def forward_start(place, small):
    width = small[3].shape[1]
    return jnp.zeros((STATE, width), f32), jnp.zeros((8, width + MAPS), f32)


def factor_of(place, small, squares):
    return lax.rsqrt(squares / (place.tensors * place.parts * small[3].shape[1]) + epsilon)


def out_share(place, h, branch):
    return (own_share(place, h).astype(f32) + branch).astype(bf16)


def gates_piece(place, dn, q, pull, kept, small):
    _, _, _, _, z, y, _ = kept
    return gate_call(place, dn, z, y, q[:, None], pull[:, None], small[3])


def normal_piece(e, q, kept, weights, small):
    _, _, _, _, z, y, _ = kept
    dn, pull, n, gain = normal_call(e, weights, z, y, q[:, None], small[3])
    return dn, pull[:, 0], n, gain


def backward_piece(place, exact, gates, kept, weights, small, carry):
    _, before, _, vbd, _, _, states = kept
    mixed = small[3].shape[1] + MAPS
    count = min(STEP * CHUNK, vbd.shape[0])
    tails = vbd.reshape(-1, count, vbd.shape[1])[:-1, count - 8 :, :mixed]
    before = jnp.concatenate([before[None], tails], axis=0)
    own, send, dvbd, adjoint, du, sums = backward_call(
        place, exact, gates[0], gates[1], vbd, before, states, weights, small, carry[0], carry[1]
    )
    return (own, send), (adjoint, du), dvbd, sums


def input_grad(place, e, h, norm_gain, dxn):
    ho = own_share(place, h).astype(f32)
    eo = own_share(place, e).astype(f32)
    r = lax.rsqrt(jnp.mean(ho * ho, axis=2, keepdims=True) + epsilon)
    scaled = dxn * norm_gain
    grad = eo + r * scaled - ho * (r * r * r * jnp.mean(scaled * ho, axis=2, keepdims=True))
    return grad.astype(bf16), jnp.sum(dxn * ho * r, axis=(0, 1))


class Scatter:
    def __init__(self, place, arrays):
        self.place = place
        parts = place.parts
        shape = [2] * len(bits_of(place.micros))
        views = [array.reshape(place.micros, parts, -1, array.shape[1]) for array in arrays]
        self.held = [[view[:, p].reshape(shape + list(view.shape[2:])) for view in views] for p in range(parts)]
        self.came = [[] for _ in range(parts)]
        self.left = [sorted(bits_of(place.micros), reverse=True) for _ in range(parts)]

    def prepare(self):
        place = self.place
        self.out, self.masks = [], []
        for p, left in enumerate(self.left):
            mask = left[0] if p % 2 else left[-1]
            axis = left.index(mask)
            mine = (place.micro // mask) % 2

            def side(bit):
                total = jnp.concatenate([pick(block, bit, axis) for block in self.held[p]], axis=-1)
                for block in self.came[p]:
                    total = total.astype(f32) + pick(block, bit, axis).astype(f32)
                return total.astype(bf16)

            self.out.append(side(1 - mine))
            self.masks.append(mask)
            self.held[p] = [pick(block, mine, axis) for block in self.held[p]]
            self.came[p] = [pick(block, mine, axis) for block in self.came[p]]
            left.remove(mask)

    def launch(self):
        self.next = [self.place.swap_micro(block, mask) for block, mask in zip(self.out, self.masks)]

    def land(self):
        for p, block in enumerate(self.next):
            self.came[p].append(block)

    def trade(self):
        place = self.place
        chip = []
        for held, came in zip(self.held, self.came):
            total = jnp.concatenate(held, axis=-1).astype(f32)
            for block in came:
                total = total + block.astype(f32)
            chip.append(total)

        def chosen(index):
            result = chip[0]
            for p in range(1, place.parts):
                result = jnp.where(index == p, chip[p], result)
            return result

        result = [chosen(place.part)]
        for d in range(1, place.parts):
            result.append(place.swap_part(chosen(place.part ^ d).astype(bf16), d).astype(f32))
        return result


def body(
    block_input,
    norm_gain,
    w_gate,
    w_value,
    w_bc,
    w_dt,
    conv_value,
    conv_bc,
    conv_value_bias,
    conv_bc_bias,
    dt_bias,
    decay_log,
    skip,
    gate_gain,
    w_out,
    cotangent,
):
    sections = lax.axis_size("section")
    section = lax.axis_index("section")
    place = Place(block_input.shape[0])
    parts, part = place.parts, place.part
    width = w_gate.shape[2] // parts
    heads_here = w_dt.shape[2] // parts
    mixed = width + MAPS

    def share(vector, size):
        return lax.dynamic_slice_in_dim(vector, part * size, size, vector.ndim - 1)

    def padded(vector):
        return jnp.pad(vector, (0, head_rows(width) - heads_here))

    h0 = spread_tokens(place, block_input)
    weights = gather_weights(place, w_gate[0], w_value[0], w_bc[0], w_dt[0], w_out[0])
    taps = jnp.concatenate(
        [
            jnp.concatenate([share(conv_value[0], width), conv_bc[0]], axis=1),
            jnp.concatenate([share(conv_value_bias[0], width), conv_bc_bias[0]])[None],
            jnp.zeros((8 - CONV - 1, mixed), f32),
        ],
        axis=0,
    )
    own_skip = share(skip[0], heads_here)
    rate = jnp.exp(share(decay_log[0], heads_here))
    heads = jnp.concatenate([padded(share(dt_bias[0], heads_here)), padded(rate)])
    heads = jnp.broadcast_to(heads[:, None], (heads.size, LANES))
    inner = jnp.stack([jnp.repeat(own_skip, HEAD_DIM), share(gate_gain[0], width)])
    inner = jnp.concatenate([inner, jnp.zeros((6, width), f32)], axis=0)
    small = (norm_gain[0], taps, heads, inner)

    span = range(PIECES)
    first, last = section == 0, section == sections - 1
    flip = 1 if place.tensors > 1 else 0

    def leave(place_of, block, came, step, others):
        if came:
            newest = list(came)[-1]
            block, came[newest], others = tie(block, came[newest], others)
        else:
            block, others = tie(block, others)
        came[place_of] = place.next_section(block, step, flip if step > 0 else 0)
        return others

    def arrive(i, came, stays, originals, others, flip):
        block, others = tie(came[i], others)
        return jnp.where(stays, own_share(place, originals[i], flip), block), others

    came = None
    for turn in range(sections - 1):
        carry = forward_start(place, small)
        shares_in, came = came, {}
        pieces, halves, terms, e_blocks = list(h0), [], None, None
        for i in span:
            if shares_in is not None:
                share, terms = arrive(i, shares_in, first, h0, terms, flip)
                pieces[i] = gather_shares(place, [share], flip)[0]
            if i:
                pieces[i], halves[-1][1], cotangent = tie(pieces[i], halves[-1][1], cotangent)
                crossing = [place.swap_tensor(halves[-1][1], mask) for mask in bits_of(place.tensors)]
                if turn == 0 and i == 1:
                    e_blocks = whole_tokens(place, cotangent)
            terms, carry = forward_piece(place, pieces[i], weights, small, carry)
            if i:
                terms, crossing, e_blocks = tie(terms, crossing, e_blocks)
                halves[-1][1] = halves[-1][1] + sum(crossing)
            halves.append([terms[0], sum_all(place, terms[1][0, :, 0], micro=False, tensor=False)])
        halves[-1][1] = sum_all(place, halves[-1][1], micro=False, part=False)
        if turn == 0 and e_blocks is None:
            e_blocks = whole_tokens(place, cotangent)
        red = []
        for g, squares in halves:
            own, send = out_call(place, g, factor_of(place, small, squares), weights, small[3])
            red.append(Reduction(place, own, send, jnp.float16))
            red[-1].launch()
        if turn == 0:
            e0 = lay_tokens(place, e_blocks)
            e0, dn0 = red[0].land((e0, [rows_dot(e, weights[2]) for e in e0]))
        for i, item in enumerate(red):
            leave(i, out_share(place, pieces[i], item.result()), came, 1, None)
    if sections == 1:
        e0 = lay_tokens(place, whole_tokens(place, cotangent))
        dn0 = [rows_dot(e, weights[2]) for e in e0]

    carry = forward_start(place, small)
    kept, sums, lines, terms = [], [], [], None
    for i in span:
        h = h0[i]
        if came is not None:
            block, terms = arrive(i, came, first, h0, terms, flip)
            h = gather_shares(place, [block], flip)[0]
        terms, carry, keep = forward_piece(place, h, weights, small, carry, dn0[i])
        kept.append(keep)
        lines.append(terms[2][:, :, 0])
        sums.append(Reduction(place, terms[0], terms[1]))
    lines = sum_all(place, jnp.stack(lines), micro=False)
    qs = [factor_of(place, small, lines[i, 0]) for i in span]
    dots = [lines[i, 1] for i in span]

    def gradient_of(i, came, others):
        share, others = arrive(i, came, last, e0, others, 0)
        gathering = Gathering(place, [share])
        gathering.launch()
        return gathering, others

    def outputs_of():
        outs = []
        for k in span:
            branch = sums[k].result() * own_share(place, qs[k].reshape(-1, 1))
            outs.append(out_share(place, kept[k][0], branch))
        return Homing(place, jnp.concatenate(outs, axis=0))

    came, homing, ready = None, None, None
    es = list(e0)
    for turn in range(sections - 1):
        carry = forward_start(place, small)
        shares_in, came = came, {}
        es, terms = list(e0), None
        for i in reversed(span):
            dn, pull = dn0[i], dots[i]
            if shares_in is not None:
                ready, terms = gradient_of(i, shares_in, terms)
                es[i] = ready.result()[0]
                dn, pull, _, _ = normal_piece(es[i], qs[i], kept[i], weights, small)
                pull = sum_all(place, pull, micro=False)
            elif homing is None:
                for item in sums:
                    dn = item.launch(dn)
            gates = gates_piece(place, dn, qs[i], pull, kept[i], small)
            if i + 1 < PIECES:
                gates = leave(i + 1, share, came, -1, gates)
            terms, carry, _, _ = backward_piece(place, False, gates, kept[i], weights, small, carry)
            if i + 1 < PIECES:
                terms, came[i + 1] = tie(terms, came[i + 1])
            if homing is None:
                for item in sums:
                    terms = item.land(terms)
            red = Reduction(place, terms[0], terms[1])
            red.launch()
            if homing is None:
                homing = outputs_of()
            if not i and turn == sections - 2 and PIECES > 1:
                ready, _ = gradient_of(PIECES - 1, came, None)
                ready.came = red.land(ready.came)
            share, _ = input_grad(place, es[i], kept[i][0], norm_gain[0], red.result())
        leave(0, share, came, -1, None)
    if homing is None:
        for item in sums:
            item.launch()
        homing = outputs_of()

    carry = forward_start(place, small)
    red, matrix, small_sums, terms = [], [None] * 3, None, None

    def add(old, a, b):
        now = columns_dot(a, b)
        return now if old is None else old + now

    for i in reversed(span):
        if came is not None:
            if red or ready is None:
                ready, terms = gradient_of(i, came, terms)
            es[i] = ready.result()[0]
        dn, pull, n, gain_grad = normal_piece(es[i], qs[i], kept[i], weights, small)
        pull = sum_all(place, pull, micro=False)
        matrix[0] = add(matrix[0], es[i], n)
        pull, matrix[0] = tie(pull, matrix[0])
        if red:
            pull = homing.turn(red[-1].launch(pull))
        else:
            pull, homing.sends = tie(pull, homing.sends)
            homing.launch()
        gates = gates_piece(place, dn, qs[i], pull, kept[i], small)
        if not i:
            scatter = Scatter(place, [matrix[0].astype(bf16), add(matrix[1], kept[i][2], gates[1]).astype(bf16)])
            scatter.prepare()
            gates, scatter.out = tie(gates, scatter.out)
            scatter.launch()
        terms, carry, dvbd, now = backward_piece(place, True, gates, kept[i], weights, small, carry)
        if red:
            terms = red[-1].land(terms)
        else:
            homing.came, terms, gates, dvbd, now = tie(homing.came, terms, gates, dvbd, now)
            if PIECES == 1:
                homing.turn()
        now = [now, gain_grad]
        if i:
            red.append(Reduction(place, terms[0], terms[1]))
            for k, b in ((1, gates[1]), (2, dvbd)):
                matrix[k] = add(matrix[k], kept[i][2], b)
        else:
            ahead = Reduction(place, terms[0], terms[1])
            ahead.own, dvbd, now, scatter.next, homing.swapped = tie(
                ahead.own, dvbd, now, scatter.next, homing.swapped
            )
            scatter.land()
            red.append(ahead)
        small_sums = now if small_sums is None else [a + b for a, b in zip(small_sums, now)]
    outputs = homing.result().reshape(block_input.shape)
    mixes = Scatter(place, [add(matrix[2], kept[0][2], dvbd).astype(bf16)])
    grads, norm_grad = [], 0.0
    for i, item in zip(reversed(span), red[:-1]):
        block, now = input_grad(place, es[i], kept[i][0], norm_gain[0], item.result())
        grads.insert(0, block)
        norm_grad = norm_grad + now
    for one in (mixes, scatter):
        one.prepare()
    mixes.out, scatter.out = red[-1].launch((mixes.out, scatter.out))
    for one in (scatter, mixes):
        one.launch()
    scatter.next = red[-1].land(scatter.next)
    block, now = input_grad(place, es[0], kept[0][0], norm_gain[0], red[-1].result())
    norm_grad = norm_grad + now
    homing = Homing(place, jnp.concatenate([block] + grads, axis=0))
    homing.launch()
    homing.came, mixes.next = tie(homing.came, mixes.next)
    homing.turn()
    mixes.land()
    mixes.prepare()
    mixes.launch()
    for one in (scatter, mixes):
        one.land()
        while one.left[0]:
            one.prepare()
            one.launch()
            one.land()
    input_grads = homing.result().reshape(block_input.shape).astype(f32)
    scatter, mixes = scatter.trade(), mixes.trade()
    gates = [block[:, width:] for block in scatter]
    out_t = [block[:, :width] for block in scatter]
    gate_grad = beside(gates, part)
    out_grad = order([block.T for block in out_t], part, 0).reshape(-1, w_out.shape[2])
    value_grad = beside([block[:, :width] for block in mixes], part)
    step_grad = beside([block[:, mixed : mixed + heads_here] for block in mixes], part)
    maps_grad = sum(block[:, width:mixed] for block in mixes).astype(bf16)
    maps_sum = maps_grad.astype(f32)
    for mask in bits_of(place.tensors):
        maps_sum = maps_sum + place.swap_tensor(maps_sum, mask)

    packed, gain_grad = small_sums
    row = lax.broadcasted_iota(jnp.int32, (8, mixed), 0)
    packed = jnp.where(row == GAIN_ROW, jnp.pad(gain_grad, ((0, 0), (0, MAPS))), packed)
    lanes = max(mixed, norm_grad.size)
    packed = jnp.concatenate(
        [jnp.pad(packed, ((0, 0), (0, lanes - mixed))), jnp.pad(norm_grad[None], ((0, 7), (0, lanes - norm_grad.size)))],
        axis=0,
    )
    packed, homing.rows = tie(packed, homing.rows)
    packed = sum_all(place, packed, part=False, tensor=False)
    by_part = [packed] + [place.swap_part(packed, d) for d in range(1, parts)]
    both = by_part[0]
    for distance in range(1, parts):
        both = both + by_part[distance]
    both = sum_all(place, both, micro=False, part=False)
    wide, bias_grad, gain_grad, maps_small, maps_bias, norm_sum, by_head = unpack(
        place, both, by_part, width, heads_here, norm_grad.size
    )
    total_heads = parts * heads_here
    return (
        outputs[None],
        input_grads[None],
        norm_sum,
        gate_grad[None],
        value_grad[None],
        maps_sum[None],
        step_grad[None],
        wide[None],
        maps_small[None],
        bias_grad,
        maps_bias,
        by_head[0:1, :total_heads],
        by_head[1:2, :total_heads],
        by_head[2:3, :total_heads],
        gain_grad,
        out_grad[None],
    )


def solution(mesh):
    placed = (
        P(None, "context", None),
        P("section", None),
        P("section", "context", "tensor"),
        P("section", "context", "tensor"),
        P("section", "context", None),
        P("section", "context", "tensor"),
        P("section", None, "tensor"),
        P("section", None, None),
        P("section", "tensor"),
        P("section", None),
        P("section", "tensor"),
        P("section", "tensor"),
        P("section", "tensor"),
        P("section", "tensor"),
        P("section", "tensor", "context"),
        P(None, "context", None),
    )
    return jax.shard_map(
        body,
        mesh=mesh,
        in_specs=placed,
        out_specs=(
            P("section", None, "context", None),
            P("section", None, "context", None),
            P("section", None),
            P("section", "context", "tensor"),
            P("section", "context", "tensor"),
            P("section", "context", None),
            P("section", "context", "tensor"),
            P("section", None, "tensor"),
            P("section", None, None),
            P("section", "tensor"),
            P("section", None),
            P("section", "tensor"),
            P("section", "tensor"),
            P("section", "tensor"),
            P("section", "tensor"),
            P("section", "tensor", "context"),
        ),
        check_vma=False,
    )
```

```python
import functools

import jax
import jax.numpy as jnp
from jax import lax
from jax.experimental import pallas as pl
from jax.experimental.pallas import tpu as pltpu
from jax.sharding import PartitionSpec as P

HEAD_DIM = 64
STATE = 128
CONV = 4
MAPS = 2 * STATE
CHUNK = 128
LANES = 128
PIECES = 2

epsilon = 1e-05
bf16 = jnp.bfloat16
f32 = jnp.float32


def low_dot(a, b, contract):
    return lax.dot_general(
        a.astype(bf16), b.astype(bf16), ((contract[0], contract[1]), ((), ())), preferred_element_type=f32
    )


def mm(a, b):
    return low_dot(a, b, ((1,), (0,)))


def mm_nt(a, b):
    return low_dot(a, b, ((1,), (1,)))


def mm_tn(a, b):
    return low_dot(a, b, ((0,), (0,)))


def softplus(v):
    return jnp.maximum(v, 0.0) + jnp.log(1.0 + jnp.exp(-jnp.abs(v)))


def groups_of(width):
    return [
        (at, min(LANES, width - at), at // HEAD_DIM, min(LANES, width - at) // HEAD_DIM)
        for at in range(0, width, LANES)
    ]


def head_rows(width):
    return -(-(width // HEAD_DIM) // 16) * 16


def column(cols, head):
    return jnp.broadcast_to(cols[:, head : head + 1], (cols.shape[0], LANES))


def choose(first, second, lanes):
    if second is None:
        return first[:, :lanes]
    lane = lax.broadcasted_iota(jnp.int32, (first.shape[0], lanes), 1)
    return jnp.where(lane < HEAD_DIM, first, second)


def only(value, which, count):
    if count == 1:
        return value
    lane = lax.broadcasted_iota(jnp.int32, value.shape, 1)
    return jnp.where((lane < HEAD_DIM) == (which == 0), value, jnp.zeros_like(value))


def pieces_of(value, count):
    terms = []
    for _ in range(count):
        term = value.astype(bf16)
        terms.append(term)
        value = value - term.astype(f32)
    return terms


def mm3(a, b):
    (a_hi, a_lo), (b_hi, b_lo) = pieces_of(a, 2), pieces_of(b, 2)
    return mm(jnp.concatenate([a_hi, a_lo, a_hi], axis=1), jnp.concatenate([b_hi, b_hi, b_lo], axis=0))


def mm3_nt(a, b):
    (a_hi, a_lo), (b_hi, b_lo) = pieces_of(a, 2), pieces_of(b, 2)
    return mm_nt(jnp.concatenate([a_hi, a_lo, a_hi], axis=1), jnp.concatenate([b_hi, b_hi, b_lo], axis=1))


def sum_dot(value, zero_one, count):
    return sum(mm(term, zero_one) for term in pieces_of(value, count))


def iotas():
    row = lax.broadcasted_iota(jnp.int32, (CHUNK, CHUNK), 0)
    col = lax.broadcasted_iota(jnp.int32, (CHUNK, CHUNK), 1)
    return row, col


def conv_rows(pad, taps_ref, at, lanes):
    here = slice(at, at + lanes)
    pre = taps_ref[CONV : CONV + 1, here] + taps_ref[CONV - 1 : CONV, here] * pad[8 : 8 + CHUNK, here]
    for k in range(CONV - 1):
        first = 8 - (CONV - 1) + k
        pre = pre + taps_ref[k : k + 1, here] * pad[first : first + CHUNK, here]
    return pre


def decay_terms(dt_pre, heads_ref, rows, row, col):
    wide = dt_pre.T[:rows] + heads_ref[0:rows, :]
    dt = softplus(wide)
    log_decay = sum_dot(-heads_ref[rows : 2 * rows, :] * dt, (row <= col).astype(bf16), 3)
    cols = jnp.concatenate([log_decay, dt, jnp.zeros((CHUNK - 2 * rows, CHUNK), f32)], axis=0).T
    return wide, dt, log_decay, cols


def as_row(value):
    return jnp.sum(value.T, axis=0, keepdims=True)


def filled(value):
    rows, lanes = value.shape
    if lanes == LANES:
        return value
    return jnp.concatenate([value, jnp.zeros((rows, LANES - lanes), f32)], axis=1)


def as_column(row):
    return jnp.broadcast_to(row, (CHUNK, LANES)).T


def deal(part, parts, first, count, total, own_ref, send_ref):
    def one(c, _):
        index = first + c
        distance = (index % parts) ^ part
        rows = total[pl.ds(pl.multiple_of(c * CHUNK, CHUNK), CHUNK), :]

        @pl.when(distance == 0)
        def _():
            own_ref[index // parts] = rows

        @pl.when(distance != 0)
        def _():
            send_ref[jnp.maximum(distance - 1, 0), index // parts] = rows.astype(send_ref.dtype)

        return 0

    lax.fori_loop(0, count, one, 0)


def forward_kernel(keep, width, parts, per_step, part_ref, h_ref, w1_ref, wg_ref, norm_ref, taps_ref, heads_ref, inner_ref, s0_ref, tail0_ref, *rest):
    if keep:
        wo_ref, dn_ref, own_ref, send_ref, sums_ref, st_ref, tail_ref, xn_ref, vbd_ref, z_ref, y_ref, sin_ref, pad, gg, total = rest
    else:
        g_ref, sums_ref, st_ref, tail_ref, xn_ref, vbd_ref, z_ref, pad = rest
    mixed = width + MAPS
    rows = head_rows(width)
    step = pl.program_id(0)

    @pl.when(step == 0)
    def _():
        st_ref[...] = s0_ref[...]
        tail_ref[...] = tail0_ref[...]

    def norm(c, _):
        here = pl.ds(pl.multiple_of(c * 64, 64), 64)
        hf = h_ref[here, :].astype(f32)
        scale = lax.rsqrt(jnp.mean(hf * hf, axis=1, keepdims=True) + epsilon)
        xn_ref[here, :] = (hf * scale * norm_ref[...]).astype(bf16)
        return 0

    lax.fori_loop(0, per_step * 2, norm, 0)
    vbd_ref[...] = jnp.dot(xn_ref[...], w1_ref[...], preferred_element_type=f32)
    z_ref[...] = jnp.dot(xn_ref[...], wg_ref[...], preferred_element_type=f32)
    row, col = iotas()

    def chunk(c, _):
        here = pl.ds(pl.multiple_of(c * CHUNK, CHUNK), CHUNK)
        pad[0:8, :] = tail_ref[...]
        pad[8 : 8 + CHUNK, :] = vbd_ref[here, :mixed]
        tail_ref[...] = pad[CHUNK : CHUNK + 8, :]
        pre = conv_rows(pad, taps_ref, width, MAPS)
        maps = pre * jax.nn.sigmoid(pre)
        b, c_map = maps[:, :STATE], maps[:, STATE:]
        b_rows = b.T
        _, _, log_row, cols = decay_terms(vbd_ref[here, mixed:], heads_ref, rows, row, col)
        contact = jnp.where(row >= col, mm3(c_map, b_rows), 0.0)
        if keep:
            sin_ref[c] = st_ref[...]
        carried = mm3(c_map, st_ref[...])
        squares = jnp.zeros((CHUNK, LANES), f32)
        pulls = jnp.zeros((CHUNK, LANES), f32)
        for at, lanes, head, count in groups_of(width):
            span = slice(at, at + lanes)
            pre = conv_rows(pad, taps_ref, at, lanes)
            own = pre * jax.nn.sigmoid(pre)
            logs = [column(cols, head + j) for j in range(count)]
            steps = [column(cols, rows + head + j) for j in range(count)]
            log_x = choose(logs[0], logs[-1] if count == 2 else None, lanes)
            step_x = choose(steps[0], steps[-1] if count == 2 else None, lanes)
            last_x = log_x[CHUNK - 1 : CHUNK, :]
            xd = own * step_x
            mixing = [
                jnp.exp(jnp.minimum(logs[j] - log_row[head + j : head + j + 1, :], 0.0)) * contact
                for j in range(count)
            ]
            inside = mm3(
                jnp.concatenate(mixing, axis=1),
                jnp.concatenate([only(xd, j, count) for j in range(count)], axis=0),
            )
            y = inside + jnp.exp(log_x) * carried[:, span] + inner_ref[0:1, span] * own
            st_ref[:, span] = jnp.exp(last_x) * st_ref[:, span] + mm3(b_rows, jnp.exp(last_x - log_x) * xd)
            z = z_ref[here, span]
            g = y * (z * jax.nn.sigmoid(z))
            if keep:
                gg[here, span] = (g * inner_ref[1:2, span]).astype(bf16)
                y_ref[here, span] = y
            else:
                g_ref[here, span] = g
            squares = squares + filled(g * g)
            if keep:
                pulls = pulls + filled(dn_ref[here, span] * inner_ref[1:2, span] * g)
        sums_ref[0, c] = as_row(squares)
        if keep:
            sums_ref[1, c] = as_row(pulls)
        return 0

    lax.fori_loop(0, per_step, chunk, 0)
    if keep:
        total[...] = lax.dot_general(
            gg[...], wo_ref[...], (((1,), (1,)), ((), ())), preferred_element_type=f32
        )
        deal(part_ref[0], parts, step * per_step, per_step, total, own_ref, send_ref)


def out_kernel(parts, per_step, part_ref, g_ref, q_ref, inner_ref, wo_ref, own_ref, send_ref, n, total):
    def chunk(c, _):
        here = pl.ds(pl.multiple_of(c * CHUNK, CHUNK), CHUNK)
        q = as_column(q_ref[c])
        for at, lanes, _, _ in groups_of(n.shape[1]):
            span = slice(at, at + lanes)
            n[here, span] = (g_ref[here, span] * q[:, :lanes] * inner_ref[1:2, span]).astype(bf16)
        return 0

    lax.fori_loop(0, per_step, chunk, 0)
    total[...] = lax.dot_general(n[...], wo_ref[...], (((1,), (1,)), ((), ())), preferred_element_type=f32)
    deal(part_ref[0], parts, pl.program_id(0) * per_step, per_step, total, own_ref, send_ref)


def out_call(place, g, q, weights, inner):
    wo = weights[2]
    tokens, width = g.shape
    depth = wo.shape[0]
    chunks = tokens // CHUNK
    per_step = min(STEP, chunks)
    steps = chunks // per_step
    count = per_step * CHUNK
    blocks = chunks // place.parts
    shapes = [(blocks, CHUNK, depth), (place.parts - 1, blocks, CHUNK, depth)]
    return pl.pallas_call(
        functools.partial(out_kernel, place.parts, per_step),
        grid_spec=pltpu.PrefetchScalarGridSpec(
            num_scalar_prefetch=1,
            grid=(steps,),
            in_specs=[
                block(steps, (count, width), lambda i, _: (i, 0)),
                block(steps, (per_step, 1, LANES), lambda i, _: (i, 0, 0)),
                once(inner.shape),
                once(wo.shape),
            ],
            out_specs=[once(shape) for shape in shapes],
            scratch_shapes=[pltpu.VMEM((count, width), bf16), pltpu.VMEM((count, depth), f32)],
        ),
        out_shape=[jax.ShapeDtypeStruct(shape, f32) for shape in shapes],
        compiler_params=kernel_params(steps, 8),
        cost_estimate=pl.CostEstimate(
            flops=tokens * width * 6000, bytes_accessed=tokens * depth * 8, transcendentals=0
        ),
        name="out_forward",
    )(place.part.reshape(1), g, q[:, None], inner, wo)


STEP = 4
GAIN_ROW = CONV + 1
HEAD_ROW = CONV + 2


def kernel_params(steps, megabytes):
    return pltpu.CompilerParams(vmem_limit_bytes=(megabytes if steps == 1 else 40) * 1024 * 1024)


def once(shape):
    return pl.BlockSpec(memory_space=pltpu.VMEM)


def block(steps, shape, index_map):
    return once(shape) if steps == 1 else pl.BlockSpec(shape, index_map)


def forward_call(place, h, weights, small, s0, tail0, dn=None):
    w1, wg = weights[:2]
    norm_gain, taps, heads, inner = small
    keep = dn is not None
    tokens, depth = h.shape
    width = inner.shape[1]
    mixed = width + MAPS
    chunks = tokens // CHUNK
    per_step = min(STEP, chunks)
    steps = chunks // per_step
    count = per_step * CHUNK
    blocks = chunks // place.parts
    rows = lambda lanes: block(steps, (count, lanes), lambda i, _: (i, 0))
    if keep:
        shapes = [((blocks, CHUNK, depth), f32), ((place.parts - 1, blocks, CHUNK, depth), bf16)]
        out_shape = [jax.ShapeDtypeStruct(*item) for item in shapes]
        out_specs = [once(shape) for shape, _ in shapes]
    else:
        out_shape = [jax.ShapeDtypeStruct((tokens, width), f32)]
        out_specs = [rows(width)]
    out_shape += [
        jax.ShapeDtypeStruct((2, chunks, 1, LANES), f32),
        jax.ShapeDtypeStruct((STATE, width), f32),
        jax.ShapeDtypeStruct((8, mixed), f32),
    ]
    out_specs += [
        block(steps, (2, per_step, 1, LANES), lambda i, _: (0, i, 0, 0)),
        once((STATE, width)),
        once((8, mixed)),
    ]
    in_specs = [
        rows(depth),
        once(w1.shape),
        once(wg.shape),
        once((1, depth)),
        once(taps.shape),
        once(heads.shape),
        once(inner.shape),
        once(s0.shape),
        once(tail0.shape),
    ]
    args = [h, w1, wg, norm_gain[None], taps, heads, inner, s0, tail0]
    held = [((tokens, depth), bf16), ((tokens, w1.shape[1]), f32), ((tokens, width), f32)]
    scratch = []
    if keep:
        in_specs += [once(weights[2].shape), rows(width)]
        args += [weights[2], dn]
        held.append(((tokens, width), f32))
        out_shape += [jax.ShapeDtypeStruct(*item) for item in held]
        out_specs += [rows(shape[1]) for shape, _ in held]
        out_shape.append(jax.ShapeDtypeStruct((chunks, STATE, width), f32))
        out_specs.append(block(steps, (per_step, STATE, width), lambda i, _: (i, 0, 0)))
    else:
        scratch = [pltpu.VMEM((count, shape[1]), kind) for shape, kind in held]
    scratch.append(pltpu.VMEM((CHUNK + 8, mixed), f32))
    if keep:
        scratch += [pltpu.VMEM((count, width), bf16), pltpu.VMEM((count, depth), f32)]
    return pl.pallas_call(
        functools.partial(forward_kernel, keep, width, place.parts, per_step),
        grid_spec=pltpu.PrefetchScalarGridSpec(
            num_scalar_prefetch=1, grid=(steps,), in_specs=in_specs, out_specs=out_specs, scratch_shapes=scratch
        ),
        out_shape=out_shape,
        compiler_params=kernel_params(steps, 10 if keep else 11),
        cost_estimate=pl.CostEstimate(
            flops=tokens * width * 40000, bytes_accessed=tokens * depth * 16, transcendentals=0
        ),
        name="section_forward",
    )(place.part.reshape(1), *args)


def normal_kernel(full, width, per_step, e_ref, wo_ref, z_ref, y_ref, q_ref, inner_ref, dn_ref, pull_ref, n_ref, gain_ref, gains):
    dn_ref[...] = jnp.dot(e_ref[...], wo_ref[...], preferred_element_type=f32)

    @pl.when(pl.program_id(0) == 0)
    def _():
        gains[...] = jnp.zeros_like(gains)

    def chunk(c, _):
        here = pl.ds(pl.multiple_of(c * CHUNK, CHUNK), CHUNK)
        q = as_column(q_ref[c])
        pulls = jnp.zeros((CHUNK, LANES), f32)
        for at, lanes, _, _ in groups_of(width):
            span = slice(at, at + lanes)
            z, dn_x, gain = z_ref[here, span], dn_ref[here, span], inner_ref[1:2, span]
            g = y_ref[here, span] * (z * jax.nn.sigmoid(z))
            gq = g * q[:, :lanes]
            pulls = pulls + filled(dn_x * gain * g)
            n_ref[here, span] = (gq * gain).astype(bf16)
            gains[:, span] += fold(dn_x * gq)
        pull_ref[c] = as_row(pulls)
        return 0

    lax.fori_loop(0, per_step, chunk, 0)
    gain_ref[...] = jnp.broadcast_to(jnp.sum(gains[...], axis=0, keepdims=True), gains.shape)


def gate_kernel(width, per_step, total, dn_ref, z_ref, y_ref, q_ref, pull_ref, inner_ref, dy_ref, dz_ref):
    def chunk(c, _):
        here = pl.ds(pl.multiple_of(c * CHUNK, CHUNK), CHUNK)
        q = as_column(q_ref[c])
        pull = as_column(pull_ref[c]) * (q * q * q) * (1.0 / total)
        for at, lanes, _, _ in groups_of(width):
            span = slice(at, at + lanes)
            z, y = z_ref[here, span], y_ref[here, span]
            sig = jax.nn.sigmoid(z)
            silu = z * sig
            dg = q[:, :lanes] * (dn_ref[here, span] * inner_ref[1:2, span]) - y * silu * pull[:, :lanes]
            dy_ref[here, span] = dg * silu
            dz_ref[here, span] = (dg * y * (sig + silu * (1.0 - sig))).astype(bf16)
        return 0

    lax.fori_loop(0, per_step, chunk, 0)


def normal_call(e, weights, z, y, q, inner):
    wo = weights[2]
    tokens, depth = e.shape
    width = inner.shape[1]
    chunks = tokens // CHUNK
    per_step = min(STEP, chunks)
    steps = chunks // per_step
    rows = lambda lanes: block(steps, (per_step * CHUNK, lanes), lambda i: (i, 0))
    lines = block(steps, (per_step, 1, LANES), lambda i: (i, 0, 0))
    return pl.pallas_call(
        functools.partial(normal_kernel, True, width, per_step),
        grid=(steps,),
        in_specs=[rows(depth), once(wo.shape), rows(width), rows(width), lines, once(inner.shape)],
        out_specs=[rows(width), lines, rows(width), once((8, width))],
        out_shape=[
            jax.ShapeDtypeStruct((tokens, width), f32),
            jax.ShapeDtypeStruct((chunks, 1, LANES), f32),
            jax.ShapeDtypeStruct((tokens, width), bf16),
            jax.ShapeDtypeStruct((8, width), f32),
        ],
        scratch_shapes=[pltpu.VMEM((8, width), f32)],
        compiler_params=kernel_params(steps, 4),
        cost_estimate=pl.CostEstimate(
            flops=tokens * width * 9000, bytes_accessed=tokens * depth * 16, transcendentals=0
        ),
        name="norm_backward",
    )(e, wo, z, y, q, inner)


def gate_call(place, dn, z, y, q, pull, inner):
    tokens, width = dn.shape
    chunks = tokens // CHUNK
    per_step = min(STEP, chunks)
    steps = chunks // per_step
    rows = lambda lanes: block(steps, (per_step * CHUNK, lanes), lambda i: (i, 0))
    lines = block(steps, (per_step, 1, LANES), lambda i: (i, 0, 0))
    return pl.pallas_call(
        functools.partial(gate_kernel, width, per_step, place.tensors * place.parts * width),
        grid=(steps,),
        in_specs=[rows(width), rows(width), rows(width), lines, lines, once(inner.shape)],
        out_specs=[rows(width), rows(width)],
        out_shape=[jax.ShapeDtypeStruct((tokens, width), f32), jax.ShapeDtypeStruct((tokens, width), bf16)],
        compiler_params=kernel_params(steps, 4),
        cost_estimate=pl.CostEstimate(
            flops=tokens * width * 6000, bytes_accessed=tokens * width * 16, transcendentals=0
        ),
        name="gate_backward",
    )(dn, z, y, q, pull, inner)


def fold(value):
    return jnp.sum(value.reshape(CHUNK // 8, 8, value.shape[1]), axis=0)


def backward_kernel(
    exact,
    width,
    parts,
    per_step,
    steps,
    part_ref,
    dy_ref,
    dz_ref,
    vbd_ref,
    before_ref,
    sin_ref,
    w1_ref,
    wg_ref,
    taps_ref,
    heads_ref,
    inner_ref,
    g0_ref,
    du0_ref,
    own_ref,
    send_ref,
    dvbd_ref,
    gt_ref,
    dut_ref,
    tapg_ref,
    pad,
    dpad,
    sums,
    y_in,
    dxd_out,
    dy_in_all,
    xd_out_all,
    total,
    taps_sum,
    headg_ref,
    skipg_ref,
    back_all,
):
    mixed = width + MAPS
    rows = head_rows(width)
    step = steps - 1 - pl.program_id(0)

    @pl.when(pl.program_id(0) == 0)
    def _():
        gt_ref[...] = g0_ref[...]
        dut_ref[...] = du0_ref[...]
        taps_sum[...] = jnp.zeros_like(taps_sum)
        headg_ref[...] = jnp.zeros_like(headg_ref)
        skipg_ref[...] = jnp.zeros_like(skipg_ref)

    row, col = iotas()
    causal = col >= row
    strict = col > row
    onward = (row >= col).astype(bf16)
    head_of = lax.broadcasted_iota(jnp.int32, (rows, width), 1) // HEAD_DIM
    ones = (head_of == lax.broadcasted_iota(jnp.int32, (rows, width), 0)).astype(bf16)

    def conv_back(here, at, lanes, du):
        span = slice(at, at + lanes)
        dpad[0:CHUNK, span] = du
        m = pad[8 : 8 + CHUNK, span]
        taps_sum[CONV * 8 : CONV * 8 + 8, span] += fold(du)
        taps_sum[CONV * 8 - 8 : CONV * 8, span] += fold(m * du)
        dm = taps_ref[CONV - 1 : CONV, span] * du
        for k in range(CONV - 1):
            first = CONV - 1 - k
            moved = dpad[first : first + CHUNK, span]
            dm = dm + taps_ref[k : k + 1, span] * moved
            taps_sum[k * 8 : k * 8 + 8, span] += fold(m * moved)
        dvbd_ref[here, span] = dm.astype(bf16)

    def chunk(reverse, _):
        c = per_step - 1 - reverse
        here = pl.ds(pl.multiple_of(c * CHUNK, CHUNK), CHUNK)
        dpad[CHUNK : CHUNK + 8, :] = dut_ref[...]
        pad[8 : 8 + CHUNK, :] = vbd_ref[here, :mixed]

        @pl.when(c == 0)
        def _():
            pad[0:8, :] = before_ref[0]

        @pl.when(c != 0)
        def _():
            pad[0:8, :] = vbd_ref[pl.ds(pl.multiple_of(jnp.maximum(c * CHUNK - 8, 0), 8), 8), :mixed]

        pre = conv_rows(pad, taps_ref, width, MAPS)
        sig = jax.nn.sigmoid(pre)
        maps = pre * sig
        maps_slope = sig + maps * (1.0 - sig)
        b_maps, c_maps = maps[:, :STATE], maps[:, STATE:]
        b_low, c_low = b_maps.astype(bf16), c_maps.astype(bf16)
        wide, dt, log_row, cols = decay_terms(vbd_ref[here, mixed:], heads_ref, rows, row, col)
        contact = jnp.where(causal, mm_nt(b_low, c_low), 0.0)
        back_low = gt_ref[...].astype(bf16)
        if exact:
            back_all[...] = gt_ref[...]
        c_rows = c_low.T
        y_in[...] = mm(c_low, sin_ref[c])
        dxd_out[...] = mm(b_low, back_low)
        dcontact = jnp.zeros((CHUNK, CHUNK), f32)
        log_rows, through = [], []
        for at, lanes, head, count in groups_of(width):
            span = slice(at, at + lanes)
            pre = conv_rows(pad, taps_ref, at, lanes)
            sig = jax.nn.sigmoid(pre)
            own = pre * sig
            slope = sig + own * (1.0 - sig)
            logs = [column(cols, head + j) for j in range(count)]
            steps_of = [column(cols, rows + head + j) for j in range(count)]
            log_x = choose(logs[0], logs[-1] if count == 2 else None, lanes)
            step_x = choose(steps_of[0], steps_of[-1] if count == 2 else None, lanes)
            last_x = log_x[CHUNK - 1 : CHUNK, :]
            dy = dy_ref[here, span]
            xd = own * step_x
            xd_low = xd.astype(bf16)
            dy_low = dy.astype(bf16)
            to_end = jnp.exp(last_x - log_x)
            dy_in = jnp.exp(log_x) * dy
            dy_in_low = dy_in.astype(bf16)
            if exact:
                dy_in_all[:, span] = dy_in
                xd_out_all[:, span] = to_end * xd
                dmix = mm3_nt(jnp.concatenate([only(xd, j, count) for j in range(count)], axis=0), dy)
            else:
                dy_in_all[:, span] = dy_in_low
                xd_out_all[:, span] = (to_end * xd).astype(bf16)
                dmix = mm_nt(jnp.concatenate([only(xd_low, j, count) for j in range(count)], axis=0), dy_low)
            mixing, products = [], []
            for j in range(count):
                decay = jnp.exp(jnp.minimum(log_row[head + j : head + j + 1, :] - logs[j], 0.0))
                one = decay * contact
                d_one = dmix[j * CHUNK : (j + 1) * CHUNK]
                dcontact = dcontact + decay * d_one
                mixing.append(one.astype(bf16))
                products.append((one * d_one).astype(bf16))
            dxd_in = mm(
                jnp.concatenate(mixing, axis=1),
                jnp.concatenate([only(dy_low, j, count) for j in range(count)], axis=0),
            )
            later = mm(jnp.concatenate(products, axis=0), onward)
            for j in range(count):
                log_rows.append(
                    jnp.sum(jnp.where(strict, later[j * CHUNK : (j + 1) * CHUNK], 0.0), axis=0, keepdims=True)
                )
            from_end = to_end * dxd_out[:, span]
            dxd = dxd_in + from_end
            sums[0:CHUNK, span] = (dy_in * y_in[:, span]).astype(bf16)
            sums[CHUNK : 2 * CHUNK, span] = (xd * from_end).astype(bf16)
            sums[2 * CHUNK : 3 * CHUNK, span] = (own * dxd).astype(bf16)
            carried = jnp.exp(last_x)
            back = gt_ref[:, span]
            through.append(
                jnp.sum(carried * sin_ref[c, :, span].astype(f32) * back, axis=0, keepdims=True)
            )
            skipg_ref[:, span] += fold(dy * own)
            gt_ref[:, span] = carried * back + mm(c_rows, dy_in_low)
            conv_back(here, at, lanes, (step_x * dxd + inner_ref[0:1, span] * dy) * slope)
        dcontact = jnp.where(causal, dcontact, 0.0)
        if exact:
            db = mm3_nt(xd_out_all[...], back_all[...]) + mm3(dcontact, c_maps)
            dc = mm3_nt(dy_in_all[...], sin_ref[c]) + mm3(dcontact.T, b_maps)
        else:
            db = mm_nt(xd_out_all[...], back_low) + mm(dcontact, c_low)
            dc = mm_nt(dy_in_all[...], sin_ref[c]) + mm_tn(dcontact, b_low)
        conv_back(here, width, STATE, db * maps_slope[:, :STATE])
        conv_back(here, width + STATE, STATE, dc * maps_slope[:, STATE:])
        dut_ref[...] = dpad[0:8, :]

        by_token = mm_nt(ones, sums[...])
        entering = by_token[:, :CHUNK]
        leaving = by_token[:, CHUNK : 2 * CHUNK]
        direct = by_token[:, 2 * CHUNK :]
        ends = jnp.broadcast_to(jnp.concatenate(through, axis=1), (CHUNK, width))
        ends = sum(mm_nt(ones, term) for term in pieces_of(ends, 2))
        inside = log_rows
        if rows > len(log_rows):
            inside = log_rows + [jnp.zeros((rows - len(log_rows), CHUNK), f32)]
        dlog = (
            jnp.concatenate(inside, axis=0)
            + sum_dot(entering, onward, 2)
            + sum_dot(leaving, (row < col).astype(bf16), 2)
            + ends
        )
        rate = heads_ref[rows : 2 * rows, :]
        ddt_pre = (direct - rate * dlog) * jax.nn.sigmoid(wide)
        headg_ref[0:rows, :] += ddt_pre
        headg_ref[rows : 2 * rows, :] += -rate * dt * dlog
        ddt_cols = jnp.concatenate([ddt_pre, jnp.zeros((CHUNK - rows, CHUNK), f32)], axis=0).T
        dvbd_ref[here, mixed:] = ddt_cols.astype(bf16)
        return 0

    lax.fori_loop(0, per_step, chunk, 0)
    nt = (((1,), (1,)), ((), ()))
    total[...] = lax.dot_general(dvbd_ref[...], w1_ref[...], nt, preferred_element_type=f32)
    total[...] += lax.dot_general(dz_ref[...], wg_ref[...], nt, preferred_element_type=f32)

    @pl.when(pl.program_id(0) == steps - 1)
    def _():
        tapg_ref[...] = jnp.zeros_like(tapg_ref)
        for k in range(CONV + 1):
            tapg_ref[k : k + 1, :] = jnp.sum(taps_sum[k * 8 : k * 8 + 8, :], axis=0, keepdims=True)
        skips = jnp.broadcast_to(jnp.sum(skipg_ref[...], axis=0, keepdims=True), (CHUNK, width))
        skips = sum(mm_nt(ones, term) for term in pieces_of(skips, 3))
        by_head = jnp.broadcast_to(jnp.sum(headg_ref[...], axis=1, keepdims=True), (2 * rows, LANES))
        columns = jnp.concatenate([by_head, skips, jnp.zeros((CHUNK - 3 * rows, LANES), f32)], axis=0)
        tapg_ref[HEAD_ROW : HEAD_ROW + 1, 0:LANES] = columns.T[0:1]

    deal(part_ref[0], parts, step * per_step, per_step, total, own_ref, send_ref)


def backward_call(place, exact, dy, dz, vbd, before, states, weights, small, g0, du0):
    w1, wg, _ = weights
    _, taps, heads, inner = small
    tokens, width = dy.shape
    depth = w1.shape[0]
    mixed = width + MAPS
    chunks = tokens // CHUNK
    per_step = min(STEP, chunks)
    steps = chunks // per_step
    count = per_step * CHUNK
    blocks = chunks // place.parts
    rows = lambda lanes: block(steps, (count, lanes), lambda i, _: (steps - 1 - i, 0))
    deep = lambda number, height, lanes: block(
        steps, (number, height, lanes), lambda i, _: (steps - 1 - i, 0, 0)
    )
    shapes = [
        ((STATE, width), f32),
        ((8, mixed), f32),
        ((8, mixed), f32),
    ]
    results = pl.pallas_call(
        functools.partial(backward_kernel, exact, width, place.parts, per_step, steps),
        grid_spec=pltpu.PrefetchScalarGridSpec(
            num_scalar_prefetch=1,
            grid=(steps,),
            in_specs=[
                rows(width),
                rows(width),
                rows(vbd.shape[1]),
                deep(1, 8, mixed),
                deep(per_step, STATE, width),
                once(w1.shape),
                once(wg.shape),
                once(taps.shape),
                once(heads.shape),
                once(inner.shape),
                once(g0.shape),
                once(du0.shape),
            ],
            out_specs=[
                once((blocks, CHUNK, depth)),
                once((place.parts - 1, blocks, CHUNK, depth)),
                rows(vbd.shape[1]),
            ]
            + [once(shape) for shape, _ in shapes],
            scratch_shapes=[
                pltpu.VMEM((CHUNK + 8, mixed), f32),
                pltpu.VMEM((CHUNK + 8, mixed), f32),
                pltpu.VMEM((3 * CHUNK, width), bf16),
                pltpu.VMEM((CHUNK, width), f32),
                pltpu.VMEM((CHUNK, width), f32),
                pltpu.VMEM((CHUNK, width), f32 if exact else bf16),
                pltpu.VMEM((CHUNK, width), f32 if exact else bf16),
                pltpu.VMEM((count, depth), f32),
                pltpu.VMEM((8 * (CONV + 1), mixed), f32),
                pltpu.VMEM((2 * head_rows(width), LANES), f32),
                pltpu.VMEM((8, width), f32),
                pltpu.VMEM((STATE, width), f32),
            ],
        ),
        out_shape=[
            jax.ShapeDtypeStruct((blocks, CHUNK, depth), f32),
            jax.ShapeDtypeStruct((place.parts - 1, blocks, CHUNK, depth), bf16),
            jax.ShapeDtypeStruct(vbd.shape, bf16),
        ]
        + [jax.ShapeDtypeStruct(*item) for item in shapes],
        compiler_params=kernel_params(steps, 12),
        cost_estimate=pl.CostEstimate(
            flops=tokens * width * 60000, bytes_accessed=tokens * depth * 16, transcendentals=0
        ),
        name="section_backward",
    )(place.part.reshape(1), dy, dz, vbd, before, states, w1, wg, taps, heads, inner, g0, du0)
    own, send, dvbd, gt, dut, sums = results
    return own, send, dvbd, gt, dut, sums


def unpack_kernel(parts, heads, rows, part_ref, both_ref, *refs):
    locals_ref, outs = refs[:parts], refs[parts:]
    wide_ref, bias_ref, gain_ref, maps_ref, maps_bias_ref, norm_ref, heads_ref = outs
    width = wide_ref.shape[1] // parts
    part = part_ref[0]
    lane = lax.broadcasted_iota(jnp.int32, (1, LANES), 1)
    by_head = [jnp.zeros((1, LANES), f32) for _ in range(3)]
    for d in range(parts):
        owner = part ^ d
        here = pl.ds(pl.multiple_of(owner * width, HEAD_DIM), width)
        ref = locals_ref[d]
        if width % LANES == 0:
            wide_ref[:, here] = ref[0:CONV, 0:width]
            bias_ref[:, here] = ref[CONV : CONV + 1, 0:width]
            gain_ref[:, here] = ref[GAIN_ROW : GAIN_ROW + 1, 0:width]
        else:
            for p in range(parts):

                @pl.when(owner == p)
                def _():
                    there = slice(p * width, (p + 1) * width)
                    wide_ref[:, there] = ref[0:CONV, 0:width]
                    bias_ref[:, there] = ref[CONV : CONV + 1, 0:width]
                    gain_ref[:, there] = ref[GAIN_ROW : GAIN_ROW + 1, 0:width]

        for k in range(3):
            values = ref[HEAD_ROW : HEAD_ROW + 1, 0:LANES]
            for p in range(parts):
                moved = pltpu.roll(values, (p * heads - k * rows) % LANES, 1)
                chosen = (owner == p) & (lane >= p * heads) & (lane < (p + 1) * heads)
                by_head[k] = jnp.where(chosen, moved, by_head[k])
    heads_ref[...] = jnp.concatenate(by_head + [jnp.zeros((5, LANES), f32)], axis=0)
    maps_ref[...] = both_ref[0:CONV, width : width + MAPS]
    maps_bias_ref[...] = both_ref[CONV : CONV + 1, width : width + MAPS]
    norm_ref[...] = both_ref[8:9, 0 : norm_ref.shape[1]]


def unpack(place, both, by_part, width, heads, depth):
    total = place.parts * width
    shapes = [(CONV, total), (1, total), (1, total), (CONV, MAPS), (1, MAPS), (1, depth), (8, LANES)]
    return pl.pallas_call(
        functools.partial(unpack_kernel, place.parts, heads, head_rows(width)),
        grid_spec=pltpu.PrefetchScalarGridSpec(
            num_scalar_prefetch=1,
            grid=(1,),
            in_specs=[once(both.shape)] * (1 + place.parts),
            out_specs=[once(shape) for shape in shapes],
        ),
        out_shape=[jax.ShapeDtypeStruct(shape, f32) for shape in shapes],
        compiler_params=pltpu.CompilerParams(vmem_limit_bytes=4 * 1024 * 1024),
        name="unpack_small",
    )(place.part.reshape(1), both, *by_part)


class Place:
    def __init__(self, micro_count):
        self.context = lax.axis_size("context")
        self.micros = micro_count
        self.parts = self.context // micro_count
        self.tensors = lax.axis_size("tensor")
        index = lax.axis_index("context")
        self.micro = index // self.parts
        self.part = index % self.parts
        self.tensor = lax.axis_index("tensor")

    def swap_part(self, block, mask):
        return lax.ppermute(block, "context", [(i, i ^ mask) for i in range(self.context)])

    def swap_micro(self, block, mask):
        return self.swap_part(block, mask * self.parts)

    def swap_tensor(self, block, mask):
        return lax.ppermute(block, "tensor", [(i, i ^ mask) for i in range(self.tensors)])

    def next_section(self, block, step, flip):
        count, tensors = lax.axis_size("section"), self.tensors
        return lax.ppermute(
            block,
            ("section", "tensor"),
            [
                (i * tensors + t, (i + step) * tensors + (t ^ flip))
                for i in range(count)
                if 0 <= i + step < count
                for t in range(tensors)
            ],
        )


def pick(array, index, axis):
    return lax.dynamic_index_in_dim(array, index, axis, False)


def tie(*items):
    return lax.optimization_barrier(items)


def bits_of(count):
    masks = []
    mask = 1
    while mask < count:
        masks.append(mask)
        mask *= 2
    return masks


def order_kernel(count, axis, index_ref, *refs):
    blocks, out, sems = refs[:count], refs[count], refs[count + 1]
    copies = []
    for d, one in enumerate(blocks):
        there = (slice(None),) * axis + (index_ref[0] ^ d,)
        copies.append(pltpu.make_async_copy(one, out.at[there], sems.at[d]))
    for one in copies:
        one.start()
    for one in copies:
        one.wait()


def order(blocks, index, axis, copies=True):
    count = len(blocks)
    shape = list(blocks[0].shape)
    shape.insert(axis, count)
    if count == 1:
        return blocks[0].reshape(shape)
    if copies and axis <= blocks[0].ndim - 2 and shape[-2] % 16 == 0 and shape[-1] >= LANES:
        return pl.pallas_call(
            functools.partial(order_kernel, count, axis),
            grid_spec=pltpu.PrefetchScalarGridSpec(
                num_scalar_prefetch=1,
                grid=(1,),
                in_specs=[pl.BlockSpec(memory_space=pl.ANY)] * count,
                out_specs=pl.BlockSpec(memory_space=pltpu.VMEM),
                scratch_shapes=[pltpu.SemaphoreType.DMA((count,))],
            ),
            out_shape=jax.ShapeDtypeStruct(tuple(shape), blocks[0].dtype),
            compiler_params=pltpu.CompilerParams(vmem_limit_bytes=4 * 1024 * 1024),
            name="order_blocks",
        )(index.reshape(1).astype(jnp.int32), *blocks)
    place = lax.broadcasted_iota(jnp.int32, shape, axis) ^ index
    result = jnp.expand_dims(blocks[0], axis)
    for d in range(1, count):
        result = jnp.where(place == d, jnp.expand_dims(blocks[d], axis), result)
    return jnp.broadcast_to(result, shape)


def beside(blocks, index):
    count = len(blocks)
    if count == 2:
        return jnp.where(
            index == 0, jnp.concatenate(blocks, axis=-1), jnp.concatenate(blocks[::-1], axis=-1)
        )
    return jnp.concatenate(
        [pick(order(blocks, index, 0), i, 0) for i in range(count)], axis=-1
    )


def sum_all(place, block, micro=True, part=True, tensor=True):
    if part:
        for mask in bits_of(place.parts):
            block = block + place.swap_part(block, mask)
    if tensor:
        for mask in bits_of(place.tensors):
            block = block + place.swap_tensor(block, mask)
    if micro:
        for mask in bits_of(place.micros):
            block = block + place.swap_micro(block, mask)
    return block


def lay_kernel(sizes, widths, places_ref, *refs):
    pieces, outs, sems = refs[: len(sizes)], refs[len(sizes) : -1], refs[-1]
    copies, number = [], 0
    for piece, size in zip(pieces, sizes):
        for row in range(size):
            at = 0
            for k, lanes in enumerate(widths):
                copies.append(
                    pltpu.make_async_copy(
                        piece.at[row, :, pl.ds(at, lanes)], outs[k].at[places_ref[number]], sems.at[number, k]
                    )
                )
                at += lanes
            number += 1
    for one in copies:
        one.start()
    for one in copies:
        one.wait()


def lay_rows(pieces, places, widths):
    rows = pieces[0].shape[1]
    sizes = [piece.shape[0] for piece in pieces]
    count = sum(sizes)
    if any(lanes % LANES for lanes in widths):
        whole = jnp.zeros((count,) + pieces[0].shape[1:], pieces[0].dtype)
        for i, row in enumerate(row for piece in pieces for row in piece):
            whole = lax.dynamic_update_index_in_dim(whole, row, places[i], 0)
        whole = whole.reshape(count * rows, -1)
        starts = [sum(widths[:k]) for k in range(len(widths))]
        return [whole[:, at : at + lanes] for at, lanes in zip(starts, widths)]
    results = pl.pallas_call(
        functools.partial(lay_kernel, sizes, widths),
        grid_spec=pltpu.PrefetchScalarGridSpec(
            num_scalar_prefetch=1,
            grid=(1,),
            in_specs=[pl.BlockSpec(memory_space=pl.ANY)] * len(pieces),
            out_specs=[pl.BlockSpec(memory_space=pltpu.VMEM)] * len(widths),
            scratch_shapes=[pltpu.SemaphoreType.DMA((count, len(widths)))],
        ),
        out_shape=[jax.ShapeDtypeStruct((count, rows, lanes), pieces[0].dtype) for lanes in widths],
        compiler_params=pltpu.CompilerParams(vmem_limit_bytes=4 * 1024 * 1024),
        name="lay_rows",
    )(jnp.stack(places).astype(jnp.int32), *pieces)
    return [result.reshape(count * rows, -1) for result in results]


class Collect:
    def __init__(self, place, blocks):
        self.place = place
        self.found = [[block] for block in blocks]
        self.distances = [[0] for _ in blocks]
        self.masks = [bits_of(place.micros)[:: -1 if p % 2 else 1] for p in range(len(blocks))]

    def prepare(self):
        self.out = [found[0] if len(found) == 1 else jnp.concatenate(found, axis=0) for found in self.found]

    def launch(self):
        self.next = [self.place.swap_micro(block, masks[0]) for block, masks in zip(self.out, self.masks)]

    def land(self):
        for p, block in enumerate(self.next):
            mask = self.masks[p].pop(0)
            self.found[p].append(block)
            self.distances[p] += [distance ^ mask for distance in self.distances[p]]

    def finish(self):
        while self.masks[0]:
            self.prepare()
            self.launch()
            self.land()

    def result(self, widths):
        place, pieces, places = self.place, [], []
        for p, found in enumerate(self.found):
            pieces += found
            places += [(place.micro ^ distance) * place.parts + (place.part ^ p) for distance in self.distances[p]]
        return lay_rows(pieces, places, widths)


def gather_weights(place, w_gate, w_value, w_bc, w_dt, w_out):
    parts = place.parts
    width = w_gate.shape[1] // parts
    heads = w_dt.shape[1] // parts

    def cut_of(array, part):
        return lax.dynamic_slice_in_dim(array, part * width, width, 1)

    def columns_of(part):
        steps = lax.dynamic_slice_in_dim(w_dt, part * heads, heads, 1)
        steps = jnp.pad(steps, ((0, 0), (0, LANES - heads)))
        return jnp.concatenate([cut_of(w_value, part), w_bc, steps, cut_of(w_gate, part)], axis=1)[None]

    def collected(make):
        blocks = [make(place.part ^ p) for p in range(parts)]
        return Collect(place, blocks[:1] + [place.swap_part(block, p + 1) for p, block in enumerate(blocks[1:])])

    first = collected(columns_of)
    second = collected(lambda part: cut_of(w_out.T, part)[None])
    return first, second


def whole_tokens(place, rows):
    return [pick(rows, place.micro, 0)] + [
        place.swap_micro(pick(rows, place.micro ^ d, 0), d) for d in range(1, place.micros)
    ]


def lay_tokens(place, blocks):
    held = order(blocks, place.micro, 0, False)
    whole = order([held] + [place.swap_part(held, d) for d in range(1, place.parts)], place.part, 1, False)
    size = place.micros // PIECES
    return [whole[i * size : (i + 1) * size].reshape(-1, held.shape[-1]) for i in range(PIECES)]


class Spread:
    def __init__(self, place, rows):
        self.place, self.rows = place, rows
        micros, count, width = rows.shape
        view = rows.reshape(micros, place.tensors, count // place.tensors, width)
        self.shares = jnp.stack(
            [place.swap_micro(pick(pick(view, place.micro ^ d, 0), place.tensor, 0), d) for d in range(1, micros)]
        )
        self.came = [place.swap_tensor(self.shares, d) for d in range(1, place.tensors)]

    def result(self):
        place = self.place
        both = [self.shares] + self.came
        blocks = [pick(self.rows, place.micro, 0)]
        for d in range(place.micros - 1):
            whole = order([part[d] for part in both], place.tensor, 0, False)
            blocks.append(whole.reshape(-1, self.rows.shape[2]))
        return lay_tokens(place, blocks)


def blocks_of(place, array):
    return array.reshape(place.micros // PIECES, place.parts, place.tensors, -1, array.shape[-1])


def own_share(place, array, flip=0):
    return pick(pick(blocks_of(place, array), place.part, 1), place.tensor ^ flip, 1)


GROUP = 16


def split_kernel(parts, tensors, tensor_ref, own_ref, *refs):
    came, going_ref, kept_ref = refs[: parts - 1], refs[-2], refs[-1]
    rows = kept_ref.shape[1]

    def group(i, _):
        here = pl.ds(pl.multiple_of(i * GROUP, GROUP), GROUP)
        for d in range(tensors):
            start = (tensor_ref[0] ^ d) * rows + i * GROUP
            there = pl.ds(pl.multiple_of(start, GROUP), GROUP)
            total = own_ref[0, there, :]
            for one in came:
                total = total + one[0, there, :].astype(f32)
            if d:
                going_ref[d - 1, 0, here, :] = total.astype(bf16)
            else:
                kept_ref[0, here, :] = total
        return 0

    lax.fori_loop(0, rows // GROUP, group, 0)


def split_call(place, own, came):
    blocks, tokens, depth = own.shape
    rows = tokens // place.tensors
    others = place.tensors - 1
    return pl.pallas_call(
        functools.partial(split_kernel, place.parts, place.tensors),
        grid_spec=pltpu.PrefetchScalarGridSpec(
            num_scalar_prefetch=1,
            grid=(blocks,),
            in_specs=[pl.BlockSpec((1, tokens, depth), lambda b, _: (b, 0, 0))] * place.parts,
            out_specs=[
                pl.BlockSpec((others, 1, rows, depth), lambda b, _: (0, b, 0, 0)),
                pl.BlockSpec((1, rows, depth), lambda b, _: (b, 0, 0)),
            ],
        ),
        out_shape=[
            jax.ShapeDtypeStruct((others, blocks, rows, depth), bf16),
            jax.ShapeDtypeStruct((blocks, rows, depth), f32),
        ],
        compiler_params=pltpu.CompilerParams(vmem_limit_bytes=8 * 1024 * 1024),
        name="split_terms",
    )(place.tensor.reshape(1), own, *came)


def finish_kernel(places_ref, kept_ref, h_ref, e_ref, norm_ref, *refs):
    sent, grad_ref, sum_ref = refs[:-2], refs[-2], refs[-1]
    rows = kept_ref.shape[1]

    @pl.when(pl.program_id(0) == 0)
    def _():
        sum_ref[...] = jnp.zeros_like(sum_ref)

    def group(i, _):
        here = pl.ds(pl.multiple_of(i * GROUP, GROUP), GROUP)
        dxn = kept_ref[0, here, :]
        for one in sent:
            dxn = dxn + one[0, here, :].astype(f32)
        h = h_ref[0, 0, 0, here, :].astype(f32)
        r = lax.rsqrt(jnp.mean(h * h, axis=1, keepdims=True) + epsilon)
        scaled = dxn * norm_ref[...]
        pull = r * r * r * jnp.mean(scaled * h, axis=1, keepdims=True)
        grad_ref[0, here, :] = (e_ref[0, 0, 0, here, :].astype(f32) + r * scaled - h * pull).astype(bf16)
        found = dxn * h * r
        sum_ref[...] += found[0:8] + found[8:16]
        return 0

    lax.fori_loop(0, rows // GROUP, group, 0)


def finish_call(place, kept, sent, h, e, norm_gain):
    blocks, rows, depth = kept.shape
    share = pl.BlockSpec((1, rows, depth), lambda b, _: (b, 0, 0))
    whole = pl.BlockSpec((1, 1, 1, rows, depth), lambda b, places: (b, places[0], places[1], 0, 0))
    return pl.pallas_call(
        finish_kernel,
        grid_spec=pltpu.PrefetchScalarGridSpec(
            num_scalar_prefetch=1,
            grid=(blocks,),
            in_specs=[share, whole, whole, pl.BlockSpec((1, depth), lambda b, _: (0, 0))] + [share] * len(sent),
            out_specs=[share, pl.BlockSpec((8, depth), lambda b, _: (0, 0))],
        ),
        out_shape=[jax.ShapeDtypeStruct(kept.shape, bf16), jax.ShapeDtypeStruct((8, depth), f32)],
        compiler_params=pltpu.CompilerParams(vmem_limit_bytes=8 * 1024 * 1024),
        name="finish_gradient",
    )(jnp.stack([place.part, place.tensor]), kept, blocks_of(place, h), blocks_of(place, e), norm_gain[None], *sent)


def deal_kernel(parts, widths, rounds, part_ref, *refs):
    mine_ref, send_ref = refs[-2], refs[-1]
    each = len(widths) + rounds
    rows = mine_ref.shape[0]

    def group(i, _):
        here = pl.ds(pl.multiple_of(i * GROUP, GROUP), GROUP)
        for p in range(parts):
            arrays = refs[p * each : (p + 1) * each]
            total = jnp.concatenate([one[here, :].astype(f32) for one in arrays[: len(widths)]], axis=1)
            for one in arrays[len(widths) :]:
                total = total + one[here, :].astype(f32)
            distance = part_ref[0] ^ p

            @pl.when(distance == 0)
            def _():
                mine_ref[here, :] = total

            @pl.when(distance != 0)
            def _():
                send_ref[jnp.maximum(distance - 1, 0), here, :] = total.astype(bf16)

        return 0

    lax.fori_loop(0, rows // GROUP, group, 0)


def deal_call(place, groups, came):
    widths = [block.shape[-1] for block in groups[0]]
    rows, total = groups[0][0].shape[0], sum(widths)
    args = [one for held, round_ in zip(groups, came) for one in list(held) + list(round_)]
    others = place.parts - 1
    step = 3 * GROUP
    return pl.pallas_call(
        functools.partial(deal_kernel, place.parts, widths, len(came[0])),
        grid_spec=pltpu.PrefetchScalarGridSpec(
            num_scalar_prefetch=1,
            grid=(rows // step,),
            in_specs=[pl.BlockSpec((step, one.shape[1]), lambda i, _: (i, 0)) for one in args],
            out_specs=[
                pl.BlockSpec((step, total), lambda i, _: (i, 0)),
                pl.BlockSpec((others, step, total), lambda i, _: (0, i, 0)),
            ],
        ),
        out_shape=[jax.ShapeDtypeStruct((rows, total), f32), jax.ShapeDtypeStruct((others, rows, total), bf16)],
        compiler_params=pltpu.CompilerParams(vmem_limit_bytes=8 * 1024 * 1024),
        name="deal_rows",
    )(place.part.reshape(1), *args)


def beside_kernel(parts, at, part_ref, *refs):
    blocks, out_ref = refs[:parts], refs[-1]
    rows, width = out_ref.shape[0], out_ref.shape[1] // parts

    def group(i, _):
        here = pl.ds(pl.multiple_of(i * GROUP, GROUP), GROUP)
        for d, one in enumerate(blocks):
            there = pl.ds(pl.multiple_of((part_ref[0] ^ d) * width, LANES), width)
            out_ref[here, there] = one[here, at : at + width].astype(f32)
        return 0

    lax.fori_loop(0, rows // GROUP, group, 0)


def columns_beside(place, blocks, at, width):
    if width % LANES or at % LANES:
        return beside([block[:, at : at + width].astype(f32) for block in blocks], place.part)
    shape = (blocks[0].shape[0], place.parts * width)
    step = 3 * GROUP
    return pl.pallas_call(
        functools.partial(beside_kernel, place.parts, at),
        grid_spec=pltpu.PrefetchScalarGridSpec(
            num_scalar_prefetch=1,
            grid=(shape[0] // step,),
            in_specs=[pl.BlockSpec((step, block.shape[1]), lambda i, _: (i, 0)) for block in blocks],
            out_specs=pl.BlockSpec((step, shape[1]), lambda i, _: (i, 0)),
        ),
        out_shape=jax.ShapeDtypeStruct(shape, f32),
        compiler_params=pltpu.CompilerParams(vmem_limit_bytes=8 * 1024 * 1024),
        name="columns_beside",
    )(place.part.reshape(1), *blocks)


def cut(place, block):
    return block.reshape(block.shape[:-2] + (place.tensors, -1, block.shape[-1]))


class Reduction:
    def __init__(self, place, own, send, kind=bf16):
        self.place, self.kind, self.going = place, kind, None
        sends = [send.reshape(own.shape)] if place.parts == 2 else [send[d] for d in range(place.parts - 1)]
        self.came = [place.swap_part(block, d + 1) for d, block in enumerate(sends)]
        self.own = own

    def prepare(self):
        place = self.place
        if self.kind == bf16:
            going, self.kept = split_call(place, self.own, self.came)
            self.going = [going.reshape(self.kept.shape)] if place.tensors == 2 else list(going)
        else:
            own, came = cut(place, self.own), [cut(place, block) for block in self.came]

            def side(tensor):
                return pick(own, tensor, 1) + sum(pick(block, tensor, 1).astype(f32) for block in came)

            self.going = [side(place.tensor ^ d).astype(self.kind) for d in range(1, place.tensors)]
            self.kept = side(place.tensor)

    def launch(self, others=None):
        if self.going is None:
            self.prepare()
        self.going, others = tie(self.going, others)
        self.sent = [self.place.swap_tensor(block, d + 1) for d, block in enumerate(self.going)]
        return others

    def land(self, others):
        self.sent, others = tie(self.sent, others)
        return others

    def result(self):
        return self.kept + sum(block.astype(f32) for block in self.sent)


class Gathering:
    def __init__(self, place, shares, flip=0):
        self.place, self.shares, self.flip = place, shares, flip
        self.came = None

    def launch(self):
        place = self.place
        self.came = [[place.swap_tensor(share, d) for share in self.shares] for d in range(1, place.tensors)]

    def result(self):
        place = self.place
        came = tie(self.came)[0]
        held = [order(list(group), place.tensor ^ self.flip, 1) for group in zip(self.shares, *came)]
        came = tie([[place.swap_part(block, d) for block in held] for d in range(1, place.parts)])[0]
        whole = [order(list(group), place.part, 1) for group in zip(held, *came)]
        return [block.reshape((-1,) + share.shape[2:]) for block, share in zip(whole, self.shares)]


def gather_shares(place, shares, flip=0):
    gathering = Gathering(place, shares, flip)
    gathering.launch()
    return gathering.result()


class Homing:
    def __init__(self, place, own):
        self.place = place
        self.rows = None
        self.own = pick(own, place.micro, 0)
        self.sends = [pick(own, place.micro ^ d, 0) for d in range(1, place.micros)]

    def launch(self):
        self.came = [self.place.swap_micro(block, d + 1) for d, block in enumerate(self.sends)]

    def collect(self):
        self.rows = order([self.own] + self.came, self.place.micro, 0)

    def turn(self, others=None):
        place = self.place
        if self.rows is None:
            self.collect()
        self.rows, others = tie(self.rows, others)
        self.swapped = [place.swap_tensor(self.rows, d) for d in range(1, place.tensors)]
        return others

    def result(self):
        return order([self.rows] + self.swapped, self.place.tensor, 1)


def rows_dot(a, b):
    return jnp.dot(a, b, preferred_element_type=f32)


def columns_dot(a, b):
    return lax.dot_general(a, b, (((0,), (0,)), ((), ())), preferred_element_type=f32)


def forward_piece(place, h, weights, small, carry, dn=None):
    results = forward_call(place, h, weights, small, carry[0], carry[1], dn)
    if dn is None:
        return results[:2], (results[2], results[3])
    kept = (h, carry[1]) + tuple(results[5:])
    return results[:3], (results[3], results[4]), kept


def forward_start(place, small):
    width = small[3].shape[1]
    return jnp.zeros((STATE, width), f32), jnp.zeros((8, width + MAPS), f32)


def factor_of(place, small, squares):
    return lax.rsqrt(squares / (place.tensors * place.parts * small[3].shape[1]) + epsilon)


def out_share(place, h, branch):
    return (own_share(place, h).astype(f32) + branch).astype(bf16)


def gates_piece(place, dn, q, pull, kept, small):
    _, _, _, _, z, y, _ = kept
    return gate_call(place, dn, z, y, q[:, None], pull[:, None], small[3])


def normal_piece(e, q, kept, weights, small):
    _, _, _, _, z, y, _ = kept
    dn, pull, n, gain = normal_call(e, weights, z, y, q[:, None], small[3])
    return dn, pull[:, 0], n, gain


def backward_piece(place, exact, gates, kept, weights, small, carry):
    _, before, _, vbd, _, _, states = kept
    mixed = small[3].shape[1] + MAPS
    count = min(STEP * CHUNK, vbd.shape[0])
    tails = vbd.reshape(-1, count, vbd.shape[1])[:-1, count - 8 :, :mixed]
    before = jnp.concatenate([before[None], tails], axis=0)
    own, send, dvbd, adjoint, du, sums = backward_call(
        place, exact, gates[0], gates[1], vbd, before, states, weights, small, carry[0], carry[1]
    )
    return (own, send), (adjoint, du), dvbd, sums


def input_grad(place, e, h, norm_gain, item):
    return finish_call(place, item.kept, item.sent, h, e, norm_gain)


class Scatter:
    def __init__(self, place, arrays):
        self.place = place
        parts = place.parts
        shape = [2] * len(bits_of(place.micros))
        views = [array.reshape(place.micros, parts, -1, array.shape[1]) for array in arrays]
        self.held = [[view[:, p].reshape(shape + list(view.shape[2:])) for view in views] for p in range(parts)]
        self.came = [[] for _ in range(parts)]
        self.left = [sorted(bits_of(place.micros), reverse=True) for _ in range(parts)]

    def prepare(self):
        place = self.place
        self.out, self.masks = [], []
        for p, left in enumerate(self.left):
            mask = left[0] if p % 2 else left[-1]
            axis = left.index(mask)
            mine = (place.micro // mask) % 2

            def side(bit):
                total = jnp.concatenate([pick(block, bit, axis) for block in self.held[p]], axis=-1)
                for block in self.came[p]:
                    total = total.astype(f32) + pick(block, bit, axis).astype(f32)
                return total.astype(bf16)

            self.out.append(side(1 - mine))
            self.masks.append(mask)
            self.held[p] = [pick(block, mine, axis) for block in self.held[p]]
            self.came[p] = [pick(block, mine, axis) for block in self.came[p]]
            left.remove(mask)

    def launch(self):
        self.next = [self.place.swap_micro(block, mask) for block, mask in zip(self.out, self.masks)]

    def land(self):
        for p, block in enumerate(self.next):
            self.came[p].append(block)

    def trade(self):
        place = self.place
        mine, send = deal_call(place, self.held, self.came)
        sends = [send.reshape(mine.shape)] if place.parts == 2 else list(send)
        return [mine] + [place.swap_part(block, d + 1) for d, block in enumerate(sends)]


def body(
    block_input,
    norm_gain,
    w_gate,
    w_value,
    w_bc,
    w_dt,
    conv_value,
    conv_bc,
    conv_value_bias,
    conv_bc_bias,
    dt_bias,
    decay_log,
    skip,
    gate_gain,
    w_out,
    cotangent,
):
    sections = lax.axis_size("section")
    section = lax.axis_index("section")
    place = Place(block_input.shape[0])
    parts, part = place.parts, place.part
    width = w_gate.shape[2] // parts
    heads_here = w_dt.shape[2] // parts
    mixed = width + MAPS

    def share(vector, size):
        return lax.dynamic_slice_in_dim(vector, part * size, size, vector.ndim - 1)

    def padded(vector):
        return jnp.pad(vector, (0, head_rows(width) - heads_here))

    spread = Spread(place, block_input)
    collected, second = gather_weights(place, w_gate[0], w_value[0], w_bc[0], w_dt[0], w_out[0])
    collected.prepare()
    collected.launch()
    spread.came, collected.next = tie(spread.came, collected.next)
    collected.land()
    collected.finish()
    weights = tuple(collected.result([mixed + LANES, width]))
    h0 = spread.result()
    taps = jnp.concatenate(
        [
            jnp.concatenate([share(conv_value[0], width), conv_bc[0]], axis=1),
            jnp.concatenate([share(conv_value_bias[0], width), conv_bc_bias[0]])[None],
            jnp.zeros((8 - CONV - 1, mixed), f32),
        ],
        axis=0,
    )
    own_skip = share(skip[0], heads_here)
    rate = jnp.exp(share(decay_log[0], heads_here))
    heads = jnp.concatenate([padded(share(dt_bias[0], heads_here)), padded(rate)])
    heads = jnp.broadcast_to(heads[:, None], (heads.size, LANES))
    inner = jnp.stack([jnp.repeat(own_skip, HEAD_DIM), share(gate_gain[0], width)])
    inner = jnp.concatenate([inner, jnp.zeros((6, width), f32)], axis=0)
    small = (norm_gain[0], taps, heads, inner)

    span = range(PIECES)
    first, last = section == 0, section == sections - 1
    flip = 1 if place.tensors > 1 else 0

    def leave(place_of, block, came, step, others):
        if came:
            newest = list(came)[-1]
            block, came[newest], others = tie(block, came[newest], others)
        else:
            block, others = tie(block, others)
        came[place_of] = place.next_section(block, step, flip if step > 0 else 0)
        return others

    def arrive(i, came, stays, originals, others, flip):
        block, others = tie(came[i], others)
        return jnp.where(stays, own_share(place, originals[i], flip), block), others

    came = None
    for turn in range(sections - 1):
        carry = forward_start(place, small)
        shares_in, came = came, {}
        pieces, halves, terms, crossing = list(h0), [], None, []
        for i in span:
            if shares_in is not None:
                share, terms = arrive(i, shares_in, first, h0, terms, flip)
                pieces[i] = gather_shares(place, [share], flip)[0]
            if i:
                pieces[i], halves[-1][1] = tie(pieces[i], halves[-1][1])
                crossing = [place.swap_tensor(halves[-1][1], mask) for mask in bits_of(place.tensors)]
            if second.masks[0]:
                second.prepare()
                pieces[i], second.out = tie(pieces[i], second.out)
                second.launch()
                terms, carry = forward_piece(place, pieces[i], weights, small, carry)
                terms, crossing, second.next = tie(terms, crossing, second.next)
                second.land()
            else:
                terms, carry = forward_piece(place, pieces[i], weights, small, carry)
                terms, crossing = tie(terms, crossing)
            if i:
                halves[-1][1] = halves[-1][1] + sum(crossing)
            halves.append([terms[0], sum_all(place, terms[1][0, :, 0], micro=False, tensor=False)])
        halves[-1][1] = sum_all(place, halves[-1][1], micro=False, part=False)
        second.finish()
        if len(weights) == 2:
            weights += tuple(second.result([width]))
        red = []
        for g, squares in halves:
            if red:
                g = red[-1].launch(g)
            elif turn == 0:
                g, cotangent = tie(g, cotangent)
                e_blocks = whole_tokens(place, cotangent)
            own, send = out_call(place, g, factor_of(place, small, squares), weights, small[3])
            red.append(Reduction(place, own, send, jnp.float16))
        red[-1].launch()
        if turn == 0:
            e_blocks = red[0].land(e_blocks)
            e0 = lay_tokens(place, e_blocks)
            e0, dn0 = red[-1].land((e0, [rows_dot(e, weights[2]) for e in e0]))
        for i, item in enumerate(red):
            leave(i, out_share(place, pieces[i], item.result()), came, 1, None)
    second.finish()
    if len(weights) == 2:
        weights += tuple(second.result([width]))
    if sections == 1:
        e0 = lay_tokens(place, whole_tokens(place, cotangent))
        dn0 = [rows_dot(e, weights[2]) for e in e0]

    carry = forward_start(place, small)
    kept, sums, lines, terms, ahead = [], [], [], None, None
    for i in span:
        h = h0[i]
        if came is not None:
            if ahead is None:
                share, terms = arrive(i, came, first, h0, terms, flip)
                ahead = Gathering(place, [share], flip)
                ahead.launch()
                if i + 1 < PIECES:
                    ahead.came, came[i + 1] = tie(ahead.came, came[i + 1])
            h = ahead.result()[0]
            ahead = None
            if i + 1 < PIECES:
                share, h = arrive(i + 1, came, first, h0, h, flip)
                h, share = tie(h, share)
                ahead = Gathering(place, [share], flip)
                ahead.launch()
        terms, carry, keep = forward_piece(place, h, weights, small, carry, dn0[i])
        if ahead is not None:
            terms, ahead.came = tie(terms, ahead.came)
        kept.append(keep)
        lines.append(terms[2][:, :, 0])
        sums.append(Reduction(place, terms[0], terms[1]))
    lines = sum_all(place, jnp.stack(lines), micro=False)
    qs = [factor_of(place, small, lines[i, 0]) for i in span]
    dots = [lines[i, 1] for i in span]

    def gradient_of(i, came, others):
        share, others = arrive(i, came, last, e0, others, 0)
        gathering = Gathering(place, [share])
        gathering.launch()
        return gathering, others

    def outputs_of():
        outs = []
        for k in span:
            branch = sums[k].result() * own_share(place, qs[k].reshape(-1, 1))
            outs.append(out_share(place, kept[k][0], branch))
        return Homing(place, jnp.concatenate(outs, axis=0))

    came, homing, ready = None, None, None
    es = list(e0)
    for turn in range(sections - 1):
        carry = forward_start(place, small)
        shares_in, came = came, {}
        es, terms = list(e0), None
        for i in reversed(span):
            dn, pull = dn0[i], dots[i]
            if shares_in is not None:
                ready, terms = gradient_of(i, shares_in, terms)
                es[i] = ready.result()[0]
                dn, pull, _, _ = normal_piece(es[i], qs[i], kept[i], weights, small)
                pull = sum_all(place, pull, micro=False)
            elif homing is None:
                for item in sums:
                    dn = item.launch(dn)
            gates = gates_piece(place, dn, qs[i], pull, kept[i], small)
            if i + 1 < PIECES:
                gates = leave(i + 1, share, came, -1, gates)
            terms, carry, _, _ = backward_piece(place, False, gates, kept[i], weights, small, carry)
            if i + 1 < PIECES:
                terms, came[i + 1] = tie(terms, came[i + 1])
            if homing is None:
                for item in sums:
                    terms = item.land(terms)
            red = Reduction(place, terms[0], terms[1])
            red.launch()
            if homing is None:
                homing = outputs_of()
            if not i and turn == sections - 2 and PIECES > 1:
                ready, _ = gradient_of(PIECES - 1, came, None)
                ready.came = red.land(ready.came)
            share, _ = input_grad(place, es[i], kept[i][0], norm_gain[0], red)
        leave(0, share, came, -1, None)
    if homing is None:
        for item in sums:
            item.launch()
        homing = outputs_of()

    carry = forward_start(place, small)
    red, matrix, small_sums, terms = [], [None] * 3, None, None

    def add(old, a, b):
        now = columns_dot(a, b)
        return now if old is None else old + now

    for i in reversed(span):
        if came is not None:
            if red or ready is None:
                ready, terms = gradient_of(i, came, terms)
            if red:
                red[-1].prepare()
                homing.collect()
                ready.came, red[-1].going, homing.rows = tie(ready.came, red[-1].going, homing.rows)
            es[i] = ready.result()[0]
        dn, pull, n, gain_grad = normal_piece(es[i], qs[i], kept[i], weights, small)
        pull = sum_all(place, pull, micro=False)
        matrix[0] = add(matrix[0], es[i], n)
        pull, matrix[0] = tie(pull, matrix[0])
        if red:
            pull = homing.turn(red[-1].launch(pull))
        else:
            pull, homing.sends = tie(pull, homing.sends)
            homing.launch()
        gates = gates_piece(place, dn, qs[i], pull, kept[i], small)
        if not i:
            scatter = Scatter(place, [matrix[0].astype(bf16), add(matrix[1], kept[i][2], gates[1]).astype(bf16)])
            scatter.prepare()
            gates, scatter.out = tie(gates, scatter.out)
            scatter.launch()
        terms, carry, dvbd, now = backward_piece(place, True, gates, kept[i], weights, small, carry)
        if red:
            terms = red[-1].land(terms)
        else:
            homing.came, terms, gates, dvbd, now = tie(homing.came, terms, gates, dvbd, now)
            if PIECES == 1:
                homing.turn()
        now = [now, gain_grad]
        if i:
            red.append(Reduction(place, terms[0], terms[1]))
            for k, b in ((1, gates[1]), (2, dvbd)):
                matrix[k] = add(matrix[k], kept[i][2], b)
        else:
            ahead = Reduction(place, terms[0], terms[1])
            ahead.own, dvbd, now, scatter.next, homing.swapped = tie(
                ahead.own, dvbd, now, scatter.next, homing.swapped
            )
            scatter.land()
            red.append(ahead)
        small_sums = now if small_sums is None else [a + b for a, b in zip(small_sums, now)]
    outputs = homing.result().reshape(block_input.shape)
    scatter.prepare()
    scatter.launch()
    red[-1].prepare()
    red[-1].going, dvbd = tie(red[-1].going, dvbd)
    red[-1].launch()
    mixes = Scatter(place, [add(matrix[2], kept[0][2], dvbd).astype(bf16)])
    mixes.prepare()
    mixes.launch()
    grads, norm_grad = [], jnp.zeros((8, norm_gain.shape[1]), f32)
    for i, item in zip(reversed(span), red[:-1]):
        block, now = input_grad(place, es[i], kept[i][0], norm_gain[0], item)
        grads.insert(0, block)
        norm_grad = norm_grad + now
    scatter.next = red[-1].land(scatter.next)
    scatter.land()
    while scatter.left[0]:
        scatter.prepare()
        scatter.launch()
        scatter.land()
    block, now = input_grad(place, es[0], kept[0][0], norm_gain[0], red[-1])
    norm_grad = norm_grad + now
    homing = Homing(place, jnp.concatenate([block] + grads, axis=0))
    homing.launch()
    scatter = scatter.trade()
    gate_grad = columns_beside(place, scatter, width, width)
    out_grad = order([block[:, :width].astype(f32).T for block in scatter], part, 0).reshape(-1, w_out.shape[2])
    homing.came, mixes.next, gate_grad, out_grad = tie(homing.came, mixes.next, gate_grad, out_grad)
    mixes.land()
    mixes.prepare()
    homing.collect()
    mixes.out, homing.rows = tie(mixes.out, homing.rows)
    homing.turn()
    mixes.launch()
    packed, gain_grad = small_sums
    norm_grad = jnp.sum(norm_grad, axis=0)
    row = lax.broadcasted_iota(jnp.int32, (8, mixed), 0)
    packed = jnp.where(row == GAIN_ROW, jnp.pad(gain_grad, ((0, 0), (0, MAPS))), packed)
    lanes = max(mixed, norm_grad.size)
    packed = jnp.concatenate(
        [jnp.pad(packed, ((0, 0), (0, lanes - mixed))), jnp.pad(norm_grad[None], ((0, 7), (0, lanes - norm_grad.size)))],
        axis=0,
    )
    packed, mixes.next = tie(packed, mixes.next)
    mixes.land()
    while mixes.left[0]:
        mixes.prepare()
        mixes.launch()
        mixes.land()
    packed = sum_all(place, packed, part=False, tensor=False)
    by_part = [packed] + [place.swap_part(packed, d) for d in range(1, parts)]
    input_grads = homing.result().reshape(block_input.shape).astype(f32)
    mixes = mixes.trade()
    value_grad = columns_beside(place, mixes, 0, width)
    step_grad = beside([block[:, mixed : mixed + heads_here].astype(f32) for block in mixes], part)
    maps_grad = sum(block[:, width:mixed].astype(f32) for block in mixes).astype(bf16)
    maps_sum = maps_grad.astype(f32)
    for mask in bits_of(place.tensors):
        maps_sum = maps_sum + place.swap_tensor(maps_sum, mask)

    both = by_part[0]
    for distance in range(1, parts):
        both = both + by_part[distance]
    both = sum_all(place, both, micro=False, part=False)
    wide, bias_grad, gain_grad, maps_small, maps_bias, norm_sum, by_head = unpack(
        place, both, by_part, width, heads_here, norm_grad.size
    )
    total_heads = parts * heads_here
    return (
        outputs[None],
        input_grads[None],
        norm_sum,
        gate_grad[None],
        value_grad[None],
        maps_sum[None],
        step_grad[None],
        wide[None],
        maps_small[None],
        bias_grad,
        maps_bias,
        by_head[0:1, :total_heads],
        by_head[1:2, :total_heads],
        by_head[2:3, :total_heads],
        gain_grad,
        out_grad[None],
    )


def solution(mesh):
    placed = (
        P(None, "context", None),
        P("section", None),
        P("section", "context", "tensor"),
        P("section", "context", "tensor"),
        P("section", "context", None),
        P("section", "context", "tensor"),
        P("section", None, "tensor"),
        P("section", None, None),
        P("section", "tensor"),
        P("section", None),
        P("section", "tensor"),
        P("section", "tensor"),
        P("section", "tensor"),
        P("section", "tensor"),
        P("section", "tensor", "context"),
        P(None, "context", None),
    )
    return jax.shard_map(
        body,
        mesh=mesh,
        in_specs=placed,
        out_specs=(
            P("section", None, "context", None),
            P("section", None, "context", None),
            P("section", None),
            P("section", "context", "tensor"),
            P("section", "context", "tensor"),
            P("section", "context", None),
            P("section", "context", "tensor"),
            P("section", None, "tensor"),
            P("section", None, None),
            P("section", "tensor"),
            P("section", None),
            P("section", "tensor"),
            P("section", "tensor"),
            P("section", "tensor"),
            P("section", "tensor"),
            P("section", "tensor", "context"),
        ),
        check_vma=False,
    )
```

```python
import functools

import jax
import jax.numpy as jnp
from jax import lax
from jax.experimental import pallas as pl
from jax.experimental.pallas import tpu as pltpu
from jax.sharding import PartitionSpec as P

HEAD_DIM = 64
STATE = 128
CONV = 4
MAPS = 2 * STATE
CHUNK = 128
LANES = 128
PIECES = 2

epsilon = 1e-05
bf16 = jnp.bfloat16
f32 = jnp.float32


def low_dot(a, b, contract):
    return lax.dot_general(
        a.astype(bf16), b.astype(bf16), ((contract[0], contract[1]), ((), ())), preferred_element_type=f32
    )


def mm(a, b):
    return low_dot(a, b, ((1,), (0,)))


def mm_nt(a, b):
    return low_dot(a, b, ((1,), (1,)))


def mm_tn(a, b):
    return low_dot(a, b, ((0,), (0,)))


def softplus(v):
    return jnp.maximum(v, 0.0) + jnp.log(1.0 + jnp.exp(-jnp.abs(v)))


def groups_of(width):
    return [
        (at, min(LANES, width - at), at // HEAD_DIM, min(LANES, width - at) // HEAD_DIM)
        for at in range(0, width, LANES)
    ]


def head_rows(width):
    return -(-(width // HEAD_DIM) // 16) * 16


def column(cols, head):
    return jnp.broadcast_to(cols[:, head : head + 1], (cols.shape[0], LANES))


def choose(first, second, lanes):
    if second is None:
        return first[:, :lanes]
    lane = lax.broadcasted_iota(jnp.int32, (first.shape[0], lanes), 1)
    return jnp.where(lane < HEAD_DIM, first, second)


def only(value, which, count):
    if count == 1:
        return value
    lane = lax.broadcasted_iota(jnp.int32, value.shape, 1)
    return jnp.where((lane < HEAD_DIM) == (which == 0), value, jnp.zeros_like(value))


def pieces_of(value, count):
    terms = []
    for _ in range(count):
        term = value.astype(bf16)
        terms.append(term)
        value = value - term.astype(f32)
    return terms


def mm3(a, b):
    (a_hi, a_lo), (b_hi, b_lo) = pieces_of(a, 2), pieces_of(b, 2)
    return mm(jnp.concatenate([a_hi, a_lo, a_hi], axis=1), jnp.concatenate([b_hi, b_hi, b_lo], axis=0))


def mm3_nt(a, b):
    (a_hi, a_lo), (b_hi, b_lo) = pieces_of(a, 2), pieces_of(b, 2)
    return mm_nt(jnp.concatenate([a_hi, a_lo, a_hi], axis=1), jnp.concatenate([b_hi, b_hi, b_lo], axis=1))


def sum_dot(value, zero_one, count):
    return sum(mm(term, zero_one) for term in pieces_of(value, count))


def iotas():
    row = lax.broadcasted_iota(jnp.int32, (CHUNK, CHUNK), 0)
    col = lax.broadcasted_iota(jnp.int32, (CHUNK, CHUNK), 1)
    return row, col


def conv_rows(pad, taps_ref, at, lanes):
    here = slice(at, at + lanes)
    pre = taps_ref[CONV : CONV + 1, here] + taps_ref[CONV - 1 : CONV, here] * pad[8 : 8 + CHUNK, here]
    for k in range(CONV - 1):
        first = 8 - (CONV - 1) + k
        pre = pre + taps_ref[k : k + 1, here] * pad[first : first + CHUNK, here]
    return pre


def decay_terms(dt_pre, heads_ref, rows, row, col):
    wide = dt_pre.T[:rows] + heads_ref[0:rows, :]
    dt = softplus(wide)
    log_decay = sum_dot(-heads_ref[rows : 2 * rows, :] * dt, (row <= col).astype(bf16), 3)
    cols = jnp.concatenate([log_decay, dt, jnp.zeros((CHUNK - 2 * rows, CHUNK), f32)], axis=0).T
    return wide, dt, log_decay, cols


def as_row(value):
    return jnp.sum(value.T, axis=0, keepdims=True)


def filled(value):
    rows, lanes = value.shape
    if lanes == LANES:
        return value
    return jnp.concatenate([value, jnp.zeros((rows, LANES - lanes), f32)], axis=1)


def as_column(row):
    return jnp.broadcast_to(row, (CHUNK, LANES)).T


def deal(part, parts, first, count, total, own_ref, send_ref, sems):
    def own_copy(c):
        rows = total.at[pl.ds(pl.multiple_of(c * CHUNK, CHUNK), CHUNK), :]
        return pltpu.make_async_copy(rows, own_ref.at[(first + c) // parts], sems.at[c])

    def one(c, _):
        index = first + c
        distance = (index % parts) ^ part

        @pl.when(distance == 0)
        def _():
            own_copy(c).start()

        @pl.when(distance != 0)
        def _():
            rows = total[pl.ds(pl.multiple_of(c * CHUNK, CHUNK), CHUNK), :]
            send_ref[jnp.maximum(distance - 1, 0), index // parts] = rows.astype(send_ref.dtype)

        return 0

    def end(c, _):
        @pl.when(((first + c) % parts) ^ part == 0)
        def _():
            own_copy(c).wait()

        return 0

    lax.fori_loop(0, count, one, 0)
    lax.fori_loop(0, count, end, 0)


def forward_kernel(keep, width, parts, per_step, part_ref, h_ref, w1_ref, wg_ref, norm_ref, taps_ref, heads_ref, inner_ref, s0_ref, tail0_ref, *rest):
    if keep:
        wo_ref, dn_ref, own_ref, send_ref, sums_ref, st_ref, tail_ref, xn_ref, vbd_ref, z_ref, y_ref, sin_ref, pad, gg, total, sems = rest
    else:
        g_ref, sums_ref, st_ref, tail_ref, xn_ref, vbd_ref, z_ref, pad = rest
    mixed = width + MAPS
    rows = head_rows(width)
    step = pl.program_id(0)

    @pl.when(step == 0)
    def _():
        st_ref[...] = s0_ref[...]
        tail_ref[...] = tail0_ref[...]

    def norm(c, _):
        here = pl.ds(pl.multiple_of(c * 64, 64), 64)
        hf = h_ref[here, :].astype(f32)
        scale = lax.rsqrt(jnp.mean(hf * hf, axis=1, keepdims=True) + epsilon)
        xn_ref[here, :] = (hf * scale * norm_ref[...]).astype(bf16)
        return 0

    lax.fori_loop(0, per_step * 2, norm, 0)
    vbd_ref[...] = jnp.dot(xn_ref[...], w1_ref[...], preferred_element_type=f32)
    z_ref[...] = jnp.dot(xn_ref[...], wg_ref[...], preferred_element_type=f32)
    row, col = iotas()

    def chunk(c, _):
        here = pl.ds(pl.multiple_of(c * CHUNK, CHUNK), CHUNK)
        pad[0:8, :] = tail_ref[...]
        pad[8 : 8 + CHUNK, :] = vbd_ref[here, :mixed]
        tail_ref[...] = pad[CHUNK : CHUNK + 8, :]
        pre = conv_rows(pad, taps_ref, width, MAPS)
        maps = pre * jax.nn.sigmoid(pre)
        b, c_map = maps[:, :STATE], maps[:, STATE:]
        b_rows = b.T
        _, _, log_row, cols = decay_terms(vbd_ref[here, mixed:], heads_ref, rows, row, col)
        contact = jnp.where(row >= col, mm3(c_map, b_rows), 0.0)
        if keep:
            sin_ref[c] = st_ref[...]
        carried = mm3(c_map, st_ref[...])
        squares = jnp.zeros((CHUNK, LANES), f32)
        pulls = jnp.zeros((CHUNK, LANES), f32)
        for at, lanes, head, count in groups_of(width):
            span = slice(at, at + lanes)
            pre = conv_rows(pad, taps_ref, at, lanes)
            own = pre * jax.nn.sigmoid(pre)
            logs = [column(cols, head + j) for j in range(count)]
            steps = [column(cols, rows + head + j) for j in range(count)]
            log_x = choose(logs[0], logs[-1] if count == 2 else None, lanes)
            step_x = choose(steps[0], steps[-1] if count == 2 else None, lanes)
            last_x = log_x[CHUNK - 1 : CHUNK, :]
            xd = own * step_x
            mixing = [
                jnp.exp(jnp.minimum(logs[j] - log_row[head + j : head + j + 1, :], 0.0)) * contact
                for j in range(count)
            ]
            inside = mm3(
                jnp.concatenate(mixing, axis=1),
                jnp.concatenate([only(xd, j, count) for j in range(count)], axis=0),
            )
            y = inside + jnp.exp(log_x) * carried[:, span] + inner_ref[0:1, span] * own
            st_ref[:, span] = jnp.exp(last_x) * st_ref[:, span] + mm3(b_rows, jnp.exp(last_x - log_x) * xd)
            z = z_ref[here, span]
            g = y * (z * jax.nn.sigmoid(z))
            if keep:
                gg[here, span] = (g * inner_ref[1:2, span]).astype(bf16)
                y_ref[here, span] = y
            else:
                g_ref[here, span] = g
            squares = squares + filled(g * g)
            if keep:
                pulls = pulls + filled(dn_ref[here, span] * inner_ref[1:2, span] * g)
        sums_ref[0, c] = as_row(squares)
        if keep:
            sums_ref[1, c] = as_row(pulls)
        return 0

    lax.fori_loop(0, per_step, chunk, 0)
    if keep:
        total[...] = lax.dot_general(
            gg[...], wo_ref[...], (((1,), (1,)), ((), ())), preferred_element_type=f32
        )
        deal(part_ref[0], parts, step * per_step, per_step, total, own_ref, send_ref, sems)


def out_kernel(parts, per_step, part_ref, g_ref, q_ref, inner_ref, wo_ref, own_ref, send_ref, n, total, sems):
    def chunk(c, _):
        here = pl.ds(pl.multiple_of(c * CHUNK, CHUNK), CHUNK)
        q = as_column(q_ref[c])
        for at, lanes, _, _ in groups_of(n.shape[1]):
            span = slice(at, at + lanes)
            n[here, span] = (g_ref[here, span] * q[:, :lanes] * inner_ref[1:2, span]).astype(bf16)
        return 0

    lax.fori_loop(0, per_step, chunk, 0)
    total[...] = lax.dot_general(n[...], wo_ref[...], (((1,), (1,)), ((), ())), preferred_element_type=f32)
    deal(part_ref[0], parts, pl.program_id(0) * per_step, per_step, total, own_ref, send_ref, sems)


def out_call(place, g, q, weights, inner):
    wo = weights[2]
    tokens, width = g.shape
    depth = wo.shape[0]
    chunks = tokens // CHUNK
    per_step = min(STEP, chunks)
    steps = chunks // per_step
    count = per_step * CHUNK
    blocks = chunks // place.parts
    shapes = [(blocks, CHUNK, depth), (place.parts - 1, blocks, CHUNK, depth)]
    return pl.pallas_call(
        functools.partial(out_kernel, place.parts, per_step),
        grid_spec=pltpu.PrefetchScalarGridSpec(
            num_scalar_prefetch=1,
            grid=(steps,),
            in_specs=[
                block(steps, (count, width), lambda i, _: (i, 0)),
                block(steps, (per_step, 1, LANES), lambda i, _: (i, 0, 0)),
                once(inner.shape),
                once(wo.shape),
            ],
            out_specs=[pl.BlockSpec(memory_space=pl.ANY), once(shapes[1])],
            scratch_shapes=[
                pltpu.VMEM((count, width), bf16),
                pltpu.VMEM((count, depth), f32),
                pltpu.SemaphoreType.DMA((per_step,)),
            ],
        ),
        out_shape=[jax.ShapeDtypeStruct(shape, f32) for shape in shapes],
        compiler_params=kernel_params(steps, 8),
        cost_estimate=pl.CostEstimate(
            flops=tokens * width * 6000, bytes_accessed=tokens * depth * 8, transcendentals=0
        ),
        name="out_forward",
    )(place.part.reshape(1), g, q[:, None], inner, wo)


STEP = 4
GAIN_ROW = CONV + 1
HEAD_ROW = CONV + 2


def kernel_params(steps, megabytes):
    return pltpu.CompilerParams(vmem_limit_bytes=(megabytes if steps == 1 else 40) * 1024 * 1024)


def once(shape):
    return pl.BlockSpec(memory_space=pltpu.VMEM)


def block(steps, shape, index_map):
    return once(shape) if steps == 1 else pl.BlockSpec(shape, index_map)


def forward_call(place, h, weights, small, s0, tail0, dn=None):
    w1, wg = weights[:2]
    norm_gain, taps, heads, inner = small
    keep = dn is not None
    tokens, depth = h.shape
    width = inner.shape[1]
    mixed = width + MAPS
    chunks = tokens // CHUNK
    per_step = min(STEP, chunks)
    steps = chunks // per_step
    count = per_step * CHUNK
    blocks = chunks // place.parts
    rows = lambda lanes: block(steps, (count, lanes), lambda i, _: (i, 0))
    if keep:
        shapes = [((blocks, CHUNK, depth), f32), ((place.parts - 1, blocks, CHUNK, depth), bf16)]
        out_shape = [jax.ShapeDtypeStruct(*item) for item in shapes]
        out_specs = [pl.BlockSpec(memory_space=pl.ANY), once(shapes[1][0])]
    else:
        out_shape = [jax.ShapeDtypeStruct((tokens, width), f32)]
        out_specs = [rows(width)]
    out_shape += [
        jax.ShapeDtypeStruct((2, chunks, 1, LANES), f32),
        jax.ShapeDtypeStruct((STATE, width), f32),
        jax.ShapeDtypeStruct((8, mixed), f32),
    ]
    out_specs += [
        block(steps, (2, per_step, 1, LANES), lambda i, _: (0, i, 0, 0)),
        once((STATE, width)),
        once((8, mixed)),
    ]
    in_specs = [
        rows(depth),
        once(w1.shape),
        once(wg.shape),
        once((1, depth)),
        once(taps.shape),
        once(heads.shape),
        once(inner.shape),
        once(s0.shape),
        once(tail0.shape),
    ]
    args = [h, w1, wg, norm_gain[None], taps, heads, inner, s0, tail0]
    held = [((tokens, depth), bf16), ((tokens, w1.shape[1]), f32), ((tokens, width), f32)]
    scratch = []
    if keep:
        in_specs += [once(weights[2].shape), rows(width)]
        args += [weights[2], dn]
        held.append(((tokens, width), f32))
        out_shape += [jax.ShapeDtypeStruct(*item) for item in held]
        out_specs += [rows(shape[1]) for shape, _ in held]
        out_shape.append(jax.ShapeDtypeStruct((chunks, STATE, width), f32))
        out_specs.append(block(steps, (per_step, STATE, width), lambda i, _: (i, 0, 0)))
    else:
        scratch = [pltpu.VMEM((count, shape[1]), kind) for shape, kind in held]
    scratch.append(pltpu.VMEM((CHUNK + 8, mixed), f32))
    if keep:
        scratch += [
            pltpu.VMEM((count, width), bf16),
            pltpu.VMEM((count, depth), f32),
            pltpu.SemaphoreType.DMA((per_step,)),
        ]
    return pl.pallas_call(
        functools.partial(forward_kernel, keep, width, place.parts, per_step),
        grid_spec=pltpu.PrefetchScalarGridSpec(
            num_scalar_prefetch=1, grid=(steps,), in_specs=in_specs, out_specs=out_specs, scratch_shapes=scratch
        ),
        out_shape=out_shape,
        compiler_params=kernel_params(steps, 10 if keep else 11),
        cost_estimate=pl.CostEstimate(
            flops=tokens * width * 40000, bytes_accessed=tokens * depth * 16, transcendentals=0
        ),
        name="section_forward",
    )(place.part.reshape(1), *args)


def normal_kernel(full, width, per_step, e_ref, wo_ref, z_ref, y_ref, q_ref, inner_ref, dn_ref, pull_ref, n_ref, gain_ref, gains):
    dn_ref[...] = jnp.dot(e_ref[...], wo_ref[...], preferred_element_type=f32)

    @pl.when(pl.program_id(0) == 0)
    def _():
        gains[...] = jnp.zeros_like(gains)

    def chunk(c, _):
        here = pl.ds(pl.multiple_of(c * CHUNK, CHUNK), CHUNK)
        q = as_column(q_ref[c])
        pulls = jnp.zeros((CHUNK, LANES), f32)
        for at, lanes, _, _ in groups_of(width):
            span = slice(at, at + lanes)
            z, dn_x, gain = z_ref[here, span], dn_ref[here, span], inner_ref[1:2, span]
            g = y_ref[here, span] * (z * jax.nn.sigmoid(z))
            gq = g * q[:, :lanes]
            pulls = pulls + filled(dn_x * gain * g)
            n_ref[here, span] = (gq * gain).astype(bf16)
            gains[:, span] += fold(dn_x * gq)
        pull_ref[c] = as_row(pulls)
        return 0

    lax.fori_loop(0, per_step, chunk, 0)
    gain_ref[...] = jnp.broadcast_to(jnp.sum(gains[...], axis=0, keepdims=True), gains.shape)


def gate_kernel(width, per_step, total, dn_ref, z_ref, y_ref, q_ref, pull_ref, inner_ref, dy_ref, dz_ref):
    def chunk(c, _):
        here = pl.ds(pl.multiple_of(c * CHUNK, CHUNK), CHUNK)
        q = as_column(q_ref[c])
        pull = as_column(pull_ref[c]) * (q * q * q) * (1.0 / total)
        for at, lanes, _, _ in groups_of(width):
            span = slice(at, at + lanes)
            z, y = z_ref[here, span], y_ref[here, span]
            sig = jax.nn.sigmoid(z)
            silu = z * sig
            dg = q[:, :lanes] * (dn_ref[here, span] * inner_ref[1:2, span]) - y * silu * pull[:, :lanes]
            dy_ref[here, span] = dg * silu
            dz_ref[here, span] = (dg * y * (sig + silu * (1.0 - sig))).astype(bf16)
        return 0

    lax.fori_loop(0, per_step, chunk, 0)


def normal_call(e, weights, z, y, q, inner):
    wo = weights[2]
    tokens, depth = e.shape
    width = inner.shape[1]
    chunks = tokens // CHUNK
    per_step = min(STEP, chunks)
    steps = chunks // per_step
    rows = lambda lanes: block(steps, (per_step * CHUNK, lanes), lambda i: (i, 0))
    lines = block(steps, (per_step, 1, LANES), lambda i: (i, 0, 0))
    return pl.pallas_call(
        functools.partial(normal_kernel, True, width, per_step),
        grid=(steps,),
        in_specs=[rows(depth), once(wo.shape), rows(width), rows(width), lines, once(inner.shape)],
        out_specs=[rows(width), lines, rows(width), once((8, width))],
        out_shape=[
            jax.ShapeDtypeStruct((tokens, width), f32),
            jax.ShapeDtypeStruct((chunks, 1, LANES), f32),
            jax.ShapeDtypeStruct((tokens, width), bf16),
            jax.ShapeDtypeStruct((8, width), f32),
        ],
        scratch_shapes=[pltpu.VMEM((8, width), f32)],
        compiler_params=kernel_params(steps, 4),
        cost_estimate=pl.CostEstimate(
            flops=tokens * width * 9000, bytes_accessed=tokens * depth * 16, transcendentals=0
        ),
        name="norm_backward",
    )(e, wo, z, y, q, inner)


def gate_call(place, dn, z, y, q, pull, inner):
    tokens, width = dn.shape
    chunks = tokens // CHUNK
    per_step = min(STEP, chunks)
    steps = chunks // per_step
    rows = lambda lanes: block(steps, (per_step * CHUNK, lanes), lambda i: (i, 0))
    lines = block(steps, (per_step, 1, LANES), lambda i: (i, 0, 0))
    return pl.pallas_call(
        functools.partial(gate_kernel, width, per_step, place.tensors * place.parts * width),
        grid=(steps,),
        in_specs=[rows(width), rows(width), rows(width), lines, lines, once(inner.shape)],
        out_specs=[rows(width), rows(width)],
        out_shape=[jax.ShapeDtypeStruct((tokens, width), f32), jax.ShapeDtypeStruct((tokens, width), bf16)],
        compiler_params=kernel_params(steps, 4),
        cost_estimate=pl.CostEstimate(
            flops=tokens * width * 6000, bytes_accessed=tokens * width * 16, transcendentals=0
        ),
        name="gate_backward",
    )(dn, z, y, q, pull, inner)


def fold(value):
    return jnp.sum(value.reshape(CHUNK // 8, 8, value.shape[1]), axis=0)


def backward_kernel(
    exact,
    width,
    parts,
    per_step,
    steps,
    part_ref,
    dy_ref,
    dz_ref,
    vbd_ref,
    before_ref,
    sin_ref,
    w1_ref,
    wg_ref,
    taps_ref,
    heads_ref,
    inner_ref,
    g0_ref,
    du0_ref,
    own_ref,
    send_ref,
    dvbd_ref,
    gt_ref,
    dut_ref,
    tapg_ref,
    pad,
    dpad,
    sums,
    y_in,
    dxd_out,
    dy_in_all,
    xd_out_all,
    total,
    taps_sum,
    headg_ref,
    skipg_ref,
    back_all,
    sems,
):
    mixed = width + MAPS
    rows = head_rows(width)
    step = steps - 1 - pl.program_id(0)

    @pl.when(pl.program_id(0) == 0)
    def _():
        gt_ref[...] = g0_ref[...]
        dut_ref[...] = du0_ref[...]
        taps_sum[...] = jnp.zeros_like(taps_sum)
        headg_ref[...] = jnp.zeros_like(headg_ref)
        skipg_ref[...] = jnp.zeros_like(skipg_ref)

    row, col = iotas()
    causal = col >= row
    strict = col > row
    onward = (row >= col).astype(bf16)
    head_of = lax.broadcasted_iota(jnp.int32, (rows, width), 1) // HEAD_DIM
    ones = (head_of == lax.broadcasted_iota(jnp.int32, (rows, width), 0)).astype(bf16)

    def conv_back(here, at, lanes, du):
        span = slice(at, at + lanes)
        dpad[0:CHUNK, span] = du
        m = pad[8 : 8 + CHUNK, span]
        taps_sum[CONV * 8 : CONV * 8 + 8, span] += fold(du)
        taps_sum[CONV * 8 - 8 : CONV * 8, span] += fold(m * du)
        dm = taps_ref[CONV - 1 : CONV, span] * du
        for k in range(CONV - 1):
            first = CONV - 1 - k
            moved = dpad[first : first + CHUNK, span]
            dm = dm + taps_ref[k : k + 1, span] * moved
            taps_sum[k * 8 : k * 8 + 8, span] += fold(m * moved)
        dvbd_ref[here, span] = dm.astype(bf16)

    def chunk(reverse, _):
        c = per_step - 1 - reverse
        here = pl.ds(pl.multiple_of(c * CHUNK, CHUNK), CHUNK)
        dpad[CHUNK : CHUNK + 8, :] = dut_ref[...]
        pad[8 : 8 + CHUNK, :] = vbd_ref[here, :mixed]

        @pl.when(c == 0)
        def _():
            pad[0:8, :] = before_ref[0]

        @pl.when(c != 0)
        def _():
            pad[0:8, :] = vbd_ref[pl.ds(pl.multiple_of(jnp.maximum(c * CHUNK - 8, 0), 8), 8), :mixed]

        pre = conv_rows(pad, taps_ref, width, MAPS)
        sig = jax.nn.sigmoid(pre)
        maps = pre * sig
        maps_slope = sig + maps * (1.0 - sig)
        b_maps, c_maps = maps[:, :STATE], maps[:, STATE:]
        b_low, c_low = b_maps.astype(bf16), c_maps.astype(bf16)
        wide, dt, log_row, cols = decay_terms(vbd_ref[here, mixed:], heads_ref, rows, row, col)
        contact = jnp.where(causal, mm_nt(b_low, c_low), 0.0)
        back_low = gt_ref[...].astype(bf16)
        if exact:
            back_all[...] = gt_ref[...]
        c_rows = c_low.T
        y_in[...] = mm(c_low, sin_ref[c])
        dxd_out[...] = mm(b_low, back_low)
        dcontact = jnp.zeros((CHUNK, CHUNK), f32)
        log_rows, through = [], []
        for at, lanes, head, count in groups_of(width):
            span = slice(at, at + lanes)
            pre = conv_rows(pad, taps_ref, at, lanes)
            sig = jax.nn.sigmoid(pre)
            own = pre * sig
            slope = sig + own * (1.0 - sig)
            logs = [column(cols, head + j) for j in range(count)]
            steps_of = [column(cols, rows + head + j) for j in range(count)]
            log_x = choose(logs[0], logs[-1] if count == 2 else None, lanes)
            step_x = choose(steps_of[0], steps_of[-1] if count == 2 else None, lanes)
            last_x = log_x[CHUNK - 1 : CHUNK, :]
            dy = dy_ref[here, span]
            xd = own * step_x
            xd_low = xd.astype(bf16)
            dy_low = dy.astype(bf16)
            to_end = jnp.exp(last_x - log_x)
            dy_in = jnp.exp(log_x) * dy
            dy_in_low = dy_in.astype(bf16)
            if exact:
                dy_in_all[:, span] = dy_in
                xd_out_all[:, span] = to_end * xd
                dmix = mm3_nt(jnp.concatenate([only(xd, j, count) for j in range(count)], axis=0), dy)
            else:
                dy_in_all[:, span] = dy_in_low
                xd_out_all[:, span] = (to_end * xd).astype(bf16)
                dmix = mm_nt(jnp.concatenate([only(xd_low, j, count) for j in range(count)], axis=0), dy_low)
            mixing, products = [], []
            for j in range(count):
                decay = jnp.exp(jnp.minimum(log_row[head + j : head + j + 1, :] - logs[j], 0.0))
                one = decay * contact
                d_one = dmix[j * CHUNK : (j + 1) * CHUNK]
                dcontact = dcontact + decay * d_one
                mixing.append(one.astype(bf16))
                products.append((one * d_one).astype(bf16))
            dxd_in = mm(
                jnp.concatenate(mixing, axis=1),
                jnp.concatenate([only(dy_low, j, count) for j in range(count)], axis=0),
            )
            later = mm(jnp.concatenate(products, axis=0), onward)
            for j in range(count):
                log_rows.append(
                    jnp.sum(jnp.where(strict, later[j * CHUNK : (j + 1) * CHUNK], 0.0), axis=0, keepdims=True)
                )
            from_end = to_end * dxd_out[:, span]
            dxd = dxd_in + from_end
            sums[0:CHUNK, span] = (dy_in * y_in[:, span]).astype(bf16)
            sums[CHUNK : 2 * CHUNK, span] = (xd * from_end).astype(bf16)
            sums[2 * CHUNK : 3 * CHUNK, span] = (own * dxd).astype(bf16)
            carried = jnp.exp(last_x)
            back = gt_ref[:, span]
            through.append(
                jnp.sum(carried * sin_ref[c, :, span].astype(f32) * back, axis=0, keepdims=True)
            )
            skipg_ref[:, span] += fold(dy * own)
            gt_ref[:, span] = carried * back + mm(c_rows, dy_in_low)
            conv_back(here, at, lanes, (step_x * dxd + inner_ref[0:1, span] * dy) * slope)
        dcontact = jnp.where(causal, dcontact, 0.0)
        if exact:
            db = mm3_nt(xd_out_all[...], back_all[...]) + mm3(dcontact, c_maps)
            dc = mm3_nt(dy_in_all[...], sin_ref[c]) + mm3(dcontact.T, b_maps)
        else:
            db = mm_nt(xd_out_all[...], back_low) + mm(dcontact, c_low)
            dc = mm_nt(dy_in_all[...], sin_ref[c]) + mm_tn(dcontact, b_low)
        conv_back(here, width, STATE, db * maps_slope[:, :STATE])
        conv_back(here, width + STATE, STATE, dc * maps_slope[:, STATE:])
        dut_ref[...] = dpad[0:8, :]

        by_token = mm_nt(ones, sums[...])
        entering = by_token[:, :CHUNK]
        leaving = by_token[:, CHUNK : 2 * CHUNK]
        direct = by_token[:, 2 * CHUNK :]
        ends = jnp.broadcast_to(jnp.concatenate(through, axis=1), (CHUNK, width))
        ends = sum(mm_nt(ones, term) for term in pieces_of(ends, 2))
        inside = log_rows
        if rows > len(log_rows):
            inside = log_rows + [jnp.zeros((rows - len(log_rows), CHUNK), f32)]
        dlog = (
            jnp.concatenate(inside, axis=0)
            + sum_dot(entering, onward, 2)
            + sum_dot(leaving, (row < col).astype(bf16), 2)
            + ends
        )
        rate = heads_ref[rows : 2 * rows, :]
        ddt_pre = (direct - rate * dlog) * jax.nn.sigmoid(wide)
        headg_ref[0:rows, :] += ddt_pre
        headg_ref[rows : 2 * rows, :] += -rate * dt * dlog
        ddt_cols = jnp.concatenate([ddt_pre, jnp.zeros((CHUNK - rows, CHUNK), f32)], axis=0).T
        dvbd_ref[here, mixed:] = ddt_cols.astype(bf16)
        return 0

    lax.fori_loop(0, per_step, chunk, 0)
    nt = (((1,), (1,)), ((), ()))
    total[...] = lax.dot_general(dvbd_ref[...], w1_ref[...], nt, preferred_element_type=f32)
    total[...] += lax.dot_general(dz_ref[...], wg_ref[...], nt, preferred_element_type=f32)

    @pl.when(pl.program_id(0) == steps - 1)
    def _():
        tapg_ref[...] = jnp.zeros_like(tapg_ref)
        for k in range(CONV + 1):
            tapg_ref[k : k + 1, :] = jnp.sum(taps_sum[k * 8 : k * 8 + 8, :], axis=0, keepdims=True)
        skips = jnp.broadcast_to(jnp.sum(skipg_ref[...], axis=0, keepdims=True), (CHUNK, width))
        skips = sum(mm_nt(ones, term) for term in pieces_of(skips, 3))
        by_head = jnp.broadcast_to(jnp.sum(headg_ref[...], axis=1, keepdims=True), (2 * rows, LANES))
        columns = jnp.concatenate([by_head, skips, jnp.zeros((CHUNK - 3 * rows, LANES), f32)], axis=0)
        tapg_ref[HEAD_ROW : HEAD_ROW + 1, 0:LANES] = columns.T[0:1]

    deal(part_ref[0], parts, step * per_step, per_step, total, own_ref, send_ref, sems)


def backward_call(place, exact, dy, dz, vbd, before, states, weights, small, g0, du0):
    w1, wg, _ = weights
    _, taps, heads, inner = small
    tokens, width = dy.shape
    depth = w1.shape[0]
    mixed = width + MAPS
    chunks = tokens // CHUNK
    per_step = min(STEP, chunks)
    steps = chunks // per_step
    count = per_step * CHUNK
    blocks = chunks // place.parts
    rows = lambda lanes: block(steps, (count, lanes), lambda i, _: (steps - 1 - i, 0))
    deep = lambda number, height, lanes: block(
        steps, (number, height, lanes), lambda i, _: (steps - 1 - i, 0, 0)
    )
    shapes = [
        ((STATE, width), f32),
        ((8, mixed), f32),
        ((8, mixed), f32),
    ]
    results = pl.pallas_call(
        functools.partial(backward_kernel, exact, width, place.parts, per_step, steps),
        grid_spec=pltpu.PrefetchScalarGridSpec(
            num_scalar_prefetch=1,
            grid=(steps,),
            in_specs=[
                rows(width),
                rows(width),
                rows(vbd.shape[1]),
                deep(1, 8, mixed),
                deep(per_step, STATE, width),
                once(w1.shape),
                once(wg.shape),
                once(taps.shape),
                once(heads.shape),
                once(inner.shape),
                once(g0.shape),
                once(du0.shape),
            ],
            out_specs=[
                pl.BlockSpec(memory_space=pl.ANY),
                once((place.parts - 1, blocks, CHUNK, depth)),
                rows(vbd.shape[1]),
            ]
            + [once(shape) for shape, _ in shapes],
            scratch_shapes=[
                pltpu.VMEM((CHUNK + 8, mixed), f32),
                pltpu.VMEM((CHUNK + 8, mixed), f32),
                pltpu.VMEM((3 * CHUNK, width), bf16),
                pltpu.VMEM((CHUNK, width), f32),
                pltpu.VMEM((CHUNK, width), f32),
                pltpu.VMEM((CHUNK, width), f32 if exact else bf16),
                pltpu.VMEM((CHUNK, width), f32 if exact else bf16),
                pltpu.VMEM((count, depth), f32),
                pltpu.VMEM((8 * (CONV + 1), mixed), f32),
                pltpu.VMEM((2 * head_rows(width), LANES), f32),
                pltpu.VMEM((8, width), f32),
                pltpu.VMEM((STATE, width), f32),
                pltpu.SemaphoreType.DMA((per_step,)),
            ],
        ),
        out_shape=[
            jax.ShapeDtypeStruct((blocks, CHUNK, depth), f32),
            jax.ShapeDtypeStruct((place.parts - 1, blocks, CHUNK, depth), bf16),
            jax.ShapeDtypeStruct(vbd.shape, bf16),
        ]
        + [jax.ShapeDtypeStruct(*item) for item in shapes],
        compiler_params=kernel_params(steps, 12),
        cost_estimate=pl.CostEstimate(
            flops=tokens * width * 60000, bytes_accessed=tokens * depth * 16, transcendentals=0
        ),
        name="section_backward",
    )(place.part.reshape(1), dy, dz, vbd, before, states, w1, wg, taps, heads, inner, g0, du0)
    own, send, dvbd, gt, dut, sums = results
    return own, send, dvbd, gt, dut, sums


def unpack_kernel(parts, heads, rows, part_ref, both_ref, *refs):
    locals_ref, outs = refs[:parts], refs[parts:]
    wide_ref, bias_ref, gain_ref, maps_ref, maps_bias_ref, norm_ref, heads_ref = outs
    width = wide_ref.shape[1] // parts
    part = part_ref[0]
    lane = lax.broadcasted_iota(jnp.int32, (1, LANES), 1)
    by_head = [jnp.zeros((1, LANES), f32) for _ in range(3)]
    for d in range(parts):
        owner = part ^ d
        here = pl.ds(pl.multiple_of(owner * width, HEAD_DIM), width)
        ref = locals_ref[d]
        if width % LANES == 0:
            wide_ref[:, here] = ref[0:CONV, 0:width]
            bias_ref[:, here] = ref[CONV : CONV + 1, 0:width]
            gain_ref[:, here] = ref[GAIN_ROW : GAIN_ROW + 1, 0:width]
        else:
            for p in range(parts):

                @pl.when(owner == p)
                def _():
                    there = slice(p * width, (p + 1) * width)
                    wide_ref[:, there] = ref[0:CONV, 0:width]
                    bias_ref[:, there] = ref[CONV : CONV + 1, 0:width]
                    gain_ref[:, there] = ref[GAIN_ROW : GAIN_ROW + 1, 0:width]

        for k in range(3):
            values = ref[HEAD_ROW : HEAD_ROW + 1, 0:LANES]
            for p in range(parts):
                moved = pltpu.roll(values, (p * heads - k * rows) % LANES, 1)
                chosen = (owner == p) & (lane >= p * heads) & (lane < (p + 1) * heads)
                by_head[k] = jnp.where(chosen, moved, by_head[k])
    heads_ref[...] = jnp.concatenate(by_head + [jnp.zeros((5, LANES), f32)], axis=0)
    maps_ref[...] = both_ref[0:CONV, width : width + MAPS]
    maps_bias_ref[...] = both_ref[CONV : CONV + 1, width : width + MAPS]
    norm_ref[...] = both_ref[8:9, 0 : norm_ref.shape[1]]


def unpack(place, both, by_part, width, heads, depth):
    total = place.parts * width
    shapes = [(CONV, total), (1, total), (1, total), (CONV, MAPS), (1, MAPS), (1, depth), (8, LANES)]
    return pl.pallas_call(
        functools.partial(unpack_kernel, place.parts, heads, head_rows(width)),
        grid_spec=pltpu.PrefetchScalarGridSpec(
            num_scalar_prefetch=1,
            grid=(1,),
            in_specs=[once(both.shape)] * (1 + place.parts),
            out_specs=[once(shape) for shape in shapes],
        ),
        out_shape=[jax.ShapeDtypeStruct(shape, f32) for shape in shapes],
        compiler_params=pltpu.CompilerParams(vmem_limit_bytes=4 * 1024 * 1024),
        name="unpack_small",
    )(place.part.reshape(1), both, *by_part)


class Place:
    def __init__(self, micro_count):
        self.context = lax.axis_size("context")
        self.micros = micro_count
        self.parts = self.context // micro_count
        self.tensors = lax.axis_size("tensor")
        index = lax.axis_index("context")
        self.micro = index // self.parts
        self.part = index % self.parts
        self.tensor = lax.axis_index("tensor")

    def swap_part(self, block, mask):
        return lax.ppermute(block, "context", [(i, i ^ mask) for i in range(self.context)])

    def swap_micro(self, block, mask):
        return self.swap_part(block, mask * self.parts)

    def swap_tensor(self, block, mask):
        return lax.ppermute(block, "tensor", [(i, i ^ mask) for i in range(self.tensors)])

    def next_section(self, block, step, flip):
        count, tensors = lax.axis_size("section"), self.tensors
        return lax.ppermute(
            block,
            ("section", "tensor"),
            [
                (i * tensors + t, (i + step) * tensors + (t ^ flip))
                for i in range(count)
                if 0 <= i + step < count
                for t in range(tensors)
            ],
        )


def pick(array, index, axis):
    return lax.dynamic_index_in_dim(array, index, axis, False)


def tie(*items):
    return lax.optimization_barrier(items)


def bits_of(count):
    masks = []
    mask = 1
    while mask < count:
        masks.append(mask)
        mask *= 2
    return masks


def order_kernel(count, axis, index_ref, *refs):
    blocks, out, sems = refs[:count], refs[count], refs[count + 1]
    copies = []
    for d, one in enumerate(blocks):
        there = (slice(None),) * axis + (index_ref[0] ^ d,)
        copies.append(pltpu.make_async_copy(one, out.at[there], sems.at[d]))
    for one in copies:
        one.start()
    for one in copies:
        one.wait()


def order(blocks, index, axis, copies=True):
    count = len(blocks)
    shape = list(blocks[0].shape)
    shape.insert(axis, count)
    if count == 1:
        return blocks[0].reshape(shape)
    if copies and axis <= blocks[0].ndim - 2 and shape[-2] % 16 == 0 and shape[-1] >= LANES:
        return pl.pallas_call(
            functools.partial(order_kernel, count, axis),
            grid_spec=pltpu.PrefetchScalarGridSpec(
                num_scalar_prefetch=1,
                grid=(1,),
                in_specs=[pl.BlockSpec(memory_space=pl.ANY)] * count,
                out_specs=pl.BlockSpec(memory_space=pltpu.VMEM),
                scratch_shapes=[pltpu.SemaphoreType.DMA((count,))],
            ),
            out_shape=jax.ShapeDtypeStruct(tuple(shape), blocks[0].dtype),
            compiler_params=pltpu.CompilerParams(vmem_limit_bytes=4 * 1024 * 1024),
            name="order_blocks",
        )(index.reshape(1).astype(jnp.int32), *blocks)
    place = lax.broadcasted_iota(jnp.int32, shape, axis) ^ index
    result = jnp.expand_dims(blocks[0], axis)
    for d in range(1, count):
        result = jnp.where(place == d, jnp.expand_dims(blocks[d], axis), result)
    return jnp.broadcast_to(result, shape)


def beside(blocks, index):
    count = len(blocks)
    if count == 2:
        return jnp.where(
            index == 0, jnp.concatenate(blocks, axis=-1), jnp.concatenate(blocks[::-1], axis=-1)
        )
    return jnp.concatenate(
        [pick(order(blocks, index, 0), i, 0) for i in range(count)], axis=-1
    )


def sum_all(place, block, micro=True, part=True, tensor=True):
    if part:
        for mask in bits_of(place.parts):
            block = block + place.swap_part(block, mask)
    if tensor:
        for mask in bits_of(place.tensors):
            block = block + place.swap_tensor(block, mask)
    if micro:
        for mask in bits_of(place.micros):
            block = block + place.swap_micro(block, mask)
    return block


def lay_kernel(sizes, widths, places_ref, *refs):
    pieces, outs, sems = refs[: len(sizes)], refs[len(sizes) : -1], refs[-1]
    copies, number = [], 0
    for piece, size in zip(pieces, sizes):
        for row in range(size):
            at = 0
            for k, lanes in enumerate(widths):
                copies.append(
                    pltpu.make_async_copy(
                        piece.at[row, :, pl.ds(at, lanes)], outs[k].at[places_ref[number]], sems.at[number, k]
                    )
                )
                at += lanes
            number += 1
    for one in copies:
        one.start()
    for one in copies:
        one.wait()


def lay_rows(pieces, places, widths):
    rows = pieces[0].shape[1]
    sizes = [piece.shape[0] for piece in pieces]
    count = sum(sizes)
    if any(lanes % LANES for lanes in widths):
        whole = jnp.zeros((count,) + pieces[0].shape[1:], pieces[0].dtype)
        for i, row in enumerate(row for piece in pieces for row in piece):
            whole = lax.dynamic_update_index_in_dim(whole, row, places[i], 0)
        whole = whole.reshape(count * rows, -1)
        starts = [sum(widths[:k]) for k in range(len(widths))]
        return [whole[:, at : at + lanes] for at, lanes in zip(starts, widths)]
    results = pl.pallas_call(
        functools.partial(lay_kernel, sizes, widths),
        grid_spec=pltpu.PrefetchScalarGridSpec(
            num_scalar_prefetch=1,
            grid=(1,),
            in_specs=[pl.BlockSpec(memory_space=pl.ANY)] * len(pieces),
            out_specs=[pl.BlockSpec(memory_space=pltpu.VMEM)] * len(widths),
            scratch_shapes=[pltpu.SemaphoreType.DMA((count, len(widths)))],
        ),
        out_shape=[jax.ShapeDtypeStruct((count, rows, lanes), pieces[0].dtype) for lanes in widths],
        compiler_params=pltpu.CompilerParams(vmem_limit_bytes=4 * 1024 * 1024),
        name="lay_rows",
    )(jnp.stack(places).astype(jnp.int32), *pieces)
    return [result.reshape(count * rows, -1) for result in results]


class Collect:
    def __init__(self, place, blocks):
        self.place = place
        self.found = [[block] for block in blocks]
        self.distances = [[0] for _ in blocks]
        self.masks = [bits_of(place.micros)[:: -1 if p % 2 else 1] for p in range(len(blocks))]

    def prepare(self):
        self.out = [found[0] if len(found) == 1 else jnp.concatenate(found, axis=0) for found in self.found]

    def launch(self):
        self.next = [self.place.swap_micro(block, masks[0]) for block, masks in zip(self.out, self.masks)]

    def land(self):
        for p, block in enumerate(self.next):
            mask = self.masks[p].pop(0)
            self.found[p].append(block)
            self.distances[p] += [distance ^ mask for distance in self.distances[p]]

    def finish(self):
        while self.masks[0]:
            self.prepare()
            self.launch()
            self.land()

    def result(self, widths):
        place, pieces, places = self.place, [], []
        for p, found in enumerate(self.found):
            pieces += found
            places += [(place.micro ^ distance) * place.parts + (place.part ^ p) for distance in self.distances[p]]
        return lay_rows(pieces, places, widths)


def gather_weights(place, w_gate, w_value, w_bc, w_dt, w_out):
    parts = place.parts
    width = w_gate.shape[1] // parts
    heads = w_dt.shape[1] // parts

    def cut_of(array, part):
        return lax.dynamic_slice_in_dim(array, part * width, width, 1)

    def columns_of(part):
        steps = lax.dynamic_slice_in_dim(w_dt, part * heads, heads, 1)
        steps = jnp.pad(steps, ((0, 0), (0, LANES - heads)))
        return jnp.concatenate([cut_of(w_value, part), w_bc, steps, cut_of(w_gate, part)], axis=1)[None]

    def collected(make):
        blocks = [make(place.part ^ p) for p in range(parts)]
        return Collect(place, blocks[:1] + [place.swap_part(block, p + 1) for p, block in enumerate(blocks[1:])])

    first = collected(columns_of)
    second = collected(lambda part: cut_of(w_out.T, part)[None])
    return first, second


def whole_tokens(place, rows):
    return [pick(rows, place.micro, 0)] + [
        place.swap_micro(pick(rows, place.micro ^ d, 0), d) for d in range(1, place.micros)
    ]


def lay_tokens(place, blocks):
    held = order(blocks, place.micro, 0, False)
    whole = order([held] + [place.swap_part(held, d) for d in range(1, place.parts)], place.part, 1, False)
    size = place.micros // PIECES
    return [whole[i * size : (i + 1) * size].reshape(-1, held.shape[-1]) for i in range(PIECES)]


class Spread:
    def __init__(self, place, rows):
        self.place, self.rows = place, rows
        micros, count, width = rows.shape
        view = rows.reshape(micros, place.tensors, count // place.tensors, width)
        self.shares = jnp.stack(
            [place.swap_micro(pick(pick(view, place.micro ^ d, 0), place.tensor, 0), d) for d in range(1, micros)]
        )
        self.came = [place.swap_tensor(self.shares, d) for d in range(1, place.tensors)]

    def result(self):
        place = self.place
        both = [self.shares] + self.came
        blocks = [pick(self.rows, place.micro, 0)]
        for d in range(place.micros - 1):
            whole = order([part[d] for part in both], place.tensor, 0, False)
            blocks.append(whole.reshape(-1, self.rows.shape[2]))
        return lay_tokens(place, blocks)


def blocks_of(place, array):
    return array.reshape(place.micros // PIECES, place.parts, place.tensors, -1, array.shape[-1])


def own_share(place, array, flip=0):
    return pick(pick(blocks_of(place, array), place.part, 1), place.tensor ^ flip, 1)


GROUP = 16


def split_kernel(parts, tensors, tensor_ref, own_ref, *refs):
    came, going_ref, kept_ref = refs[: parts - 1], refs[-2], refs[-1]
    rows = kept_ref.shape[1]

    def group(i, _):
        here = pl.ds(pl.multiple_of(i * GROUP, GROUP), GROUP)
        for d in range(tensors):
            start = (tensor_ref[0] ^ d) * rows + i * GROUP
            there = pl.ds(pl.multiple_of(start, GROUP), GROUP)
            total = own_ref[0, there, :]
            for one in came:
                total = total + one[0, there, :].astype(f32)
            if d:
                going_ref[d - 1, 0, here, :] = total.astype(bf16)
            else:
                kept_ref[0, here, :] = total
        return 0

    lax.fori_loop(0, rows // GROUP, group, 0)


def split_call(place, own, came):
    blocks, tokens, depth = own.shape
    rows = tokens // place.tensors
    others = place.tensors - 1
    return pl.pallas_call(
        functools.partial(split_kernel, place.parts, place.tensors),
        grid_spec=pltpu.PrefetchScalarGridSpec(
            num_scalar_prefetch=1,
            grid=(blocks,),
            in_specs=[pl.BlockSpec((1, tokens, depth), lambda b, _: (b, 0, 0))] * place.parts,
            out_specs=[
                pl.BlockSpec((others, 1, rows, depth), lambda b, _: (0, b, 0, 0)),
                pl.BlockSpec((1, rows, depth), lambda b, _: (b, 0, 0)),
            ],
        ),
        out_shape=[
            jax.ShapeDtypeStruct((others, blocks, rows, depth), bf16),
            jax.ShapeDtypeStruct((blocks, rows, depth), f32),
        ],
        compiler_params=pltpu.CompilerParams(vmem_limit_bytes=8 * 1024 * 1024),
        name="split_terms",
    )(place.tensor.reshape(1), own, *came)


def finish_kernel(places_ref, kept_ref, h_ref, e_ref, norm_ref, *refs):
    sent, grad_ref, sum_ref = refs[:-2], refs[-2], refs[-1]
    rows = kept_ref.shape[1]

    @pl.when(pl.program_id(0) == 0)
    def _():
        sum_ref[...] = jnp.zeros_like(sum_ref)

    def group(i, _):
        here = pl.ds(pl.multiple_of(i * GROUP, GROUP), GROUP)
        dxn = kept_ref[0, here, :]
        for one in sent:
            dxn = dxn + one[0, here, :].astype(f32)
        h = h_ref[0, 0, 0, here, :].astype(f32)
        r = lax.rsqrt(jnp.mean(h * h, axis=1, keepdims=True) + epsilon)
        scaled = dxn * norm_ref[...]
        pull = r * r * r * jnp.mean(scaled * h, axis=1, keepdims=True)
        grad_ref[0, here, :] = (e_ref[0, 0, 0, here, :].astype(f32) + r * scaled - h * pull).astype(bf16)
        found = dxn * h * r
        sum_ref[...] += found[0:8] + found[8:16]
        return 0

    lax.fori_loop(0, rows // GROUP, group, 0)


def finish_call(place, kept, sent, h, e, norm_gain):
    blocks, rows, depth = kept.shape
    share = pl.BlockSpec((1, rows, depth), lambda b, _: (b, 0, 0))
    whole = pl.BlockSpec((1, 1, 1, rows, depth), lambda b, places: (b, places[0], places[1], 0, 0))
    return pl.pallas_call(
        finish_kernel,
        grid_spec=pltpu.PrefetchScalarGridSpec(
            num_scalar_prefetch=1,
            grid=(blocks,),
            in_specs=[share, whole, whole, pl.BlockSpec((1, depth), lambda b, _: (0, 0))] + [share] * len(sent),
            out_specs=[share, pl.BlockSpec((8, depth), lambda b, _: (0, 0))],
        ),
        out_shape=[jax.ShapeDtypeStruct(kept.shape, bf16), jax.ShapeDtypeStruct((8, depth), f32)],
        compiler_params=pltpu.CompilerParams(vmem_limit_bytes=8 * 1024 * 1024),
        name="finish_gradient",
    )(jnp.stack([place.part, place.tensor]), kept, blocks_of(place, h), blocks_of(place, e), norm_gain[None], *sent)


def deal_kernel(parts, widths, rounds, part_ref, *refs):
    mine_ref, send_ref = refs[-2], refs[-1]
    each = len(widths) + rounds
    rows = mine_ref.shape[0]

    def group(i, _):
        here = pl.ds(pl.multiple_of(i * GROUP, GROUP), GROUP)
        for p in range(parts):
            arrays = refs[p * each : (p + 1) * each]
            total = jnp.concatenate([one[here, :].astype(f32) for one in arrays[: len(widths)]], axis=1)
            for one in arrays[len(widths) :]:
                total = total + one[here, :].astype(f32)
            distance = part_ref[0] ^ p

            @pl.when(distance == 0)
            def _():
                mine_ref[here, :] = total

            @pl.when(distance != 0)
            def _():
                send_ref[jnp.maximum(distance - 1, 0), here, :] = total.astype(bf16)

        return 0

    lax.fori_loop(0, rows // GROUP, group, 0)


def deal_call(place, groups, came):
    widths = [block.shape[-1] for block in groups[0]]
    rows, total = groups[0][0].shape[0], sum(widths)
    args = [one for held, round_ in zip(groups, came) for one in list(held) + list(round_)]
    others = place.parts - 1
    step = 3 * GROUP
    return pl.pallas_call(
        functools.partial(deal_kernel, place.parts, widths, len(came[0])),
        grid_spec=pltpu.PrefetchScalarGridSpec(
            num_scalar_prefetch=1,
            grid=(rows // step,),
            in_specs=[pl.BlockSpec((step, one.shape[1]), lambda i, _: (i, 0)) for one in args],
            out_specs=[
                pl.BlockSpec((step, total), lambda i, _: (i, 0)),
                pl.BlockSpec((others, step, total), lambda i, _: (0, i, 0)),
            ],
        ),
        out_shape=[jax.ShapeDtypeStruct((rows, total), f32), jax.ShapeDtypeStruct((others, rows, total), bf16)],
        compiler_params=pltpu.CompilerParams(vmem_limit_bytes=8 * 1024 * 1024),
        name="deal_rows",
    )(place.part.reshape(1), *args)


def beside_kernel(parts, at, part_ref, *refs):
    blocks, out_ref = refs[:parts], refs[-1]
    rows, width = out_ref.shape[0], out_ref.shape[1] // parts

    def group(i, _):
        here = pl.ds(pl.multiple_of(i * GROUP, GROUP), GROUP)
        for d, one in enumerate(blocks):
            there = pl.ds(pl.multiple_of((part_ref[0] ^ d) * width, LANES), width)
            out_ref[here, there] = one[here, at : at + width].astype(f32)
        return 0

    lax.fori_loop(0, rows // GROUP, group, 0)


def columns_beside(place, blocks, at, width):
    if width % LANES or at % LANES:
        return beside([block[:, at : at + width].astype(f32) for block in blocks], place.part)
    shape = (blocks[0].shape[0], place.parts * width)
    step = 3 * GROUP
    return pl.pallas_call(
        functools.partial(beside_kernel, place.parts, at),
        grid_spec=pltpu.PrefetchScalarGridSpec(
            num_scalar_prefetch=1,
            grid=(shape[0] // step,),
            in_specs=[pl.BlockSpec((step, block.shape[1]), lambda i, _: (i, 0)) for block in blocks],
            out_specs=pl.BlockSpec((step, shape[1]), lambda i, _: (i, 0)),
        ),
        out_shape=jax.ShapeDtypeStruct(shape, f32),
        compiler_params=pltpu.CompilerParams(vmem_limit_bytes=8 * 1024 * 1024),
        name="columns_beside",
    )(place.part.reshape(1), *blocks)


def cut(place, block):
    return block.reshape(block.shape[:-2] + (place.tensors, -1, block.shape[-1]))


class Reduction:
    def __init__(self, place, own, send, kind=bf16):
        self.place, self.kind, self.going = place, kind, None
        sends = [send.reshape(own.shape)] if place.parts == 2 else [send[d] for d in range(place.parts - 1)]
        self.came = [place.swap_part(block, d + 1) for d, block in enumerate(sends)]
        self.own = own

    def prepare(self):
        place = self.place
        if self.kind == bf16:
            going, self.kept = split_call(place, self.own, self.came)
            self.going = [going.reshape(self.kept.shape)] if place.tensors == 2 else list(going)
        else:
            own, came = cut(place, self.own), [cut(place, block) for block in self.came]

            def side(tensor):
                return pick(own, tensor, 1) + sum(pick(block, tensor, 1).astype(f32) for block in came)

            self.going = [side(place.tensor ^ d).astype(self.kind) for d in range(1, place.tensors)]
            self.kept = side(place.tensor)

    def launch(self, others=None):
        if self.going is None:
            self.prepare()
        self.going, others = tie(self.going, others)
        self.sent = [self.place.swap_tensor(block, d + 1) for d, block in enumerate(self.going)]
        return others

    def land(self, others):
        self.sent, others = tie(self.sent, others)
        return others

    def result(self):
        return self.kept + sum(block.astype(f32) for block in self.sent)


class Gathering:
    def __init__(self, place, shares, flip=0):
        self.place, self.shares, self.flip = place, shares, flip
        self.came = None

    def launch(self):
        place = self.place
        self.came = [[place.swap_tensor(share, d) for share in self.shares] for d in range(1, place.tensors)]

    def result(self):
        place = self.place
        came = tie(self.came)[0]
        held = [order(list(group), place.tensor ^ self.flip, 1) for group in zip(self.shares, *came)]
        came = tie([[place.swap_part(block, d) for block in held] for d in range(1, place.parts)])[0]
        whole = [order(list(group), place.part, 1) for group in zip(held, *came)]
        return [block.reshape((-1,) + share.shape[2:]) for block, share in zip(whole, self.shares)]


def gather_shares(place, shares, flip=0):
    gathering = Gathering(place, shares, flip)
    gathering.launch()
    return gathering.result()


class Homing:
    def __init__(self, place, own):
        self.place = place
        self.rows = None
        self.own = pick(own, place.micro, 0)
        self.sends = [pick(own, place.micro ^ d, 0) for d in range(1, place.micros)]

    def launch(self):
        self.came = [self.place.swap_micro(block, d + 1) for d, block in enumerate(self.sends)]

    def collect(self):
        self.rows = order([self.own] + self.came, self.place.micro, 0)

    def turn(self, others=None):
        place = self.place
        if self.rows is None:
            self.collect()
        self.rows, others = tie(self.rows, others)
        self.swapped = [place.swap_tensor(self.rows, d) for d in range(1, place.tensors)]
        return others

    def result(self):
        return order([self.rows] + self.swapped, self.place.tensor, 1)


def rows_dot(a, b):
    return jnp.dot(a, b, preferred_element_type=f32)


def columns_dot(a, b):
    return lax.dot_general(a, b, (((0,), (0,)), ((), ())), preferred_element_type=f32)


def forward_piece(place, h, weights, small, carry, dn=None):
    results = forward_call(place, h, weights, small, carry[0], carry[1], dn)
    if dn is None:
        return results[:2], (results[2], results[3])
    kept = (h, carry[1]) + tuple(results[5:])
    return results[:3], (results[3], results[4]), kept


def forward_start(place, small):
    width = small[3].shape[1]
    return jnp.zeros((STATE, width), f32), jnp.zeros((8, width + MAPS), f32)


def factor_of(place, small, squares):
    return lax.rsqrt(squares / (place.tensors * place.parts * small[3].shape[1]) + epsilon)


def out_share(place, h, branch):
    return (own_share(place, h).astype(f32) + branch).astype(bf16)


def gates_piece(place, dn, q, pull, kept, small):
    _, _, _, _, z, y, _ = kept
    return gate_call(place, dn, z, y, q[:, None], pull[:, None], small[3])


def normal_piece(e, q, kept, weights, small):
    _, _, _, _, z, y, _ = kept
    dn, pull, n, gain = normal_call(e, weights, z, y, q[:, None], small[3])
    return dn, pull[:, 0], n, gain


def backward_piece(place, exact, gates, kept, weights, small, carry):
    _, before, _, vbd, _, _, states = kept
    mixed = small[3].shape[1] + MAPS
    count = min(STEP * CHUNK, vbd.shape[0])
    tails = vbd.reshape(-1, count, vbd.shape[1])[:-1, count - 8 :, :mixed]
    before = jnp.concatenate([before[None], tails], axis=0)
    own, send, dvbd, adjoint, du, sums = backward_call(
        place, exact, gates[0], gates[1], vbd, before, states, weights, small, carry[0], carry[1]
    )
    return (own, send), (adjoint, du), dvbd, sums


def input_grad(place, e, h, norm_gain, item):
    return finish_call(place, item.kept, item.sent, h, e, norm_gain)


class Scatter:
    def __init__(self, place, arrays):
        self.place = place
        parts = place.parts
        shape = [2] * len(bits_of(place.micros))
        views = [array.reshape(place.micros, parts, -1, array.shape[1]) for array in arrays]
        self.held = [[view[:, p].reshape(shape + list(view.shape[2:])) for view in views] for p in range(parts)]
        self.came = [[] for _ in range(parts)]
        self.left = [sorted(bits_of(place.micros), reverse=True) for _ in range(parts)]

    def prepare(self):
        place = self.place
        self.out, self.masks = [], []
        for p, left in enumerate(self.left):
            mask = left[0] if p % 2 else left[-1]
            axis = left.index(mask)
            mine = (place.micro // mask) % 2

            def side(bit):
                total = jnp.concatenate([pick(block, bit, axis) for block in self.held[p]], axis=-1)
                for block in self.came[p]:
                    total = total.astype(f32) + pick(block, bit, axis).astype(f32)
                return total.astype(bf16)

            self.out.append(side(1 - mine))
            self.masks.append(mask)
            self.held[p] = [pick(block, mine, axis) for block in self.held[p]]
            self.came[p] = [pick(block, mine, axis) for block in self.came[p]]
            left.remove(mask)

    def launch(self):
        self.next = [self.place.swap_micro(block, mask) for block, mask in zip(self.out, self.masks)]

    def land(self):
        for p, block in enumerate(self.next):
            self.came[p].append(block)

    def trade(self):
        place = self.place
        mine, send = deal_call(place, self.held, self.came)
        sends = [send.reshape(mine.shape)] if place.parts == 2 else list(send)
        return [mine] + [place.swap_part(block, d + 1) for d, block in enumerate(sends)]


def body(
    block_input,
    norm_gain,
    w_gate,
    w_value,
    w_bc,
    w_dt,
    conv_value,
    conv_bc,
    conv_value_bias,
    conv_bc_bias,
    dt_bias,
    decay_log,
    skip,
    gate_gain,
    w_out,
    cotangent,
):
    sections = lax.axis_size("section")
    section = lax.axis_index("section")
    place = Place(block_input.shape[0])
    parts, part = place.parts, place.part
    width = w_gate.shape[2] // parts
    heads_here = w_dt.shape[2] // parts
    mixed = width + MAPS

    def share(vector, size):
        return lax.dynamic_slice_in_dim(vector, part * size, size, vector.ndim - 1)

    def padded(vector):
        return jnp.pad(vector, (0, head_rows(width) - heads_here))

    spread = Spread(place, block_input)
    collected, second = gather_weights(place, w_gate[0], w_value[0], w_bc[0], w_dt[0], w_out[0])
    collected.prepare()
    collected.launch()
    spread.came, collected.next = tie(spread.came, collected.next)
    collected.land()
    h0 = spread.result()
    while collected.masks[0]:
        collected.prepare()
        collected.launch()
        h0, collected.next = tie(h0, collected.next)
        collected.land()
    weights = tuple(collected.result([mixed + LANES, width]))
    taps = jnp.concatenate(
        [
            jnp.concatenate([share(conv_value[0], width), conv_bc[0]], axis=1),
            jnp.concatenate([share(conv_value_bias[0], width), conv_bc_bias[0]])[None],
            jnp.zeros((8 - CONV - 1, mixed), f32),
        ],
        axis=0,
    )
    own_skip = share(skip[0], heads_here)
    rate = jnp.exp(share(decay_log[0], heads_here))
    heads = jnp.concatenate([padded(share(dt_bias[0], heads_here)), padded(rate)])
    heads = jnp.broadcast_to(heads[:, None], (heads.size, LANES))
    inner = jnp.stack([jnp.repeat(own_skip, HEAD_DIM), share(gate_gain[0], width)])
    inner = jnp.concatenate([inner, jnp.zeros((6, width), f32)], axis=0)
    small = (norm_gain[0], taps, heads, inner)

    span = range(PIECES)
    first, last = section == 0, section == sections - 1
    flip = 1 if place.tensors > 1 else 0

    def leave(place_of, block, came, step, others):
        if came:
            newest = list(came)[-1]
            block, came[newest], others = tie(block, came[newest], others)
        else:
            block, others = tie(block, others)
        came[place_of] = place.next_section(block, step, flip if step > 0 else 0)
        return others

    def arrive(i, came, stays, originals, others, flip):
        block, others = tie(came[i], others)
        return jnp.where(stays, own_share(place, originals[i], flip), block), others

    came = None
    for turn in range(sections - 1):
        carry = forward_start(place, small)
        shares_in, came = came, {}
        pieces, halves, terms, crossing = list(h0), [], None, []
        for i in span:
            if shares_in is not None:
                share, terms = arrive(i, shares_in, first, h0, terms, flip)
                pieces[i] = gather_shares(place, [share], flip)[0]
            if i:
                pieces[i], halves[-1][1] = tie(pieces[i], halves[-1][1])
                crossing = [place.swap_tensor(halves[-1][1], mask) for mask in bits_of(place.tensors)]
            if second.masks[0]:
                second.prepare()
                pieces[i], second.out = tie(pieces[i], second.out)
                second.launch()
                terms, carry = forward_piece(place, pieces[i], weights, small, carry)
                terms, crossing, second.next = tie(terms, crossing, second.next)
                second.land()
            else:
                terms, carry = forward_piece(place, pieces[i], weights, small, carry)
                terms, crossing = tie(terms, crossing)
            if i:
                halves[-1][1] = halves[-1][1] + sum(crossing)
            halves.append([terms[0], sum_all(place, terms[1][0, :, 0], micro=False, tensor=False)])
        halves[-1][1] = sum_all(place, halves[-1][1], micro=False, part=False)
        second.finish()
        if len(weights) == 2:
            weights += tuple(second.result([width]))
        red = []
        for g, squares in halves:
            if red:
                g = red[-1].launch(g)
            elif turn == 0:
                g, cotangent = tie(g, cotangent)
                e_blocks = whole_tokens(place, cotangent)
            own, send = out_call(place, g, factor_of(place, small, squares), weights, small[3])
            red.append(Reduction(place, own, send, jnp.float16))
        red[-1].launch()
        if turn == 0:
            e_blocks = red[0].land(e_blocks)
            e0 = lay_tokens(place, e_blocks)
            e0, dn0 = red[-1].land((e0, [rows_dot(e, weights[2]) for e in e0]))
        for i, item in enumerate(red):
            leave(i, out_share(place, pieces[i], item.result()), came, 1, None)
    second.finish()
    if len(weights) == 2:
        weights += tuple(second.result([width]))
    if sections == 1:
        e0 = lay_tokens(place, whole_tokens(place, cotangent))
        dn0 = [rows_dot(e, weights[2]) for e in e0]

    carry = forward_start(place, small)
    kept, sums, lines, terms, ahead = [], [], [], None, None
    for i in span:
        h = h0[i]
        if came is not None:
            if ahead is None:
                share, terms = arrive(i, came, first, h0, terms, flip)
                ahead = Gathering(place, [share], flip)
                ahead.launch()
                if i + 1 < PIECES:
                    ahead.came, came[i + 1] = tie(ahead.came, came[i + 1])
            h = ahead.result()[0]
            ahead = None
            if i + 1 < PIECES:
                share, h = arrive(i + 1, came, first, h0, h, flip)
                h, share = tie(h, share)
                ahead = Gathering(place, [share], flip)
                ahead.launch()
        terms, carry, keep = forward_piece(place, h, weights, small, carry, dn0[i])
        if ahead is not None:
            terms, ahead.came = tie(terms, ahead.came)
        kept.append(keep)
        lines.append(terms[2][:, :, 0])
        sums.append(Reduction(place, terms[0], terms[1]))
    lines = sum_all(place, jnp.stack(lines), micro=False)
    qs = [factor_of(place, small, lines[i, 0]) for i in span]
    dots = [lines[i, 1] for i in span]

    def gradient_of(i, came, others):
        share, others = arrive(i, came, last, e0, others, 0)
        gathering = Gathering(place, [share])
        gathering.launch()
        return gathering, others

    def outputs_of():
        outs = []
        for k in span:
            branch = sums[k].result() * own_share(place, qs[k].reshape(-1, 1))
            outs.append(out_share(place, kept[k][0], branch))
        return Homing(place, jnp.concatenate(outs, axis=0))

    came, homing, ready = None, None, None
    es = list(e0)
    for turn in range(sections - 1):
        carry = forward_start(place, small)
        shares_in, came = came, {}
        es, terms = list(e0), None
        for i in reversed(span):
            dn, pull = dn0[i], dots[i]
            if shares_in is not None:
                ready, terms = gradient_of(i, shares_in, terms)
                es[i] = ready.result()[0]
                dn, pull, _, _ = normal_piece(es[i], qs[i], kept[i], weights, small)
                pull = sum_all(place, pull, micro=False)
            elif homing is None:
                for item in sums:
                    dn = item.launch(dn)
            gates = gates_piece(place, dn, qs[i], pull, kept[i], small)
            if i + 1 < PIECES:
                gates = leave(i + 1, share, came, -1, gates)
            terms, carry, _, _ = backward_piece(place, False, gates, kept[i], weights, small, carry)
            if i + 1 < PIECES:
                terms, came[i + 1] = tie(terms, came[i + 1])
            if homing is None:
                for item in sums:
                    terms = item.land(terms)
            red = Reduction(place, terms[0], terms[1])
            red.launch()
            if homing is None:
                homing = outputs_of()
            if not i and turn == sections - 2 and PIECES > 1:
                ready, _ = gradient_of(PIECES - 1, came, None)
                ready.came = red.land(ready.came)
            share, _ = input_grad(place, es[i], kept[i][0], norm_gain[0], red)
        leave(0, share, came, -1, None)
    if homing is None:
        for item in sums:
            item.launch()
        homing = outputs_of()

    carry = forward_start(place, small)
    red, matrix, small_sums, terms = [], [None] * 3, None, None

    def add(old, a, b):
        now = columns_dot(a, b)
        return now if old is None else old + now

    for i in reversed(span):
        if came is not None:
            if red or ready is None:
                ready, terms = gradient_of(i, came, terms)
            if red:
                red[-1].prepare()
                homing.collect()
                ready.came, red[-1].going, homing.rows = tie(ready.came, red[-1].going, homing.rows)
            es[i] = ready.result()[0]
        dn, pull, n, gain_grad = normal_piece(es[i], qs[i], kept[i], weights, small)
        pull = sum_all(place, pull, micro=False)
        matrix[0] = add(matrix[0], es[i], n)
        pull, matrix[0] = tie(pull, matrix[0])
        if red:
            pull = homing.turn(red[-1].launch(pull))
        else:
            pull, homing.sends = tie(pull, homing.sends)
            homing.launch()
        gates = gates_piece(place, dn, qs[i], pull, kept[i], small)
        if not i:
            scatter = Scatter(place, [matrix[0].astype(bf16), add(matrix[1], kept[i][2], gates[1]).astype(bf16)])
            scatter.prepare()
            gates, scatter.out = tie(gates, scatter.out)
            scatter.launch()
        terms, carry, dvbd, now = backward_piece(place, True, gates, kept[i], weights, small, carry)
        if red:
            terms = red[-1].land(terms)
        else:
            homing.came, terms, gates, dvbd, now = tie(homing.came, terms, gates, dvbd, now)
            if PIECES == 1:
                homing.turn()
        now = [now, gain_grad]
        if i:
            red.append(Reduction(place, terms[0], terms[1]))
            for k, b in ((1, gates[1]), (2, dvbd)):
                matrix[k] = add(matrix[k], kept[i][2], b)
        else:
            ahead = Reduction(place, terms[0], terms[1])
            ahead.own, dvbd, now, scatter.next, homing.swapped = tie(
                ahead.own, dvbd, now, scatter.next, homing.swapped
            )
            scatter.land()
            red.append(ahead)
        small_sums = now if small_sums is None else [a + b for a, b in zip(small_sums, now)]
    outputs = homing.result().reshape(block_input.shape)
    scatter.prepare()
    scatter.launch()
    red[-1].prepare()
    red[-1].going, dvbd = tie(red[-1].going, dvbd)
    red[-1].launch()
    mixes = Scatter(place, [add(matrix[2], kept[0][2], dvbd).astype(bf16)])
    mixes.prepare()
    mixes.launch()
    grads, norm_grad = [], jnp.zeros((8, norm_gain.shape[1]), f32)
    for i, item in zip(reversed(span), red[:-1]):
        block, now = input_grad(place, es[i], kept[i][0], norm_gain[0], item)
        grads.insert(0, block)
        norm_grad = norm_grad + now
    scatter.next = red[-1].land(scatter.next)
    scatter.land()
    while scatter.left[0]:
        scatter.prepare()
        scatter.launch()
        scatter.land()
    block, now = input_grad(place, es[0], kept[0][0], norm_gain[0], red[-1])
    norm_grad = norm_grad + now
    homing = Homing(place, jnp.concatenate([block] + grads, axis=0))
    homing.launch()
    scatter = scatter.trade()
    gate_grad = columns_beside(place, scatter, width, width)
    out_grad = order([block[:, :width].astype(f32).T for block in scatter], part, 0).reshape(-1, w_out.shape[2])
    homing.came, mixes.next, gate_grad, out_grad = tie(homing.came, mixes.next, gate_grad, out_grad)
    mixes.land()
    mixes.prepare()
    homing.collect()
    mixes.out, homing.rows = tie(mixes.out, homing.rows)
    homing.turn()
    mixes.launch()
    packed, gain_grad = small_sums
    norm_grad = jnp.sum(norm_grad, axis=0)
    row = lax.broadcasted_iota(jnp.int32, (8, mixed), 0)
    packed = jnp.where(row == GAIN_ROW, jnp.pad(gain_grad, ((0, 0), (0, MAPS))), packed)
    lanes = max(mixed, norm_grad.size)
    packed = jnp.concatenate(
        [jnp.pad(packed, ((0, 0), (0, lanes - mixed))), jnp.pad(norm_grad[None], ((0, 7), (0, lanes - norm_grad.size)))],
        axis=0,
    )
    packed, mixes.next = tie(packed, mixes.next)
    mixes.land()
    while mixes.left[0]:
        mixes.prepare()
        mixes.launch()
        mixes.land()
    packed = sum_all(place, packed, part=False, tensor=False)
    by_part = [packed] + [place.swap_part(packed, d) for d in range(1, parts)]
    input_grads = homing.result().reshape(block_input.shape).astype(f32)
    mixes = mixes.trade()
    value_grad = columns_beside(place, mixes, 0, width)
    step_grad = beside([block[:, mixed : mixed + heads_here].astype(f32) for block in mixes], part)
    maps_grad = sum(block[:, width:mixed].astype(f32) for block in mixes).astype(bf16)
    maps_sum = maps_grad.astype(f32)
    for mask in bits_of(place.tensors):
        maps_sum = maps_sum + place.swap_tensor(maps_sum, mask)

    both = by_part[0]
    for distance in range(1, parts):
        both = both + by_part[distance]
    both = sum_all(place, both, micro=False, part=False)
    wide, bias_grad, gain_grad, maps_small, maps_bias, norm_sum, by_head = unpack(
        place, both, by_part, width, heads_here, norm_grad.size
    )
    total_heads = parts * heads_here
    return (
        outputs[None],
        input_grads[None],
        norm_sum,
        gate_grad[None],
        value_grad[None],
        maps_sum[None],
        step_grad[None],
        wide[None],
        maps_small[None],
        bias_grad,
        maps_bias,
        by_head[0:1, :total_heads],
        by_head[1:2, :total_heads],
        by_head[2:3, :total_heads],
        gain_grad,
        out_grad[None],
    )


def solution(mesh):
    placed = (
        P(None, "context", None),
        P("section", None),
        P("section", "context", "tensor"),
        P("section", "context", "tensor"),
        P("section", "context", None),
        P("section", "context", "tensor"),
        P("section", None, "tensor"),
        P("section", None, None),
        P("section", "tensor"),
        P("section", None),
        P("section", "tensor"),
        P("section", "tensor"),
        P("section", "tensor"),
        P("section", "tensor"),
        P("section", "tensor", "context"),
        P(None, "context", None),
    )
    return jax.shard_map(
        body,
        mesh=mesh,
        in_specs=placed,
        out_specs=(
            P("section", None, "context", None),
            P("section", None, "context", None),
            P("section", None),
            P("section", "context", "tensor"),
            P("section", "context", "tensor"),
            P("section", "context", None),
            P("section", "context", "tensor"),
            P("section", None, "tensor"),
            P("section", None, None),
            P("section", "tensor"),
            P("section", None),
            P("section", "tensor"),
            P("section", "tensor"),
            P("section", "tensor"),
            P("section", "tensor"),
            P("section", "tensor", "context"),
        ),
        check_vma=False,
    )
```

```python
import functools

import jax
import jax.numpy as jnp
from jax import lax
from jax.experimental import pallas as pl
from jax.experimental.pallas import tpu as pltpu
from jax.sharding import PartitionSpec as P

HEAD_DIM = 64
STATE = 128
CONV = 4
MAPS = 2 * STATE
CHUNK = 128
LANES = 128
PIECES = 2

epsilon = 1e-05
bf16 = jnp.bfloat16
f32 = jnp.float32


def low_dot(a, b, contract):
    return lax.dot_general(
        a.astype(bf16), b.astype(bf16), ((contract[0], contract[1]), ((), ())), preferred_element_type=f32
    )


def mm(a, b):
    return low_dot(a, b, ((1,), (0,)))


def mm_nt(a, b):
    return low_dot(a, b, ((1,), (1,)))


def mm_tn(a, b):
    return low_dot(a, b, ((0,), (0,)))


def softplus(v):
    return jnp.maximum(v, 0.0) + jnp.log(1.0 + jnp.exp(-jnp.abs(v)))


def groups_of(width):
    return [
        (at, min(LANES, width - at), at // HEAD_DIM, min(LANES, width - at) // HEAD_DIM)
        for at in range(0, width, LANES)
    ]


def head_rows(width):
    return -(-(width // HEAD_DIM) // 16) * 16


def column(cols, head):
    return jnp.broadcast_to(cols[:, head : head + 1], (cols.shape[0], LANES))


def choose(first, second, lanes):
    if second is None:
        return first[:, :lanes]
    lane = lax.broadcasted_iota(jnp.int32, (first.shape[0], lanes), 1)
    return jnp.where(lane < HEAD_DIM, first, second)


def only(value, which, count):
    if count == 1:
        return value
    lane = lax.broadcasted_iota(jnp.int32, value.shape, 1)
    return jnp.where((lane < HEAD_DIM) == (which == 0), value, jnp.zeros_like(value))


def pieces_of(value, count):
    terms = []
    for _ in range(count):
        term = value.astype(bf16)
        terms.append(term)
        value = value - term.astype(f32)
    return terms


def mm3(a, b):
    (a_hi, a_lo), (b_hi, b_lo) = pieces_of(a, 2), pieces_of(b, 2)
    return mm(jnp.concatenate([a_hi, a_lo, a_hi], axis=1), jnp.concatenate([b_hi, b_hi, b_lo], axis=0))


def mm3_nt(a, b):
    (a_hi, a_lo), (b_hi, b_lo) = pieces_of(a, 2), pieces_of(b, 2)
    return mm_nt(jnp.concatenate([a_hi, a_lo, a_hi], axis=1), jnp.concatenate([b_hi, b_hi, b_lo], axis=1))


def sum_dot(value, zero_one, count):
    return sum(mm(term, zero_one) for term in pieces_of(value, count))


def iotas():
    row = lax.broadcasted_iota(jnp.int32, (CHUNK, CHUNK), 0)
    col = lax.broadcasted_iota(jnp.int32, (CHUNK, CHUNK), 1)
    return row, col


def conv_rows(pad, taps_ref, at, lanes):
    here = slice(at, at + lanes)
    pre = taps_ref[CONV : CONV + 1, here] + taps_ref[CONV - 1 : CONV, here] * pad[8 : 8 + CHUNK, here]
    for k in range(CONV - 1):
        first = 8 - (CONV - 1) + k
        pre = pre + taps_ref[k : k + 1, here] * pad[first : first + CHUNK, here]
    return pre


def decay_terms(dt_pre, heads_ref, rows, row, col):
    wide = dt_pre.T[:rows] + heads_ref[0:rows, :]
    dt = softplus(wide)
    log_decay = sum_dot(-heads_ref[rows : 2 * rows, :] * dt, (row <= col).astype(bf16), 3)
    cols = jnp.concatenate([log_decay, dt, jnp.zeros((CHUNK - 2 * rows, CHUNK), f32)], axis=0).T
    return wide, dt, log_decay, cols


def as_row(value):
    return jnp.sum(value.T, axis=0, keepdims=True)


def filled(value):
    rows, lanes = value.shape
    if lanes == LANES:
        return value
    return jnp.concatenate([value, jnp.zeros((rows, LANES - lanes), f32)], axis=1)


def as_column(row):
    return jnp.broadcast_to(row, (CHUNK, LANES)).T


def deal(part, parts, first, count, total, own_ref, send_ref, sems):
    def own_copy(c):
        rows = total.at[pl.ds(pl.multiple_of(c * CHUNK, CHUNK), CHUNK), :]
        return pltpu.make_async_copy(rows, own_ref.at[(first + c) // parts], sems.at[c])

    def one(c, _):
        index = first + c
        distance = (index % parts) ^ part

        @pl.when(distance == 0)
        def _():
            own_copy(c).start()

        @pl.when(distance != 0)
        def _():
            rows = total[pl.ds(pl.multiple_of(c * CHUNK, CHUNK), CHUNK), :]
            send_ref[jnp.maximum(distance - 1, 0), index // parts] = rows.astype(send_ref.dtype)

        return 0

    def end(c, _):
        @pl.when(((first + c) % parts) ^ part == 0)
        def _():
            own_copy(c).wait()

        return 0

    lax.fori_loop(0, count, one, 0)
    lax.fori_loop(0, count, end, 0)


def forward_kernel(keep, width, parts, per_step, part_ref, h_ref, w1_ref, wg_ref, norm_ref, taps_ref, heads_ref, inner_ref, s0_ref, tail0_ref, *rest):
    if keep:
        wo_ref, dn_ref, own_ref, send_ref, sums_ref, st_ref, tail_ref, xn_ref, vbd_ref, z_ref, y_ref, sin_ref, pad, gg, total, sems = rest
    else:
        g_ref, sums_ref, st_ref, tail_ref, xn_ref, vbd_ref, z_ref, pad = rest
    mixed = width + MAPS
    rows = head_rows(width)
    step = pl.program_id(0)

    @pl.when(step == 0)
    def _():
        st_ref[...] = s0_ref[...]
        tail_ref[...] = tail0_ref[...]

    def norm(c, _):
        here = pl.ds(pl.multiple_of(c * 64, 64), 64)
        hf = h_ref[here, :].astype(f32)
        scale = lax.rsqrt(jnp.mean(hf * hf, axis=1, keepdims=True) + epsilon)
        xn_ref[here, :] = (hf * scale * norm_ref[...]).astype(bf16)
        return 0

    lax.fori_loop(0, per_step * 2, norm, 0)
    vbd_ref[...] = jnp.dot(xn_ref[...], w1_ref[...], preferred_element_type=f32)
    z_ref[...] = jnp.dot(xn_ref[...], wg_ref[...], preferred_element_type=f32)
    row, col = iotas()

    def chunk(c, _):
        here = pl.ds(pl.multiple_of(c * CHUNK, CHUNK), CHUNK)
        pad[0:8, :] = tail_ref[...]
        pad[8 : 8 + CHUNK, :] = vbd_ref[here, :mixed]
        tail_ref[...] = pad[CHUNK : CHUNK + 8, :]
        pre = conv_rows(pad, taps_ref, width, MAPS)
        maps = pre * jax.nn.sigmoid(pre)
        b, c_map = maps[:, :STATE], maps[:, STATE:]
        b_rows = b.T
        _, _, log_row, cols = decay_terms(vbd_ref[here, mixed:], heads_ref, rows, row, col)
        contact = jnp.where(row >= col, mm3(c_map, b_rows), 0.0)
        if keep:
            sin_ref[c] = st_ref[...]
        carried = mm3(c_map, st_ref[...])
        squares = jnp.zeros((CHUNK, LANES), f32)
        pulls = jnp.zeros((CHUNK, LANES), f32)
        for at, lanes, head, count in groups_of(width):
            span = slice(at, at + lanes)
            pre = conv_rows(pad, taps_ref, at, lanes)
            own = pre * jax.nn.sigmoid(pre)
            logs = [column(cols, head + j) for j in range(count)]
            steps = [column(cols, rows + head + j) for j in range(count)]
            log_x = choose(logs[0], logs[-1] if count == 2 else None, lanes)
            step_x = choose(steps[0], steps[-1] if count == 2 else None, lanes)
            last_x = log_x[CHUNK - 1 : CHUNK, :]
            xd = own * step_x
            mixing = [
                jnp.exp(jnp.minimum(logs[j] - log_row[head + j : head + j + 1, :], 0.0)) * contact
                for j in range(count)
            ]
            inside = mm3(
                jnp.concatenate(mixing, axis=1),
                jnp.concatenate([only(xd, j, count) for j in range(count)], axis=0),
            )
            y = inside + jnp.exp(log_x) * carried[:, span] + inner_ref[0:1, span] * own
            st_ref[:, span] = jnp.exp(last_x) * st_ref[:, span] + mm3(b_rows, jnp.exp(last_x - log_x) * xd)
            z = z_ref[here, span]
            g = y * (z * jax.nn.sigmoid(z))
            if keep:
                gg[here, span] = (g * inner_ref[1:2, span]).astype(bf16)
                y_ref[here, span] = y
            else:
                g_ref[here, span] = g
            squares = squares + filled(g * g)
            if keep:
                pulls = pulls + filled(dn_ref[here, span] * inner_ref[1:2, span] * g)
        sums_ref[0, c] = as_row(squares)
        if keep:
            sums_ref[1, c] = as_row(pulls)
        return 0

    lax.fori_loop(0, per_step, chunk, 0)
    if keep:
        total[...] = lax.dot_general(
            gg[...], wo_ref[...], (((1,), (1,)), ((), ())), preferred_element_type=f32
        )
        deal(part_ref[0], parts, step * per_step, per_step, total, own_ref, send_ref, sems)


def out_kernel(parts, per_step, part_ref, g_ref, q_ref, inner_ref, wo_ref, own_ref, send_ref, n, total, sems):
    def chunk(c, _):
        here = pl.ds(pl.multiple_of(c * CHUNK, CHUNK), CHUNK)
        q = as_column(q_ref[c])
        for at, lanes, _, _ in groups_of(n.shape[1]):
            span = slice(at, at + lanes)
            n[here, span] = (g_ref[here, span] * q[:, :lanes] * inner_ref[1:2, span]).astype(bf16)
        return 0

    lax.fori_loop(0, per_step, chunk, 0)
    total[...] = lax.dot_general(n[...], wo_ref[...], (((1,), (1,)), ((), ())), preferred_element_type=f32)
    deal(part_ref[0], parts, pl.program_id(0) * per_step, per_step, total, own_ref, send_ref, sems)


def out_call(place, g, q, weights, inner):
    wo = weights[2]
    tokens, width = g.shape
    depth = wo.shape[0]
    chunks = tokens // CHUNK
    per_step = min(STEP, chunks)
    steps = chunks // per_step
    count = per_step * CHUNK
    blocks = chunks // place.parts
    shapes = [(blocks, CHUNK, depth), (place.parts - 1, blocks, CHUNK, depth)]
    return pl.pallas_call(
        functools.partial(out_kernel, place.parts, per_step),
        grid_spec=pltpu.PrefetchScalarGridSpec(
            num_scalar_prefetch=1,
            grid=(steps,),
            in_specs=[
                block(steps, (count, width), lambda i, _: (i, 0)),
                block(steps, (per_step, 1, LANES), lambda i, _: (i, 0, 0)),
                once(inner.shape),
                once(wo.shape),
            ],
            out_specs=[pl.BlockSpec(memory_space=pl.ANY), once(shapes[1])],
            scratch_shapes=[
                pltpu.VMEM((count, width), bf16),
                pltpu.VMEM((count, depth), f32),
                pltpu.SemaphoreType.DMA((per_step,)),
            ],
        ),
        out_shape=[jax.ShapeDtypeStruct(shape, f32) for shape in shapes],
        compiler_params=kernel_params(steps, 8),
        cost_estimate=pl.CostEstimate(
            flops=tokens * width * 6000, bytes_accessed=tokens * depth * 8, transcendentals=0
        ),
        name="out_forward",
    )(place.part.reshape(1), g, q[:, None], inner, wo)


STEP = 4
GAIN_ROW = CONV + 1
HEAD_ROW = CONV + 2


def kernel_params(steps, megabytes):
    return pltpu.CompilerParams(vmem_limit_bytes=(megabytes if steps == 1 else 40) * 1024 * 1024)


def once(shape):
    return pl.BlockSpec(memory_space=pltpu.VMEM)


def block(steps, shape, index_map):
    return once(shape) if steps == 1 else pl.BlockSpec(shape, index_map)


def forward_call(place, h, weights, small, s0, tail0, dn=None):
    w1, wg = weights[:2]
    norm_gain, taps, heads, inner = small
    keep = dn is not None
    tokens, depth = h.shape
    width = inner.shape[1]
    mixed = width + MAPS
    chunks = tokens // CHUNK
    per_step = min(STEP, chunks)
    steps = chunks // per_step
    count = per_step * CHUNK
    blocks = chunks // place.parts
    rows = lambda lanes: block(steps, (count, lanes), lambda i, _: (i, 0))
    if keep:
        shapes = [((blocks, CHUNK, depth), f32), ((place.parts - 1, blocks, CHUNK, depth), bf16)]
        out_shape = [jax.ShapeDtypeStruct(*item) for item in shapes]
        out_specs = [pl.BlockSpec(memory_space=pl.ANY), once(shapes[1][0])]
    else:
        out_shape = [jax.ShapeDtypeStruct((tokens, width), f32)]
        out_specs = [rows(width)]
    out_shape += [
        jax.ShapeDtypeStruct((2, chunks, 1, LANES), f32),
        jax.ShapeDtypeStruct((STATE, width), f32),
        jax.ShapeDtypeStruct((8, mixed), f32),
    ]
    out_specs += [
        block(steps, (2, per_step, 1, LANES), lambda i, _: (0, i, 0, 0)),
        once((STATE, width)),
        once((8, mixed)),
    ]
    in_specs = [
        rows(depth),
        once(w1.shape),
        once(wg.shape),
        once((1, depth)),
        once(taps.shape),
        once(heads.shape),
        once(inner.shape),
        once(s0.shape),
        once(tail0.shape),
    ]
    args = [h, w1, wg, norm_gain[None], taps, heads, inner, s0, tail0]
    held = [((tokens, depth), bf16), ((tokens, w1.shape[1]), f32), ((tokens, width), f32)]
    scratch = []
    if keep:
        in_specs += [once(weights[2].shape), rows(width)]
        args += [weights[2], dn]
        held.append(((tokens, width), f32))
        out_shape += [jax.ShapeDtypeStruct(*item) for item in held]
        out_specs += [rows(shape[1]) for shape, _ in held]
        out_shape.append(jax.ShapeDtypeStruct((chunks, STATE, width), f32))
        out_specs.append(block(steps, (per_step, STATE, width), lambda i, _: (i, 0, 0)))
    else:
        scratch = [pltpu.VMEM((count, shape[1]), kind) for shape, kind in held]
    scratch.append(pltpu.VMEM((CHUNK + 8, mixed), f32))
    if keep:
        scratch += [
            pltpu.VMEM((count, width), bf16),
            pltpu.VMEM((count, depth), f32),
            pltpu.SemaphoreType.DMA((per_step,)),
        ]
    return pl.pallas_call(
        functools.partial(forward_kernel, keep, width, place.parts, per_step),
        grid_spec=pltpu.PrefetchScalarGridSpec(
            num_scalar_prefetch=1, grid=(steps,), in_specs=in_specs, out_specs=out_specs, scratch_shapes=scratch
        ),
        out_shape=out_shape,
        compiler_params=kernel_params(steps, 10 if keep else 11),
        cost_estimate=pl.CostEstimate(
            flops=tokens * width * 40000, bytes_accessed=tokens * depth * 16, transcendentals=0
        ),
        name="section_forward",
    )(place.part.reshape(1), *args)


def normal_kernel(full, width, per_step, e_ref, wo_ref, z_ref, y_ref, q_ref, inner_ref, dn_ref, pull_ref, n_ref, gain_ref, gains):
    dn_ref[...] = jnp.dot(e_ref[...], wo_ref[...], preferred_element_type=f32)

    @pl.when(pl.program_id(0) == 0)
    def _():
        gains[...] = jnp.zeros_like(gains)

    def chunk(c, _):
        here = pl.ds(pl.multiple_of(c * CHUNK, CHUNK), CHUNK)
        q = as_column(q_ref[c])
        pulls = jnp.zeros((CHUNK, LANES), f32)
        for at, lanes, _, _ in groups_of(width):
            span = slice(at, at + lanes)
            z, dn_x, gain = z_ref[here, span], dn_ref[here, span], inner_ref[1:2, span]
            g = y_ref[here, span] * (z * jax.nn.sigmoid(z))
            gq = g * q[:, :lanes]
            pulls = pulls + filled(dn_x * gain * g)
            n_ref[here, span] = (gq * gain).astype(bf16)
            gains[:, span] += fold(dn_x * gq)
        pull_ref[c] = as_row(pulls)
        return 0

    lax.fori_loop(0, per_step, chunk, 0)
    gain_ref[...] = jnp.broadcast_to(jnp.sum(gains[...], axis=0, keepdims=True), gains.shape)


def gate_kernel(width, per_step, total, dn_ref, z_ref, y_ref, q_ref, pull_ref, inner_ref, dy_ref, dz_ref):
    def chunk(c, _):
        here = pl.ds(pl.multiple_of(c * CHUNK, CHUNK), CHUNK)
        q = as_column(q_ref[c])
        pull = as_column(pull_ref[c]) * (q * q * q) * (1.0 / total)
        for at, lanes, _, _ in groups_of(width):
            span = slice(at, at + lanes)
            z, y = z_ref[here, span], y_ref[here, span]
            sig = jax.nn.sigmoid(z)
            silu = z * sig
            dg = q[:, :lanes] * (dn_ref[here, span] * inner_ref[1:2, span]) - y * silu * pull[:, :lanes]
            dy_ref[here, span] = dg * silu
            dz_ref[here, span] = (dg * y * (sig + silu * (1.0 - sig))).astype(bf16)
        return 0

    lax.fori_loop(0, per_step, chunk, 0)


def normal_call(e, weights, z, y, q, inner):
    wo = weights[2]
    tokens, depth = e.shape
    width = inner.shape[1]
    chunks = tokens // CHUNK
    per_step = min(STEP, chunks)
    steps = chunks // per_step
    rows = lambda lanes: block(steps, (per_step * CHUNK, lanes), lambda i: (i, 0))
    lines = block(steps, (per_step, 1, LANES), lambda i: (i, 0, 0))
    return pl.pallas_call(
        functools.partial(normal_kernel, True, width, per_step),
        grid=(steps,),
        in_specs=[rows(depth), once(wo.shape), rows(width), rows(width), lines, once(inner.shape)],
        out_specs=[rows(width), lines, rows(width), once((8, width))],
        out_shape=[
            jax.ShapeDtypeStruct((tokens, width), f32),
            jax.ShapeDtypeStruct((chunks, 1, LANES), f32),
            jax.ShapeDtypeStruct((tokens, width), bf16),
            jax.ShapeDtypeStruct((8, width), f32),
        ],
        scratch_shapes=[pltpu.VMEM((8, width), f32)],
        compiler_params=kernel_params(steps, 4),
        cost_estimate=pl.CostEstimate(
            flops=tokens * width * 9000, bytes_accessed=tokens * depth * 16, transcendentals=0
        ),
        name="norm_backward",
    )(e, wo, z, y, q, inner)


def gate_call(place, dn, z, y, q, pull, inner):
    tokens, width = dn.shape
    chunks = tokens // CHUNK
    per_step = min(STEP, chunks)
    steps = chunks // per_step
    rows = lambda lanes: block(steps, (per_step * CHUNK, lanes), lambda i: (i, 0))
    lines = block(steps, (per_step, 1, LANES), lambda i: (i, 0, 0))
    return pl.pallas_call(
        functools.partial(gate_kernel, width, per_step, place.tensors * place.parts * width),
        grid=(steps,),
        in_specs=[rows(width), rows(width), rows(width), lines, lines, once(inner.shape)],
        out_specs=[rows(width), rows(width)],
        out_shape=[jax.ShapeDtypeStruct((tokens, width), f32), jax.ShapeDtypeStruct((tokens, width), bf16)],
        compiler_params=kernel_params(steps, 4),
        cost_estimate=pl.CostEstimate(
            flops=tokens * width * 6000, bytes_accessed=tokens * width * 16, transcendentals=0
        ),
        name="gate_backward",
    )(dn, z, y, q, pull, inner)


def fold(value):
    return jnp.sum(value.reshape(CHUNK // 8, 8, value.shape[1]), axis=0)


def backward_kernel(
    exact,
    width,
    parts,
    per_step,
    steps,
    part_ref,
    dy_ref,
    dz_ref,
    vbd_ref,
    before_ref,
    sin_ref,
    w1_ref,
    wg_ref,
    taps_ref,
    heads_ref,
    inner_ref,
    g0_ref,
    du0_ref,
    own_ref,
    send_ref,
    dvbd_ref,
    gt_ref,
    dut_ref,
    tapg_ref,
    pad,
    dpad,
    sums,
    y_in,
    dxd_out,
    dy_in_all,
    xd_out_all,
    total,
    taps_sum,
    headg_ref,
    skipg_ref,
    back_all,
    sems,
):
    mixed = width + MAPS
    rows = head_rows(width)
    step = steps - 1 - pl.program_id(0)

    @pl.when(pl.program_id(0) == 0)
    def _():
        gt_ref[...] = g0_ref[...]
        dut_ref[...] = du0_ref[...]
        taps_sum[...] = jnp.zeros_like(taps_sum)
        headg_ref[...] = jnp.zeros_like(headg_ref)
        skipg_ref[...] = jnp.zeros_like(skipg_ref)

    row, col = iotas()
    causal = col >= row
    strict = col > row
    onward = (row >= col).astype(bf16)
    head_of = lax.broadcasted_iota(jnp.int32, (rows, width), 1) // HEAD_DIM
    ones = (head_of == lax.broadcasted_iota(jnp.int32, (rows, width), 0)).astype(bf16)

    def conv_back(here, at, lanes, du):
        span = slice(at, at + lanes)
        dpad[0:CHUNK, span] = du
        m = pad[8 : 8 + CHUNK, span]
        taps_sum[CONV * 8 : CONV * 8 + 8, span] += fold(du)
        taps_sum[CONV * 8 - 8 : CONV * 8, span] += fold(m * du)
        dm = taps_ref[CONV - 1 : CONV, span] * du
        for k in range(CONV - 1):
            first = CONV - 1 - k
            moved = dpad[first : first + CHUNK, span]
            dm = dm + taps_ref[k : k + 1, span] * moved
            taps_sum[k * 8 : k * 8 + 8, span] += fold(m * moved)
        dvbd_ref[here, span] = dm.astype(bf16)

    def chunk(reverse, _):
        c = per_step - 1 - reverse
        here = pl.ds(pl.multiple_of(c * CHUNK, CHUNK), CHUNK)
        dpad[CHUNK : CHUNK + 8, :] = dut_ref[...]
        pad[8 : 8 + CHUNK, :] = vbd_ref[here, :mixed]

        @pl.when(c == 0)
        def _():
            pad[0:8, :] = before_ref[0]

        @pl.when(c != 0)
        def _():
            pad[0:8, :] = vbd_ref[pl.ds(pl.multiple_of(jnp.maximum(c * CHUNK - 8, 0), 8), 8), :mixed]

        pre = conv_rows(pad, taps_ref, width, MAPS)
        sig = jax.nn.sigmoid(pre)
        maps = pre * sig
        maps_slope = sig + maps * (1.0 - sig)
        b_maps, c_maps = maps[:, :STATE], maps[:, STATE:]
        b_low, c_low = b_maps.astype(bf16), c_maps.astype(bf16)
        wide, dt, log_row, cols = decay_terms(vbd_ref[here, mixed:], heads_ref, rows, row, col)
        contact = jnp.where(causal, mm_nt(b_low, c_low), 0.0)
        back_low = gt_ref[...].astype(bf16)
        if exact:
            back_all[...] = gt_ref[...]
        c_rows = c_low.T
        y_in[...] = mm(c_low, sin_ref[c])
        dxd_out[...] = mm(b_low, back_low)
        dcontact = jnp.zeros((CHUNK, CHUNK), f32)
        log_rows, through = [], []
        for at, lanes, head, count in groups_of(width):
            span = slice(at, at + lanes)
            pre = conv_rows(pad, taps_ref, at, lanes)
            sig = jax.nn.sigmoid(pre)
            own = pre * sig
            slope = sig + own * (1.0 - sig)
            logs = [column(cols, head + j) for j in range(count)]
            steps_of = [column(cols, rows + head + j) for j in range(count)]
            log_x = choose(logs[0], logs[-1] if count == 2 else None, lanes)
            step_x = choose(steps_of[0], steps_of[-1] if count == 2 else None, lanes)
            last_x = log_x[CHUNK - 1 : CHUNK, :]
            dy = dy_ref[here, span]
            xd = own * step_x
            xd_low = xd.astype(bf16)
            dy_low = dy.astype(bf16)
            to_end = jnp.exp(last_x - log_x)
            dy_in = jnp.exp(log_x) * dy
            dy_in_low = dy_in.astype(bf16)
            if exact:
                dy_in_all[:, span] = dy_in
                xd_out_all[:, span] = to_end * xd
                dmix = mm3_nt(jnp.concatenate([only(xd, j, count) for j in range(count)], axis=0), dy)
            else:
                dy_in_all[:, span] = dy_in_low
                xd_out_all[:, span] = (to_end * xd).astype(bf16)
                dmix = mm_nt(jnp.concatenate([only(xd_low, j, count) for j in range(count)], axis=0), dy_low)
            mixing, products = [], []
            for j in range(count):
                decay = jnp.exp(jnp.minimum(log_row[head + j : head + j + 1, :] - logs[j], 0.0))
                one = decay * contact
                d_one = dmix[j * CHUNK : (j + 1) * CHUNK]
                dcontact = dcontact + decay * d_one
                mixing.append(one.astype(bf16))
                products.append((one * d_one).astype(bf16))
            dxd_in = mm(
                jnp.concatenate(mixing, axis=1),
                jnp.concatenate([only(dy_low, j, count) for j in range(count)], axis=0),
            )
            later = mm(jnp.concatenate(products, axis=0), onward)
            for j in range(count):
                log_rows.append(
                    jnp.sum(jnp.where(strict, later[j * CHUNK : (j + 1) * CHUNK], 0.0), axis=0, keepdims=True)
                )
            from_end = to_end * dxd_out[:, span]
            dxd = dxd_in + from_end
            sums[0:CHUNK, span] = (dy_in * y_in[:, span]).astype(bf16)
            sums[CHUNK : 2 * CHUNK, span] = (xd * from_end).astype(bf16)
            sums[2 * CHUNK : 3 * CHUNK, span] = (own * dxd).astype(bf16)
            carried = jnp.exp(last_x)
            back = gt_ref[:, span]
            through.append(
                jnp.sum(carried * sin_ref[c, :, span].astype(f32) * back, axis=0, keepdims=True)
            )
            skipg_ref[:, span] += fold(dy * own)
            gt_ref[:, span] = carried * back + mm(c_rows, dy_in_low)
            conv_back(here, at, lanes, (step_x * dxd + inner_ref[0:1, span] * dy) * slope)
        dcontact = jnp.where(causal, dcontact, 0.0)
        if exact:
            db = mm3_nt(xd_out_all[...], back_all[...]) + mm3(dcontact, c_maps)
            dc = mm3_nt(dy_in_all[...], sin_ref[c]) + mm3(dcontact.T, b_maps)
        else:
            db = mm_nt(xd_out_all[...], back_low) + mm(dcontact, c_low)
            dc = mm_nt(dy_in_all[...], sin_ref[c]) + mm_tn(dcontact, b_low)
        conv_back(here, width, STATE, db * maps_slope[:, :STATE])
        conv_back(here, width + STATE, STATE, dc * maps_slope[:, STATE:])
        dut_ref[...] = dpad[0:8, :]

        by_token = mm_nt(ones, sums[...])
        entering = by_token[:, :CHUNK]
        leaving = by_token[:, CHUNK : 2 * CHUNK]
        direct = by_token[:, 2 * CHUNK :]
        ends = jnp.broadcast_to(jnp.concatenate(through, axis=1), (CHUNK, width))
        ends = sum(mm_nt(ones, term) for term in pieces_of(ends, 2))
        inside = log_rows
        if rows > len(log_rows):
            inside = log_rows + [jnp.zeros((rows - len(log_rows), CHUNK), f32)]
        dlog = (
            jnp.concatenate(inside, axis=0)
            + sum_dot(entering, onward, 2)
            + sum_dot(leaving, (row < col).astype(bf16), 2)
            + ends
        )
        rate = heads_ref[rows : 2 * rows, :]
        ddt_pre = (direct - rate * dlog) * jax.nn.sigmoid(wide)
        headg_ref[0:rows, :] += ddt_pre
        headg_ref[rows : 2 * rows, :] += -rate * dt * dlog
        ddt_cols = jnp.concatenate([ddt_pre, jnp.zeros((CHUNK - rows, CHUNK), f32)], axis=0).T
        dvbd_ref[here, mixed:] = ddt_cols.astype(bf16)
        return 0

    lax.fori_loop(0, per_step, chunk, 0)
    nt = (((1,), (1,)), ((), ()))
    total[...] = lax.dot_general(dvbd_ref[...], w1_ref[...], nt, preferred_element_type=f32)
    total[...] += lax.dot_general(dz_ref[...], wg_ref[...], nt, preferred_element_type=f32)

    @pl.when(pl.program_id(0) == steps - 1)
    def _():
        tapg_ref[...] = jnp.zeros_like(tapg_ref)
        for k in range(CONV + 1):
            tapg_ref[k : k + 1, :] = jnp.sum(taps_sum[k * 8 : k * 8 + 8, :], axis=0, keepdims=True)
        skips = jnp.broadcast_to(jnp.sum(skipg_ref[...], axis=0, keepdims=True), (CHUNK, width))
        skips = sum(mm_nt(ones, term) for term in pieces_of(skips, 3))
        by_head = jnp.broadcast_to(jnp.sum(headg_ref[...], axis=1, keepdims=True), (2 * rows, LANES))
        columns = jnp.concatenate([by_head, skips, jnp.zeros((CHUNK - 3 * rows, LANES), f32)], axis=0)
        tapg_ref[HEAD_ROW : HEAD_ROW + 1, 0:LANES] = columns.T[0:1]

    deal(part_ref[0], parts, step * per_step, per_step, total, own_ref, send_ref, sems)


def backward_call(place, exact, dy, dz, vbd, before, states, weights, small, g0, du0):
    w1, wg, _ = weights
    _, taps, heads, inner = small
    tokens, width = dy.shape
    depth = w1.shape[0]
    mixed = width + MAPS
    chunks = tokens // CHUNK
    per_step = min(STEP, chunks)
    steps = chunks // per_step
    count = per_step * CHUNK
    blocks = chunks // place.parts
    rows = lambda lanes: block(steps, (count, lanes), lambda i, _: (steps - 1 - i, 0))
    deep = lambda number, height, lanes: block(
        steps, (number, height, lanes), lambda i, _: (steps - 1 - i, 0, 0)
    )
    shapes = [
        ((STATE, width), f32),
        ((8, mixed), f32),
        ((8, mixed), f32),
    ]
    results = pl.pallas_call(
        functools.partial(backward_kernel, exact, width, place.parts, per_step, steps),
        grid_spec=pltpu.PrefetchScalarGridSpec(
            num_scalar_prefetch=1,
            grid=(steps,),
            in_specs=[
                rows(width),
                rows(width),
                rows(vbd.shape[1]),
                deep(1, 8, mixed),
                deep(per_step, STATE, width),
                once(w1.shape),
                once(wg.shape),
                once(taps.shape),
                once(heads.shape),
                once(inner.shape),
                once(g0.shape),
                once(du0.shape),
            ],
            out_specs=[
                pl.BlockSpec(memory_space=pl.ANY),
                once((place.parts - 1, blocks, CHUNK, depth)),
                rows(vbd.shape[1]),
            ]
            + [once(shape) for shape, _ in shapes],
            scratch_shapes=[
                pltpu.VMEM((CHUNK + 8, mixed), f32),
                pltpu.VMEM((CHUNK + 8, mixed), f32),
                pltpu.VMEM((3 * CHUNK, width), bf16),
                pltpu.VMEM((CHUNK, width), f32),
                pltpu.VMEM((CHUNK, width), f32),
                pltpu.VMEM((CHUNK, width), f32 if exact else bf16),
                pltpu.VMEM((CHUNK, width), f32 if exact else bf16),
                pltpu.VMEM((count, depth), f32),
                pltpu.VMEM((8 * (CONV + 1), mixed), f32),
                pltpu.VMEM((2 * head_rows(width), LANES), f32),
                pltpu.VMEM((8, width), f32),
                pltpu.VMEM((STATE, width), f32),
                pltpu.SemaphoreType.DMA((per_step,)),
            ],
        ),
        out_shape=[
            jax.ShapeDtypeStruct((blocks, CHUNK, depth), f32),
            jax.ShapeDtypeStruct((place.parts - 1, blocks, CHUNK, depth), bf16),
            jax.ShapeDtypeStruct(vbd.shape, bf16),
        ]
        + [jax.ShapeDtypeStruct(*item) for item in shapes],
        compiler_params=kernel_params(steps, 12),
        cost_estimate=pl.CostEstimate(
            flops=tokens * width * 60000, bytes_accessed=tokens * depth * 16, transcendentals=0
        ),
        name="section_backward",
    )(place.part.reshape(1), dy, dz, vbd, before, states, w1, wg, taps, heads, inner, g0, du0)
    own, send, dvbd, gt, dut, sums = results
    return own, send, dvbd, gt, dut, sums


def unpack_kernel(parts, heads, rows, part_ref, both_ref, *refs):
    locals_ref, outs = refs[:parts], refs[parts:]
    wide_ref, bias_ref, gain_ref, maps_ref, maps_bias_ref, norm_ref, heads_ref = outs
    width = wide_ref.shape[1] // parts
    part = part_ref[0]
    lane = lax.broadcasted_iota(jnp.int32, (1, LANES), 1)
    by_head = [jnp.zeros((1, LANES), f32) for _ in range(3)]
    for d in range(parts):
        owner = part ^ d
        here = pl.ds(pl.multiple_of(owner * width, HEAD_DIM), width)
        ref = locals_ref[d]
        if width % LANES == 0:
            wide_ref[:, here] = ref[0:CONV, 0:width]
            bias_ref[:, here] = ref[CONV : CONV + 1, 0:width]
            gain_ref[:, here] = ref[GAIN_ROW : GAIN_ROW + 1, 0:width]
        else:
            for p in range(parts):

                @pl.when(owner == p)
                def _():
                    there = slice(p * width, (p + 1) * width)
                    wide_ref[:, there] = ref[0:CONV, 0:width]
                    bias_ref[:, there] = ref[CONV : CONV + 1, 0:width]
                    gain_ref[:, there] = ref[GAIN_ROW : GAIN_ROW + 1, 0:width]

        for k in range(3):
            values = ref[HEAD_ROW : HEAD_ROW + 1, 0:LANES]
            for p in range(parts):
                moved = pltpu.roll(values, (p * heads - k * rows) % LANES, 1)
                chosen = (owner == p) & (lane >= p * heads) & (lane < (p + 1) * heads)
                by_head[k] = jnp.where(chosen, moved, by_head[k])
    heads_ref[...] = jnp.concatenate(by_head + [jnp.zeros((5, LANES), f32)], axis=0)
    maps_ref[...] = both_ref[0:CONV, width : width + MAPS]
    maps_bias_ref[...] = both_ref[CONV : CONV + 1, width : width + MAPS]
    norm_ref[...] = both_ref[8:9, 0 : norm_ref.shape[1]]


def unpack(place, both, by_part, width, heads, depth):
    total = place.parts * width
    shapes = [(CONV, total), (1, total), (1, total), (CONV, MAPS), (1, MAPS), (1, depth), (8, LANES)]
    return pl.pallas_call(
        functools.partial(unpack_kernel, place.parts, heads, head_rows(width)),
        grid_spec=pltpu.PrefetchScalarGridSpec(
            num_scalar_prefetch=1,
            grid=(1,),
            in_specs=[once(both.shape)] * (1 + place.parts),
            out_specs=[once(shape) for shape in shapes],
        ),
        out_shape=[jax.ShapeDtypeStruct(shape, f32) for shape in shapes],
        compiler_params=pltpu.CompilerParams(vmem_limit_bytes=4 * 1024 * 1024),
        name="unpack_small",
    )(place.part.reshape(1), both, *by_part)


class Place:
    def __init__(self, micro_count):
        self.context = lax.axis_size("context")
        self.micros = micro_count
        self.parts = self.context // micro_count
        self.tensors = lax.axis_size("tensor")
        index = lax.axis_index("context")
        self.micro = index // self.parts
        self.part = index % self.parts
        self.tensor = lax.axis_index("tensor")

    def swap_part(self, block, mask):
        return lax.ppermute(block, "context", [(i, i ^ mask) for i in range(self.context)])

    def swap_micro(self, block, mask):
        return self.swap_part(block, mask * self.parts)

    def swap_tensor(self, block, mask):
        return lax.ppermute(block, "tensor", [(i, i ^ mask) for i in range(self.tensors)])

    def swap_both(self, block):
        count = self.context * self.tensors
        return lax.ppermute(block, ("context", "tensor"), [(i, i ^ self.tensors ^ 1) for i in range(count)])

    def next_section(self, block, step, flip):
        count, tensors = lax.axis_size("section"), self.tensors
        return lax.ppermute(
            block,
            ("section", "tensor"),
            [
                (i * tensors + t, (i + step) * tensors + (t ^ flip))
                for i in range(count)
                if 0 <= i + step < count
                for t in range(tensors)
            ],
        )


def pick(array, index, axis):
    return lax.dynamic_index_in_dim(array, index, axis, False)


def tie(*items):
    return lax.optimization_barrier(items)


def bits_of(count):
    masks = []
    mask = 1
    while mask < count:
        masks.append(mask)
        mask *= 2
    return masks


def order_kernel(count, axis, index_ref, *refs):
    blocks, out, sems = refs[:count], refs[count], refs[count + 1]
    copies = []
    for d, one in enumerate(blocks):
        there = (slice(None),) * axis + (index_ref[0] ^ d,)
        copies.append(pltpu.make_async_copy(one, out.at[there], sems.at[d]))
    for one in copies:
        one.start()
    for one in copies:
        one.wait()


def order(blocks, index, axis, copies=True):
    count = len(blocks)
    shape = list(blocks[0].shape)
    shape.insert(axis, count)
    if count == 1:
        return blocks[0].reshape(shape)
    if copies and axis <= blocks[0].ndim - 2 and shape[-2] % 16 == 0 and shape[-1] >= LANES:
        return pl.pallas_call(
            functools.partial(order_kernel, count, axis),
            grid_spec=pltpu.PrefetchScalarGridSpec(
                num_scalar_prefetch=1,
                grid=(1,),
                in_specs=[pl.BlockSpec(memory_space=pl.ANY)] * count,
                out_specs=pl.BlockSpec(memory_space=pltpu.VMEM),
                scratch_shapes=[pltpu.SemaphoreType.DMA((count,))],
            ),
            out_shape=jax.ShapeDtypeStruct(tuple(shape), blocks[0].dtype),
            compiler_params=pltpu.CompilerParams(vmem_limit_bytes=4 * 1024 * 1024),
            name="order_blocks",
        )(index.reshape(1).astype(jnp.int32), *blocks)
    place = lax.broadcasted_iota(jnp.int32, shape, axis) ^ index
    result = jnp.expand_dims(blocks[0], axis)
    for d in range(1, count):
        result = jnp.where(place == d, jnp.expand_dims(blocks[d], axis), result)
    return jnp.broadcast_to(result, shape)


def beside(blocks, index):
    count = len(blocks)
    if count == 2:
        return jnp.where(
            index == 0, jnp.concatenate(blocks, axis=-1), jnp.concatenate(blocks[::-1], axis=-1)
        )
    return jnp.concatenate(
        [pick(order(blocks, index, 0), i, 0) for i in range(count)], axis=-1
    )


def sum_all(place, block, micro=True, part=True, tensor=True):
    if part and tensor and place.parts == place.tensors == 2:
        block = (block + place.swap_part(block, 1)) + (place.swap_tensor(block, 1) + place.swap_both(block))
    else:
        if part:
            for mask in bits_of(place.parts):
                block = block + place.swap_part(block, mask)
        if tensor:
            for mask in bits_of(place.tensors):
                block = block + place.swap_tensor(block, mask)
    if micro and place.micros == 4:
        block = (block + place.swap_micro(block, 1)) + (place.swap_micro(block, 2) + place.swap_micro(block, 3))
    elif micro:
        for mask in bits_of(place.micros):
            block = block + place.swap_micro(block, mask)
    return block


def lay_kernel(sizes, widths, places_ref, *refs):
    pieces, outs, sems = refs[: len(sizes)], refs[len(sizes) : -1], refs[-1]
    copies, number = [], 0
    for piece, size in zip(pieces, sizes):
        for row in range(size):
            at = 0
            for k, lanes in enumerate(widths):
                copies.append(
                    pltpu.make_async_copy(
                        piece.at[row, :, pl.ds(at, lanes)], outs[k].at[places_ref[number]], sems.at[number, k]
                    )
                )
                at += lanes
            number += 1
    for one in copies:
        one.start()
    for one in copies:
        one.wait()


def lay_rows(pieces, places, widths):
    rows = pieces[0].shape[1]
    sizes = [piece.shape[0] for piece in pieces]
    count = sum(sizes)
    if any(lanes % LANES for lanes in widths):
        whole = jnp.zeros((count,) + pieces[0].shape[1:], pieces[0].dtype)
        for i, row in enumerate(row for piece in pieces for row in piece):
            whole = lax.dynamic_update_index_in_dim(whole, row, places[i], 0)
        whole = whole.reshape(count * rows, -1)
        starts = [sum(widths[:k]) for k in range(len(widths))]
        return [whole[:, at : at + lanes] for at, lanes in zip(starts, widths)]
    results = pl.pallas_call(
        functools.partial(lay_kernel, sizes, widths),
        grid_spec=pltpu.PrefetchScalarGridSpec(
            num_scalar_prefetch=1,
            grid=(1,),
            in_specs=[pl.BlockSpec(memory_space=pl.ANY)] * len(pieces),
            out_specs=[pl.BlockSpec(memory_space=pltpu.VMEM)] * len(widths),
            scratch_shapes=[pltpu.SemaphoreType.DMA((count, len(widths)))],
        ),
        out_shape=[jax.ShapeDtypeStruct((count, rows, lanes), pieces[0].dtype) for lanes in widths],
        compiler_params=pltpu.CompilerParams(vmem_limit_bytes=4 * 1024 * 1024),
        name="lay_rows",
    )(jnp.stack(places).astype(jnp.int32), *pieces)
    return [result.reshape(count * rows, -1) for result in results]


class Collect:
    def __init__(self, place, blocks):
        self.place = place
        self.found = [[block] for block in blocks]
        self.distances = [[0] for _ in blocks]
        self.masks = [bits_of(place.micros)[:: -1 if p % 2 else 1] for p in range(len(blocks))]

    def prepare(self):
        self.out = [found[0] if len(found) == 1 else jnp.concatenate(found, axis=0) for found in self.found]

    def launch(self):
        self.next = [self.place.swap_micro(block, masks[0]) for block, masks in zip(self.out, self.masks)]

    def land(self):
        for p, block in enumerate(self.next):
            mask = self.masks[p].pop(0)
            self.found[p].append(block)
            self.distances[p] += [distance ^ mask for distance in self.distances[p]]

    def finish(self):
        while self.masks[0]:
            self.prepare()
            self.launch()
            self.land()

    def result(self, widths):
        place, pieces, places = self.place, [], []
        for p, found in enumerate(self.found):
            pieces += found
            places += [(place.micro ^ distance) * place.parts + (place.part ^ p) for distance in self.distances[p]]
        return lay_rows(pieces, places, widths)


def gather_weights(place, w_gate, w_value, w_bc, w_dt, w_out):
    parts = place.parts
    width = w_gate.shape[1] // parts
    heads = w_dt.shape[1] // parts

    def cut_of(array, part):
        return lax.dynamic_slice_in_dim(array, part * width, width, 1)

    def columns_of(part):
        steps = lax.dynamic_slice_in_dim(w_dt, part * heads, heads, 1)
        steps = jnp.pad(steps, ((0, 0), (0, LANES - heads)))
        return jnp.concatenate([cut_of(w_value, part), w_bc, steps, cut_of(w_gate, part)], axis=1)[None]

    def collected(make):
        blocks = [make(place.part ^ p) for p in range(parts)]
        return Collect(place, blocks[:1] + [place.swap_part(block, p + 1) for p, block in enumerate(blocks[1:])])

    first = collected(columns_of)
    second = collected(lambda part: cut_of(w_out.T, part)[None])
    return first, second


def whole_tokens(place, rows):
    return [pick(rows, place.micro, 0)] + [
        place.swap_micro(pick(rows, place.micro ^ d, 0), d) for d in range(1, place.micros)
    ]


def lay_tokens(place, blocks):
    held = order(blocks, place.micro, 0, False)
    whole = order([held] + [place.swap_part(held, d) for d in range(1, place.parts)], place.part, 1, False)
    size = place.micros // PIECES
    return [whole[i * size : (i + 1) * size].reshape(-1, held.shape[-1]) for i in range(PIECES)]


class Spread:
    def __init__(self, place, rows):
        self.place, self.rows = place, rows
        micros, count, width = rows.shape
        view = rows.reshape(micros, place.tensors, count // place.tensors, width)
        self.shares = jnp.stack(
            [place.swap_micro(pick(pick(view, place.micro ^ d, 0), place.tensor, 0), d) for d in range(1, micros)]
        )
        self.came = [place.swap_tensor(self.shares, d) for d in range(1, place.tensors)]

    def result(self):
        place = self.place
        both = [self.shares] + self.came
        blocks = [pick(self.rows, place.micro, 0)]
        for d in range(place.micros - 1):
            whole = order([part[d] for part in both], place.tensor, 0, False)
            blocks.append(whole.reshape(-1, self.rows.shape[2]))
        return lay_tokens(place, blocks)


def blocks_of(place, array):
    return array.reshape(place.micros // PIECES, place.parts, place.tensors, -1, array.shape[-1])


def own_share(place, array, flip=0):
    return pick(pick(blocks_of(place, array), place.part, 1), place.tensor ^ flip, 1)


GROUP = 16


def split_kernel(parts, tensors, tensor_ref, own_ref, *refs):
    came, going_ref, kept_ref = refs[: parts - 1], refs[-2], refs[-1]
    rows = kept_ref.shape[1]

    def group(i, _):
        here = pl.ds(pl.multiple_of(i * GROUP, GROUP), GROUP)
        for d in range(tensors):
            start = (tensor_ref[0] ^ d) * rows + i * GROUP
            there = pl.ds(pl.multiple_of(start, GROUP), GROUP)
            total = own_ref[0, there, :]
            for one in came:
                total = total + one[0, there, :].astype(f32)
            if d:
                going_ref[d - 1, 0, here, :] = total.astype(bf16)
            else:
                kept_ref[0, here, :] = total
        return 0

    lax.fori_loop(0, rows // GROUP, group, 0)


def split_call(place, own, came):
    blocks, tokens, depth = own.shape
    rows = tokens // place.tensors
    others = place.tensors - 1
    return pl.pallas_call(
        functools.partial(split_kernel, place.parts, place.tensors),
        grid_spec=pltpu.PrefetchScalarGridSpec(
            num_scalar_prefetch=1,
            grid=(blocks,),
            in_specs=[pl.BlockSpec((1, tokens, depth), lambda b, _: (b, 0, 0))] * place.parts,
            out_specs=[
                pl.BlockSpec((others, 1, rows, depth), lambda b, _: (0, b, 0, 0)),
                pl.BlockSpec((1, rows, depth), lambda b, _: (b, 0, 0)),
            ],
        ),
        out_shape=[
            jax.ShapeDtypeStruct((others, blocks, rows, depth), bf16),
            jax.ShapeDtypeStruct((blocks, rows, depth), f32),
        ],
        compiler_params=pltpu.CompilerParams(vmem_limit_bytes=8 * 1024 * 1024),
        name="split_terms",
    )(place.tensor.reshape(1), own, *came)


def finish_kernel(places_ref, kept_ref, h_ref, e_ref, norm_ref, *refs):
    sent, grad_ref, sum_ref = refs[:-2], refs[-2], refs[-1]
    rows = kept_ref.shape[1]

    @pl.when(pl.program_id(0) == 0)
    def _():
        sum_ref[...] = jnp.zeros_like(sum_ref)

    def group(i, _):
        here = pl.ds(pl.multiple_of(i * GROUP, GROUP), GROUP)
        dxn = kept_ref[0, here, :]
        for one in sent:
            dxn = dxn + one[0, here, :].astype(f32)
        h = h_ref[0, 0, 0, here, :].astype(f32)
        r = lax.rsqrt(jnp.mean(h * h, axis=1, keepdims=True) + epsilon)
        scaled = dxn * norm_ref[...]
        pull = r * r * r * jnp.mean(scaled * h, axis=1, keepdims=True)
        grad_ref[0, here, :] = (e_ref[0, 0, 0, here, :].astype(f32) + r * scaled - h * pull).astype(bf16)
        found = dxn * h * r
        sum_ref[...] += found[0:8] + found[8:16]
        return 0

    lax.fori_loop(0, rows // GROUP, group, 0)


def finish_call(place, kept, sent, h, e, norm_gain):
    blocks, rows, depth = kept.shape
    share = pl.BlockSpec((1, rows, depth), lambda b, _: (b, 0, 0))
    whole = pl.BlockSpec((1, 1, 1, rows, depth), lambda b, places: (b, places[0], places[1], 0, 0))
    return pl.pallas_call(
        finish_kernel,
        grid_spec=pltpu.PrefetchScalarGridSpec(
            num_scalar_prefetch=1,
            grid=(blocks,),
            in_specs=[share, whole, whole, pl.BlockSpec((1, depth), lambda b, _: (0, 0))] + [share] * len(sent),
            out_specs=[share, pl.BlockSpec((8, depth), lambda b, _: (0, 0))],
        ),
        out_shape=[jax.ShapeDtypeStruct(kept.shape, bf16), jax.ShapeDtypeStruct((8, depth), f32)],
        compiler_params=pltpu.CompilerParams(vmem_limit_bytes=8 * 1024 * 1024),
        name="finish_gradient",
    )(jnp.stack([place.part, place.tensor]), kept, blocks_of(place, h), blocks_of(place, e), norm_gain[None], *sent)


def deal_kernel(parts, widths, rounds, part_ref, *refs):
    mine_ref, send_ref = refs[-2], refs[-1]
    each = len(widths) + rounds
    rows = mine_ref.shape[0]

    def group(i, _):
        here = pl.ds(pl.multiple_of(i * GROUP, GROUP), GROUP)
        for p in range(parts):
            arrays = refs[p * each : (p + 1) * each]
            total = jnp.concatenate([one[here, :].astype(f32) for one in arrays[: len(widths)]], axis=1)
            for one in arrays[len(widths) :]:
                total = total + one[here, :].astype(f32)
            distance = part_ref[0] ^ p

            @pl.when(distance == 0)
            def _():
                mine_ref[here, :] = total

            @pl.when(distance != 0)
            def _():
                send_ref[jnp.maximum(distance - 1, 0), here, :] = total.astype(bf16)

        return 0

    lax.fori_loop(0, rows // GROUP, group, 0)


def deal_call(place, groups, came):
    widths = [block.shape[-1] for block in groups[0]]
    rows, total = groups[0][0].shape[0], sum(widths)
    args = [one for held, round_ in zip(groups, came) for one in list(held) + list(round_)]
    others = place.parts - 1
    step = 3 * GROUP
    return pl.pallas_call(
        functools.partial(deal_kernel, place.parts, widths, len(came[0])),
        grid_spec=pltpu.PrefetchScalarGridSpec(
            num_scalar_prefetch=1,
            grid=(rows // step,),
            in_specs=[pl.BlockSpec((step, one.shape[1]), lambda i, _: (i, 0)) for one in args],
            out_specs=[
                pl.BlockSpec((step, total), lambda i, _: (i, 0)),
                pl.BlockSpec((others, step, total), lambda i, _: (0, i, 0)),
            ],
        ),
        out_shape=[jax.ShapeDtypeStruct((rows, total), f32), jax.ShapeDtypeStruct((others, rows, total), bf16)],
        compiler_params=pltpu.CompilerParams(vmem_limit_bytes=8 * 1024 * 1024),
        name="deal_rows",
    )(place.part.reshape(1), *args)


def beside_kernel(parts, at, part_ref, *refs):
    blocks, out_ref = refs[:parts], refs[-1]
    rows, width = out_ref.shape[0], out_ref.shape[1] // parts

    def group(i, _):
        here = pl.ds(pl.multiple_of(i * GROUP, GROUP), GROUP)
        for d, one in enumerate(blocks):
            there = pl.ds(pl.multiple_of((part_ref[0] ^ d) * width, LANES), width)
            out_ref[here, there] = one[here, at : at + width].astype(f32)
        return 0

    lax.fori_loop(0, rows // GROUP, group, 0)


def columns_beside(place, blocks, at, width):
    if width % LANES or at % LANES:
        return beside([block[:, at : at + width].astype(f32) for block in blocks], place.part)
    shape = (blocks[0].shape[0], place.parts * width)
    step = 3 * GROUP
    return pl.pallas_call(
        functools.partial(beside_kernel, place.parts, at),
        grid_spec=pltpu.PrefetchScalarGridSpec(
            num_scalar_prefetch=1,
            grid=(shape[0] // step,),
            in_specs=[pl.BlockSpec((step, block.shape[1]), lambda i, _: (i, 0)) for block in blocks],
            out_specs=pl.BlockSpec((step, shape[1]), lambda i, _: (i, 0)),
        ),
        out_shape=jax.ShapeDtypeStruct(shape, f32),
        compiler_params=pltpu.CompilerParams(vmem_limit_bytes=8 * 1024 * 1024),
        name="columns_beside",
    )(place.part.reshape(1), *blocks)


def cut(place, block):
    return block.reshape(block.shape[:-2] + (place.tensors, -1, block.shape[-1]))


class Reduction:
    def __init__(self, place, own, send, kind=bf16):
        self.place, self.kind, self.going = place, kind, None
        sends = [send.reshape(own.shape)] if place.parts == 2 else [send[d] for d in range(place.parts - 1)]
        self.came = [place.swap_part(block, d + 1) for d, block in enumerate(sends)]
        self.own = own

    def prepare(self):
        place = self.place
        if self.kind == bf16:
            going, self.kept = split_call(place, self.own, self.came)
            self.going = [going.reshape(self.kept.shape)] if place.tensors == 2 else list(going)
        else:
            own, came = cut(place, self.own), [cut(place, block) for block in self.came]

            def side(tensor):
                return pick(own, tensor, 1) + sum(pick(block, tensor, 1).astype(f32) for block in came)

            self.going = [side(place.tensor ^ d).astype(self.kind) for d in range(1, place.tensors)]
            self.kept = side(place.tensor)

    def launch(self, others=None):
        if self.going is None:
            self.prepare()
        self.going, others = tie(self.going, others)
        self.sent = [self.place.swap_tensor(block, d + 1) for d, block in enumerate(self.going)]
        return others

    def land(self, others):
        self.sent, others = tie(self.sent, others)
        return others

    def result(self):
        return self.kept + sum(block.astype(f32) for block in self.sent)


class Gathering:
    def __init__(self, place, shares, flip=0):
        self.place, self.shares, self.flip = place, shares, flip
        self.came = None

    def launch(self):
        place = self.place
        self.came = [[place.swap_tensor(share, d) for share in self.shares] for d in range(1, place.tensors)]

    def result(self):
        place = self.place
        came = tie(self.came)[0]
        held = [order(list(group), place.tensor ^ self.flip, 1) for group in zip(self.shares, *came)]
        came = tie([[place.swap_part(block, d) for block in held] for d in range(1, place.parts)])[0]
        whole = [order(list(group), place.part, 1) for group in zip(held, *came)]
        return [block.reshape((-1,) + share.shape[2:]) for block, share in zip(whole, self.shares)]


def gather_shares(place, shares, flip=0):
    gathering = Gathering(place, shares, flip)
    gathering.launch()
    return gathering.result()


class Homing:
    def __init__(self, place, own):
        self.place = place
        self.rows = None
        self.own = pick(own, place.micro, 0)
        self.sends = [pick(own, place.micro ^ d, 0) for d in range(1, place.micros)]

    def launch(self):
        self.came = [self.place.swap_micro(block, d + 1) for d, block in enumerate(self.sends)]

    def collect(self):
        self.rows = order([self.own] + self.came, self.place.micro, 0)

    def turn(self, others=None):
        place = self.place
        if self.rows is None:
            self.collect()
        self.rows, others = tie(self.rows, others)
        self.swapped = [place.swap_tensor(self.rows, d) for d in range(1, place.tensors)]
        return others

    def result(self):
        return order([self.rows] + self.swapped, self.place.tensor, 1)


def rows_dot(a, b):
    return jnp.dot(a, b, preferred_element_type=f32)


def columns_dot(a, b):
    return lax.dot_general(a, b, (((0,), (0,)), ((), ())), preferred_element_type=f32)


def forward_piece(place, h, weights, small, carry, dn=None):
    results = forward_call(place, h, weights, small, carry[0], carry[1], dn)
    if dn is None:
        return results[:2], (results[2], results[3])
    kept = (h, carry[1]) + tuple(results[5:])
    return results[:3], (results[3], results[4]), kept


def forward_start(place, small):
    width = small[3].shape[1]
    return jnp.zeros((STATE, width), f32), jnp.zeros((8, width + MAPS), f32)


def factor_of(place, small, squares):
    return lax.rsqrt(squares / (place.tensors * place.parts * small[3].shape[1]) + epsilon)


def out_share(place, h, branch):
    return (own_share(place, h).astype(f32) + branch).astype(bf16)


def gates_piece(place, dn, q, pull, kept, small):
    _, _, _, _, z, y, _ = kept
    return gate_call(place, dn, z, y, q[:, None], pull[:, None], small[3])


def normal_piece(e, q, kept, weights, small):
    _, _, _, _, z, y, _ = kept
    dn, pull, n, gain = normal_call(e, weights, z, y, q[:, None], small[3])
    return dn, pull[:, 0], n, gain


def backward_piece(place, exact, gates, kept, weights, small, carry):
    _, before, _, vbd, _, _, states = kept
    mixed = small[3].shape[1] + MAPS
    count = min(STEP * CHUNK, vbd.shape[0])
    tails = vbd.reshape(-1, count, vbd.shape[1])[:-1, count - 8 :, :mixed]
    before = jnp.concatenate([before[None], tails], axis=0)
    own, send, dvbd, adjoint, du, sums = backward_call(
        place, exact, gates[0], gates[1], vbd, before, states, weights, small, carry[0], carry[1]
    )
    return (own, send), (adjoint, du), dvbd, sums


def input_grad(place, e, h, norm_gain, item):
    return finish_call(place, item.kept, item.sent, h, e, norm_gain)


class Scatter:
    def __init__(self, place, arrays):
        self.place = place
        parts = place.parts
        shape = [2] * len(bits_of(place.micros))
        views = [array.reshape(place.micros, parts, -1, array.shape[1]) for array in arrays]
        self.held = [[view[:, p].reshape(shape + list(view.shape[2:])) for view in views] for p in range(parts)]
        self.came = [[] for _ in range(parts)]
        self.left = [sorted(bits_of(place.micros), reverse=True) for _ in range(parts)]

    def prepare(self):
        place = self.place
        self.out, self.masks = [], []
        for p, left in enumerate(self.left):
            mask = left[0] if p % 2 else left[-1]
            axis = left.index(mask)
            mine = (place.micro // mask) % 2

            def side(bit):
                total = jnp.concatenate([pick(block, bit, axis) for block in self.held[p]], axis=-1)
                for block in self.came[p]:
                    total = total.astype(f32) + pick(block, bit, axis).astype(f32)
                return total.astype(bf16)

            self.out.append(side(1 - mine))
            self.masks.append(mask)
            self.held[p] = [pick(block, mine, axis) for block in self.held[p]]
            self.came[p] = [pick(block, mine, axis) for block in self.came[p]]
            left.remove(mask)

    def launch(self):
        self.next = [self.place.swap_micro(block, mask) for block, mask in zip(self.out, self.masks)]

    def land(self):
        for p, block in enumerate(self.next):
            self.came[p].append(block)

    def trade(self):
        place = self.place
        mine, send = deal_call(place, self.held, self.came)
        sends = [send.reshape(mine.shape)] if place.parts == 2 else list(send)
        return [mine] + [place.swap_part(block, d + 1) for d, block in enumerate(sends)]


def body(
    block_input,
    norm_gain,
    w_gate,
    w_value,
    w_bc,
    w_dt,
    conv_value,
    conv_bc,
    conv_value_bias,
    conv_bc_bias,
    dt_bias,
    decay_log,
    skip,
    gate_gain,
    w_out,
    cotangent,
):
    sections = lax.axis_size("section")
    section = lax.axis_index("section")
    place = Place(block_input.shape[0])
    parts, part = place.parts, place.part
    width = w_gate.shape[2] // parts
    heads_here = w_dt.shape[2] // parts
    mixed = width + MAPS

    def share(vector, size):
        return lax.dynamic_slice_in_dim(vector, part * size, size, vector.ndim - 1)

    def padded(vector):
        return jnp.pad(vector, (0, head_rows(width) - heads_here))

    spread = Spread(place, block_input)
    collected, second = gather_weights(place, w_gate[0], w_value[0], w_bc[0], w_dt[0], w_out[0])
    collected.prepare()
    collected.launch()
    spread.came, collected.next = tie(spread.came, collected.next)
    collected.land()
    h0 = spread.result()
    while collected.masks[0]:
        collected.prepare()
        collected.launch()
        h0, collected.next = tie(h0, collected.next)
        collected.land()
    weights = tuple(collected.result([mixed + LANES, width]))
    taps = jnp.concatenate(
        [
            jnp.concatenate([share(conv_value[0], width), conv_bc[0]], axis=1),
            jnp.concatenate([share(conv_value_bias[0], width), conv_bc_bias[0]])[None],
            jnp.zeros((8 - CONV - 1, mixed), f32),
        ],
        axis=0,
    )
    own_skip = share(skip[0], heads_here)
    rate = jnp.exp(share(decay_log[0], heads_here))
    heads = jnp.concatenate([padded(share(dt_bias[0], heads_here)), padded(rate)])
    heads = jnp.broadcast_to(heads[:, None], (heads.size, LANES))
    inner = jnp.stack([jnp.repeat(own_skip, HEAD_DIM), share(gate_gain[0], width)])
    inner = jnp.concatenate([inner, jnp.zeros((6, width), f32)], axis=0)
    small = (norm_gain[0], taps, heads, inner)

    span = range(PIECES)
    first, last = section == 0, section == sections - 1
    flip = 1 if place.tensors > 1 else 0

    def leave(place_of, block, came, step, others):
        if came:
            newest = list(came)[-1]
            block, came[newest], others = tie(block, came[newest], others)
        else:
            block, others = tie(block, others)
        came[place_of] = place.next_section(block, step, flip if step > 0 else 0)
        return others

    def arrive(i, came, stays, originals, others, flip):
        block, others = tie(came[i], others)
        return jnp.where(stays, own_share(place, originals[i], flip), block), others

    came = None
    for turn in range(sections - 1):
        carry = forward_start(place, small)
        shares_in, came = came, {}
        pieces, halves, terms, crossing = list(h0), [], None, []
        for i in span:
            if shares_in is not None:
                share, terms = arrive(i, shares_in, first, h0, terms, flip)
                pieces[i] = gather_shares(place, [share], flip)[0]
            if i:
                pieces[i], halves[-1][1] = tie(pieces[i], halves[-1][1])
                crossing = [place.swap_tensor(halves[-1][1], mask) for mask in bits_of(place.tensors)]
            if second.masks[0]:
                second.prepare()
                pieces[i], second.out = tie(pieces[i], second.out)
                second.launch()
                terms, carry = forward_piece(place, pieces[i], weights, small, carry)
                terms, crossing, second.next = tie(terms, crossing, second.next)
                second.land()
            else:
                terms, carry = forward_piece(place, pieces[i], weights, small, carry)
                terms, crossing = tie(terms, crossing)
            if i:
                halves[-1][1] = halves[-1][1] + sum(crossing)
            halves.append([terms[0], sum_all(place, terms[1][0, :, 0], micro=False, tensor=False)])
        halves[-1][1] = sum_all(place, halves[-1][1], micro=False, part=False)
        second.finish()
        if len(weights) == 2:
            weights += tuple(second.result([width]))
        red = []
        for g, squares in halves:
            if red:
                g = red[-1].launch(g)
            elif turn == 0:
                g, cotangent = tie(g, cotangent)
                e_blocks = whole_tokens(place, cotangent)
            own, send = out_call(place, g, factor_of(place, small, squares), weights, small[3])
            red.append(Reduction(place, own, send, jnp.float16))
        red[-1].launch()
        if turn == 0:
            e_blocks = red[0].land(e_blocks)
            e0 = lay_tokens(place, e_blocks)
            e0, dn0 = red[-1].land((e0, [rows_dot(e, weights[2]) for e in e0]))
        for i, item in enumerate(red):
            leave(i, out_share(place, pieces[i], item.result()), came, 1, None)
    second.finish()
    if len(weights) == 2:
        weights += tuple(second.result([width]))
    if sections == 1:
        e0 = lay_tokens(place, whole_tokens(place, cotangent))
        dn0 = [rows_dot(e, weights[2]) for e in e0]

    carry = forward_start(place, small)
    kept, sums, lines, terms, ahead = [], [], [], None, None
    for i in span:
        h = h0[i]
        if came is not None:
            if ahead is None:
                share, terms = arrive(i, came, first, h0, terms, flip)
                ahead = Gathering(place, [share], flip)
                ahead.launch()
                if i + 1 < PIECES:
                    ahead.came, came[i + 1] = tie(ahead.came, came[i + 1])
            h = ahead.result()[0]
            ahead = None
            if i + 1 < PIECES:
                share, h = arrive(i + 1, came, first, h0, h, flip)
                h, share = tie(h, share)
                ahead = Gathering(place, [share], flip)
                ahead.launch()
        terms, carry, keep = forward_piece(place, h, weights, small, carry, dn0[i])
        if ahead is not None:
            terms, ahead.came = tie(terms, ahead.came)
        kept.append(keep)
        lines.append(terms[2][:, :, 0])
        sums.append(Reduction(place, terms[0], terms[1]))
    lines = sum_all(place, jnp.stack(lines), micro=False)
    qs = [factor_of(place, small, lines[i, 0]) for i in span]
    dots = [lines[i, 1] for i in span]

    def gradient_of(i, came, others):
        share, others = arrive(i, came, last, e0, others, 0)
        gathering = Gathering(place, [share])
        gathering.launch()
        return gathering, others

    def outputs_of():
        outs = []
        for k in span:
            branch = sums[k].result() * own_share(place, qs[k].reshape(-1, 1))
            outs.append(out_share(place, kept[k][0], branch))
        return Homing(place, jnp.concatenate(outs, axis=0))

    came, homing, ready = None, None, None
    es = list(e0)
    for turn in range(sections - 1):
        carry = forward_start(place, small)
        shares_in, came = came, {}
        es, terms = list(e0), None
        for i in reversed(span):
            dn, pull = dn0[i], dots[i]
            if shares_in is not None:
                ready, terms = gradient_of(i, shares_in, terms)
                es[i] = ready.result()[0]
                dn, pull, _, _ = normal_piece(es[i], qs[i], kept[i], weights, small)
                pull = sum_all(place, pull, micro=False)
            elif homing is None:
                for item in sums:
                    dn = item.launch(dn)
            gates = gates_piece(place, dn, qs[i], pull, kept[i], small)
            if i + 1 < PIECES:
                gates = leave(i + 1, share, came, -1, gates)
            terms, carry, _, _ = backward_piece(place, False, gates, kept[i], weights, small, carry)
            if i + 1 < PIECES:
                terms, came[i + 1] = tie(terms, came[i + 1])
            if homing is None:
                for item in sums:
                    terms = item.land(terms)
            red = Reduction(place, terms[0], terms[1])
            red.launch()
            if homing is None:
                homing = outputs_of()
            if not i and turn == sections - 2 and PIECES > 1:
                ready, _ = gradient_of(PIECES - 1, came, None)
                ready.came = red.land(ready.came)
            share, _ = input_grad(place, es[i], kept[i][0], norm_gain[0], red)
        leave(0, share, came, -1, None)
    if homing is None:
        for item in sums:
            item.launch()
        homing = outputs_of()

    carry = forward_start(place, small)
    red, matrix, small_sums, terms = [], [None] * 3, None, None

    def add(old, a, b):
        now = columns_dot(a, b)
        return now if old is None else old + now

    for i in reversed(span):
        if came is not None:
            if red or ready is None:
                ready, terms = gradient_of(i, came, terms)
            if red:
                red[-1].prepare()
                homing.collect()
                ready.came, red[-1].going, homing.rows = tie(ready.came, red[-1].going, homing.rows)
            es[i] = ready.result()[0]
        dn, pull, n, gain_grad = normal_piece(es[i], qs[i], kept[i], weights, small)
        pull = sum_all(place, pull, micro=False)
        matrix[0] = add(matrix[0], es[i], n)
        pull, matrix[0] = tie(pull, matrix[0])
        if red:
            pull = homing.turn(red[-1].launch(pull))
        else:
            pull, homing.sends = tie(pull, homing.sends)
            homing.launch()
        gates = gates_piece(place, dn, qs[i], pull, kept[i], small)
        if not i:
            scatter = Scatter(place, [matrix[0].astype(bf16), add(matrix[1], kept[i][2], gates[1]).astype(bf16)])
            scatter.prepare()
            gates, scatter.out = tie(gates, scatter.out)
            scatter.launch()
        terms, carry, dvbd, now = backward_piece(place, True, gates, kept[i], weights, small, carry)
        if red:
            terms = red[-1].land(terms)
        else:
            homing.came, terms, gates, dvbd, now = tie(homing.came, terms, gates, dvbd, now)
            if PIECES == 1:
                homing.turn()
        now = [now, gain_grad]
        if i:
            red.append(Reduction(place, terms[0], terms[1]))
            for k, b in ((1, gates[1]), (2, dvbd)):
                matrix[k] = add(matrix[k], kept[i][2], b)
        else:
            ahead = Reduction(place, terms[0], terms[1])
            ahead.own, dvbd, now, scatter.next, homing.swapped = tie(
                ahead.own, dvbd, now, scatter.next, homing.swapped
            )
            scatter.land()
            red.append(ahead)
        small_sums = now if small_sums is None else [a + b for a, b in zip(small_sums, now)]
    outputs = homing.result().reshape(block_input.shape)
    scatter.prepare()
    scatter.launch()
    red[-1].prepare()
    red[-1].going, dvbd = tie(red[-1].going, dvbd)
    red[-1].launch()
    mixes = Scatter(place, [add(matrix[2], kept[0][2], dvbd).astype(bf16)])
    mixes.prepare()
    mixes.launch()
    grads, norm_grad = [], jnp.zeros((8, norm_gain.shape[1]), f32)
    for i, item in zip(reversed(span), red[:-1]):
        block, now = input_grad(place, es[i], kept[i][0], norm_gain[0], item)
        grads.insert(0, block)
        norm_grad = norm_grad + now
    scatter.next = red[-1].land(scatter.next)
    scatter.land()
    while scatter.left[0]:
        scatter.prepare()
        scatter.launch()
        scatter.land()
    block, now = input_grad(place, es[0], kept[0][0], norm_gain[0], red[-1])
    norm_grad = norm_grad + now
    homing = Homing(place, jnp.concatenate([block] + grads, axis=0))
    homing.launch()
    scatter = scatter.trade()
    gate_grad = columns_beside(place, scatter, width, width)
    out_grad = order([block[:, :width].astype(f32).T for block in scatter], part, 0).reshape(-1, w_out.shape[2])
    homing.came, mixes.next, gate_grad, out_grad, outputs = tie(
        homing.came, mixes.next, gate_grad, out_grad, outputs
    )
    mixes.land()
    mixes.prepare()
    homing.collect()
    mixes.out, homing.rows = tie(mixes.out, homing.rows)
    homing.turn()
    mixes.launch()
    packed, gain_grad = small_sums
    norm_grad = jnp.sum(norm_grad, axis=0)
    row = lax.broadcasted_iota(jnp.int32, (8, mixed), 0)
    packed = jnp.where(row == GAIN_ROW, jnp.pad(gain_grad, ((0, 0), (0, MAPS))), packed)
    lanes = max(mixed, norm_grad.size)
    packed = jnp.concatenate(
        [jnp.pad(packed, ((0, 0), (0, lanes - mixed))), jnp.pad(norm_grad[None], ((0, 7), (0, lanes - norm_grad.size)))],
        axis=0,
    )
    mixes.land()
    while mixes.left[0]:
        mixes.prepare()
        mixes.launch()
        mixes.land()
    mixes = mixes.trade()
    packed, mixes = tie(packed, mixes)
    packed = sum_all(place, packed, part=False, tensor=False)
    by_part = [packed] + [place.swap_part(packed, d) for d in range(1, parts)]
    input_grads = homing.result().reshape(block_input.shape).astype(f32)
    value_grad = columns_beside(place, mixes, 0, width)
    step_grad = beside([block[:, mixed : mixed + heads_here].astype(f32) for block in mixes], part)
    maps_grad = sum(block[:, width:mixed].astype(f32) for block in mixes).astype(bf16)
    maps_sum = maps_grad.astype(f32)
    for mask in bits_of(place.tensors):
        maps_sum = maps_sum + place.swap_tensor(maps_sum, mask)

    both = sum_all(place, packed, micro=False)
    wide, bias_grad, gain_grad, maps_small, maps_bias, norm_sum, by_head = unpack(
        place, both, by_part, width, heads_here, norm_grad.size
    )
    total_heads = parts * heads_here
    return (
        outputs[None],
        input_grads[None],
        norm_sum,
        gate_grad[None],
        value_grad[None],
        maps_sum[None],
        step_grad[None],
        wide[None],
        maps_small[None],
        bias_grad,
        maps_bias,
        by_head[0:1, :total_heads],
        by_head[1:2, :total_heads],
        by_head[2:3, :total_heads],
        gain_grad,
        out_grad[None],
    )


def solution(mesh):
    placed = (
        P(None, "context", None),
        P("section", None),
        P("section", "context", "tensor"),
        P("section", "context", "tensor"),
        P("section", "context", None),
        P("section", "context", "tensor"),
        P("section", None, "tensor"),
        P("section", None, None),
        P("section", "tensor"),
        P("section", None),
        P("section", "tensor"),
        P("section", "tensor"),
        P("section", "tensor"),
        P("section", "tensor"),
        P("section", "tensor", "context"),
        P(None, "context", None),
    )
    return jax.shard_map(
        body,
        mesh=mesh,
        in_specs=placed,
        out_specs=(
            P("section", None, "context", None),
            P("section", None, "context", None),
            P("section", None),
            P("section", "context", "tensor"),
            P("section", "context", "tensor"),
            P("section", "context", None),
            P("section", "context", "tensor"),
            P("section", None, "tensor"),
            P("section", None, None),
            P("section", "tensor"),
            P("section", None),
            P("section", "tensor"),
            P("section", "tensor"),
            P("section", "tensor"),
            P("section", "tensor"),
            P("section", "tensor", "context"),
        ),
        check_vma=False,
    )
```

```python
import functools

import jax
import jax.numpy as jnp
from jax import lax
from jax.experimental import pallas as pl
from jax.experimental.pallas import tpu as pltpu
from jax.sharding import PartitionSpec as P

HEAD_DIM = 64
STATE = 128
CONV = 4
MAPS = 2 * STATE
CHUNK = 128
LANES = 128
PIECES = 2

epsilon = 1e-05
bf16 = jnp.bfloat16
f32 = jnp.float32


def low_dot(a, b, contract):
    return lax.dot_general(
        a.astype(bf16), b.astype(bf16), ((contract[0], contract[1]), ((), ())), preferred_element_type=f32
    )


def mm(a, b):
    return low_dot(a, b, ((1,), (0,)))


def mm_nt(a, b):
    return low_dot(a, b, ((1,), (1,)))


def mm_tn(a, b):
    return low_dot(a, b, ((0,), (0,)))


def softplus(v):
    return jnp.maximum(v, 0.0) + jnp.log(1.0 + jnp.exp(-jnp.abs(v)))


def groups_of(width):
    return [
        (at, min(LANES, width - at), at // HEAD_DIM, min(LANES, width - at) // HEAD_DIM)
        for at in range(0, width, LANES)
    ]


def head_rows(width):
    return -(-(width // HEAD_DIM) // 16) * 16


def column(cols, head):
    return jnp.broadcast_to(cols[:, head : head + 1], (cols.shape[0], LANES))


def choose(first, second, lanes):
    if second is None:
        return first[:, :lanes]
    lane = lax.broadcasted_iota(jnp.int32, (first.shape[0], lanes), 1)
    return jnp.where(lane < HEAD_DIM, first, second)


def only(value, which, count):
    if count == 1:
        return value
    lane = lax.broadcasted_iota(jnp.int32, value.shape, 1)
    return jnp.where((lane < HEAD_DIM) == (which == 0), value, jnp.zeros_like(value))


def pieces_of(value, count):
    terms = []
    for _ in range(count):
        term = value.astype(bf16)
        terms.append(term)
        value = value - term.astype(f32)
    return terms


def mm3(a, b):
    (a_hi, a_lo), (b_hi, b_lo) = pieces_of(a, 2), pieces_of(b, 2)
    return mm(jnp.concatenate([a_hi, a_lo, a_hi], axis=1), jnp.concatenate([b_hi, b_hi, b_lo], axis=0))


def mm3_nt(a, b):
    (a_hi, a_lo), (b_hi, b_lo) = pieces_of(a, 2), pieces_of(b, 2)
    return mm_nt(jnp.concatenate([a_hi, a_lo, a_hi], axis=1), jnp.concatenate([b_hi, b_hi, b_lo], axis=1))


def sum_dot(value, zero_one, count):
    return sum(mm(term, zero_one) for term in pieces_of(value, count))


def iotas():
    row = lax.broadcasted_iota(jnp.int32, (CHUNK, CHUNK), 0)
    col = lax.broadcasted_iota(jnp.int32, (CHUNK, CHUNK), 1)
    return row, col


def conv_rows(pad, taps_ref, at, lanes):
    here = slice(at, at + lanes)
    pre = taps_ref[CONV : CONV + 1, here] + taps_ref[CONV - 1 : CONV, here] * pad[8 : 8 + CHUNK, here]
    for k in range(CONV - 1):
        first = 8 - (CONV - 1) + k
        pre = pre + taps_ref[k : k + 1, here] * pad[first : first + CHUNK, here]
    return pre


def decay_terms(dt_pre, heads_ref, rows, row, col):
    wide = dt_pre.T[:rows] + heads_ref[0:rows, :]
    dt = softplus(wide)
    log_decay = sum_dot(-heads_ref[rows : 2 * rows, :] * dt, (row <= col).astype(bf16), 3)
    cols = jnp.concatenate([log_decay, dt, jnp.zeros((CHUNK - 2 * rows, CHUNK), f32)], axis=0).T
    return wide, dt, log_decay, cols


def as_row(value):
    return jnp.sum(value.T, axis=0, keepdims=True)


def filled(value):
    rows, lanes = value.shape
    if lanes == LANES:
        return value
    return jnp.concatenate([value, jnp.zeros((rows, LANES - lanes), f32)], axis=1)


def as_column(row):
    return jnp.broadcast_to(row, (CHUNK, LANES)).T


def deal(part, parts, first, count, total, own_ref, send_ref, sems):
    def own_copy(c):
        rows = total.at[pl.ds(pl.multiple_of(c * CHUNK, CHUNK), CHUNK), :]
        return pltpu.make_async_copy(rows, own_ref.at[(first + c) // parts], sems.at[c])

    def one(c, _):
        index = first + c
        distance = (index % parts) ^ part

        @pl.when(distance == 0)
        def _():
            own_copy(c).start()

        @pl.when(distance != 0)
        def _():
            rows = total[pl.ds(pl.multiple_of(c * CHUNK, CHUNK), CHUNK), :]
            send_ref[jnp.maximum(distance - 1, 0), index // parts] = rows.astype(send_ref.dtype)

        return 0

    def end(c, _):
        @pl.when(((first + c) % parts) ^ part == 0)
        def _():
            own_copy(c).wait()

        return 0

    lax.fori_loop(0, count, one, 0)
    lax.fori_loop(0, count, end, 0)


def forward_kernel(keep, width, parts, per_step, part_ref, h_ref, w1_ref, wg_ref, norm_ref, taps_ref, heads_ref, inner_ref, s0_ref, tail0_ref, *rest):
    if keep:
        wo_ref, dn_ref, own_ref, send_ref, sums_ref, st_ref, tail_ref, xn_ref, vbd_ref, z_ref, y_ref, sin_ref, pad, gg, total, sems = rest
    else:
        g_ref, sums_ref, st_ref, tail_ref, xn_ref, vbd_ref, z_ref, pad = rest
    mixed = width + MAPS
    rows = head_rows(width)
    step = pl.program_id(0)

    @pl.when(step == 0)
    def _():
        st_ref[...] = s0_ref[...]
        tail_ref[...] = tail0_ref[...]

    def norm(c, _):
        here = pl.ds(pl.multiple_of(c * 64, 64), 64)
        hf = h_ref[here, :].astype(f32)
        scale = lax.rsqrt(jnp.mean(hf * hf, axis=1, keepdims=True) + epsilon)
        xn_ref[here, :] = (hf * scale * norm_ref[...]).astype(bf16)
        return 0

    lax.fori_loop(0, per_step * 2, norm, 0)
    vbd_ref[...] = jnp.dot(xn_ref[...], w1_ref[...], preferred_element_type=f32)
    z_ref[...] = jnp.dot(xn_ref[...], wg_ref[...], preferred_element_type=f32)
    row, col = iotas()

    def chunk(c, _):
        here = pl.ds(pl.multiple_of(c * CHUNK, CHUNK), CHUNK)
        pad[0:8, :] = tail_ref[...]
        pad[8 : 8 + CHUNK, :] = vbd_ref[here, :mixed]
        tail_ref[...] = pad[CHUNK : CHUNK + 8, :]
        pre = conv_rows(pad, taps_ref, width, MAPS)
        maps = pre * jax.nn.sigmoid(pre)
        b, c_map = maps[:, :STATE], maps[:, STATE:]
        b_rows = b.T
        _, _, log_row, cols = decay_terms(vbd_ref[here, mixed:], heads_ref, rows, row, col)
        contact = jnp.where(row >= col, mm3(c_map, b_rows), 0.0)
        if keep:
            sin_ref[c] = st_ref[...]
        carried = mm3(c_map, st_ref[...])
        squares = jnp.zeros((CHUNK, LANES), f32)
        pulls = jnp.zeros((CHUNK, LANES), f32)
        for at, lanes, head, count in groups_of(width):
            span = slice(at, at + lanes)
            pre = conv_rows(pad, taps_ref, at, lanes)
            own = pre * jax.nn.sigmoid(pre)
            logs = [column(cols, head + j) for j in range(count)]
            steps = [column(cols, rows + head + j) for j in range(count)]
            log_x = choose(logs[0], logs[-1] if count == 2 else None, lanes)
            step_x = choose(steps[0], steps[-1] if count == 2 else None, lanes)
            last_x = log_x[CHUNK - 1 : CHUNK, :]
            xd = own * step_x
            mixing = [
                jnp.exp(jnp.minimum(logs[j] - log_row[head + j : head + j + 1, :], 0.0)) * contact
                for j in range(count)
            ]
            inside = mm3(
                jnp.concatenate(mixing, axis=1),
                jnp.concatenate([only(xd, j, count) for j in range(count)], axis=0),
            )
            y = inside + jnp.exp(log_x) * carried[:, span] + inner_ref[0:1, span] * own
            st_ref[:, span] = jnp.exp(last_x) * st_ref[:, span] + mm3(b_rows, jnp.exp(last_x - log_x) * xd)
            z = z_ref[here, span]
            g = y * (z * jax.nn.sigmoid(z))
            if keep:
                gg[here, span] = (g * inner_ref[1:2, span]).astype(bf16)
                y_ref[here, span] = y
            else:
                g_ref[here, span] = g
            squares = squares + filled(g * g)
            if keep:
                pulls = pulls + filled(dn_ref[here, span] * inner_ref[1:2, span] * g)
        sums_ref[0, c] = as_row(squares)
        if keep:
            sums_ref[1, c] = as_row(pulls)
        return 0

    lax.fori_loop(0, per_step, chunk, 0, unroll=2 if per_step % 2 == 0 else 1)
    if keep:
        total[...] = lax.dot_general(
            gg[...], wo_ref[...], (((1,), (1,)), ((), ())), preferred_element_type=f32
        )
        deal(part_ref[0], parts, step * per_step, per_step, total, own_ref, send_ref, sems)


def out_kernel(parts, per_step, part_ref, g_ref, q_ref, inner_ref, wo_ref, own_ref, send_ref, n, total, sems):
    def chunk(c, _):
        here = pl.ds(pl.multiple_of(c * CHUNK, CHUNK), CHUNK)
        q = as_column(q_ref[c])
        for at, lanes, _, _ in groups_of(n.shape[1]):
            span = slice(at, at + lanes)
            n[here, span] = (g_ref[here, span] * q[:, :lanes] * inner_ref[1:2, span]).astype(bf16)
        return 0

    lax.fori_loop(0, per_step, chunk, 0, unroll=2 if per_step % 2 == 0 else 1)
    total[...] = lax.dot_general(n[...], wo_ref[...], (((1,), (1,)), ((), ())), preferred_element_type=f32)
    deal(part_ref[0], parts, pl.program_id(0) * per_step, per_step, total, own_ref, send_ref, sems)


def out_call(place, g, q, weights, inner):
    wo = weights[2]
    tokens, width = g.shape
    depth = wo.shape[0]
    chunks = tokens // CHUNK
    per_step = min(STEP, chunks)
    steps = chunks // per_step
    count = per_step * CHUNK
    blocks = chunks // place.parts
    shapes = [(blocks, CHUNK, depth), (place.parts - 1, blocks, CHUNK, depth)]
    return pl.pallas_call(
        functools.partial(out_kernel, place.parts, per_step),
        grid_spec=pltpu.PrefetchScalarGridSpec(
            num_scalar_prefetch=1,
            grid=(steps,),
            in_specs=[
                block(steps, (count, width), lambda i, _: (i, 0)),
                block(steps, (per_step, 1, LANES), lambda i, _: (i, 0, 0)),
                once(inner.shape),
                once(wo.shape),
            ],
            out_specs=[pl.BlockSpec(memory_space=pl.ANY), once(shapes[1])],
            scratch_shapes=[
                pltpu.VMEM((count, width), bf16),
                pltpu.VMEM((count, depth), f32),
                pltpu.SemaphoreType.DMA((per_step,)),
            ],
        ),
        out_shape=[jax.ShapeDtypeStruct(shape, f32) for shape in shapes],
        compiler_params=kernel_params(steps, 8),
        cost_estimate=pl.CostEstimate(
            flops=tokens * width * 6000, bytes_accessed=tokens * depth * 8, transcendentals=0
        ),
        name="out_forward",
    )(place.part.reshape(1), g, q[:, None], inner, wo)


STEP = 4
GAIN_ROW = CONV + 1
HEAD_ROW = CONV + 2


def kernel_params(steps, megabytes):
    return pltpu.CompilerParams(vmem_limit_bytes=(megabytes if steps == 1 else 40) * 1024 * 1024)


def once(shape):
    return pl.BlockSpec(memory_space=pltpu.VMEM)


def block(steps, shape, index_map):
    return once(shape) if steps == 1 else pl.BlockSpec(shape, index_map)


def forward_call(place, h, weights, small, s0, tail0, dn=None):
    w1, wg = weights[:2]
    norm_gain, taps, heads, inner = small
    keep = dn is not None
    tokens, depth = h.shape
    width = inner.shape[1]
    mixed = width + MAPS
    chunks = tokens // CHUNK
    per_step = min(STEP, chunks)
    steps = chunks // per_step
    count = per_step * CHUNK
    blocks = chunks // place.parts
    rows = lambda lanes: block(steps, (count, lanes), lambda i, _: (i, 0))
    if keep:
        shapes = [((blocks, CHUNK, depth), f32), ((place.parts - 1, blocks, CHUNK, depth), bf16)]
        out_shape = [jax.ShapeDtypeStruct(*item) for item in shapes]
        out_specs = [pl.BlockSpec(memory_space=pl.ANY), once(shapes[1][0])]
    else:
        out_shape = [jax.ShapeDtypeStruct((tokens, width), f32)]
        out_specs = [rows(width)]
    out_shape += [
        jax.ShapeDtypeStruct((2, chunks, 1, LANES), f32),
        jax.ShapeDtypeStruct((STATE, width), f32),
        jax.ShapeDtypeStruct((8, mixed), f32),
    ]
    out_specs += [
        block(steps, (2, per_step, 1, LANES), lambda i, _: (0, i, 0, 0)),
        once((STATE, width)),
        once((8, mixed)),
    ]
    in_specs = [
        rows(depth),
        once(w1.shape),
        once(wg.shape),
        once((1, depth)),
        once(taps.shape),
        once(heads.shape),
        once(inner.shape),
        once(s0.shape),
        once(tail0.shape),
    ]
    args = [h, w1, wg, norm_gain[None], taps, heads, inner, s0, tail0]
    held = [((tokens, depth), bf16), ((tokens, w1.shape[1]), f32), ((tokens, width), f32)]
    scratch = []
    if keep:
        in_specs += [once(weights[2].shape), rows(width)]
        args += [weights[2], dn]
        held.append(((tokens, width), f32))
        out_shape += [jax.ShapeDtypeStruct(*item) for item in held]
        out_specs += [rows(shape[1]) for shape, _ in held]
        out_shape.append(jax.ShapeDtypeStruct((chunks, STATE, width), f32))
        out_specs.append(block(steps, (per_step, STATE, width), lambda i, _: (i, 0, 0)))
    else:
        scratch = [pltpu.VMEM((count, shape[1]), kind) for shape, kind in held]
    scratch.append(pltpu.VMEM((CHUNK + 8, mixed), f32))
    if keep:
        scratch += [
            pltpu.VMEM((count, width), bf16),
            pltpu.VMEM((count, depth), f32),
            pltpu.SemaphoreType.DMA((per_step,)),
        ]
    return pl.pallas_call(
        functools.partial(forward_kernel, keep, width, place.parts, per_step),
        grid_spec=pltpu.PrefetchScalarGridSpec(
            num_scalar_prefetch=1, grid=(steps,), in_specs=in_specs, out_specs=out_specs, scratch_shapes=scratch
        ),
        out_shape=out_shape,
        compiler_params=kernel_params(steps, 12 if keep else 13),
        cost_estimate=pl.CostEstimate(
            flops=tokens * width * 40000, bytes_accessed=tokens * depth * 16, transcendentals=0
        ),
        name="section_forward",
    )(place.part.reshape(1), *args)


def normal_kernel(full, width, per_step, e_ref, wo_ref, z_ref, y_ref, q_ref, inner_ref, dn_ref, pull_ref, n_ref, gain_ref, gains):
    dn_ref[...] = jnp.dot(e_ref[...], wo_ref[...], preferred_element_type=f32)

    @pl.when(pl.program_id(0) == 0)
    def _():
        gains[...] = jnp.zeros_like(gains)

    def chunk(c, _):
        here = pl.ds(pl.multiple_of(c * CHUNK, CHUNK), CHUNK)
        q = as_column(q_ref[c])
        pulls = jnp.zeros((CHUNK, LANES), f32)
        for at, lanes, _, _ in groups_of(width):
            span = slice(at, at + lanes)
            z, dn_x, gain = z_ref[here, span], dn_ref[here, span], inner_ref[1:2, span]
            g = y_ref[here, span] * (z * jax.nn.sigmoid(z))
            gq = g * q[:, :lanes]
            pulls = pulls + filled(dn_x * gain * g)
            n_ref[here, span] = (gq * gain).astype(bf16)
            gains[:, span] += fold(dn_x * gq)
        pull_ref[c] = as_row(pulls)
        return 0

    lax.fori_loop(0, per_step, chunk, 0, unroll=2 if per_step % 2 == 0 else 1)
    gain_ref[...] = jnp.broadcast_to(jnp.sum(gains[...], axis=0, keepdims=True), gains.shape)


def gate_kernel(width, per_step, total, dn_ref, z_ref, y_ref, q_ref, pull_ref, inner_ref, dy_ref, dz_ref):
    def chunk(c, _):
        here = pl.ds(pl.multiple_of(c * CHUNK, CHUNK), CHUNK)
        q = as_column(q_ref[c])
        pull = as_column(pull_ref[c]) * (q * q * q) * (1.0 / total)
        for at, lanes, _, _ in groups_of(width):
            span = slice(at, at + lanes)
            z, y = z_ref[here, span], y_ref[here, span]
            sig = jax.nn.sigmoid(z)
            silu = z * sig
            dg = q[:, :lanes] * (dn_ref[here, span] * inner_ref[1:2, span]) - y * silu * pull[:, :lanes]
            dy_ref[here, span] = dg * silu
            dz_ref[here, span] = (dg * y * (sig + silu * (1.0 - sig))).astype(bf16)
        return 0

    lax.fori_loop(0, per_step, chunk, 0, unroll=2 if per_step % 2 == 0 else 1)


def normal_call(e, weights, z, y, q, inner):
    wo = weights[2]
    tokens, depth = e.shape
    width = inner.shape[1]
    chunks = tokens // CHUNK
    per_step = min(STEP, chunks)
    steps = chunks // per_step
    rows = lambda lanes: block(steps, (per_step * CHUNK, lanes), lambda i: (i, 0))
    lines = block(steps, (per_step, 1, LANES), lambda i: (i, 0, 0))
    return pl.pallas_call(
        functools.partial(normal_kernel, True, width, per_step),
        grid=(steps,),
        in_specs=[rows(depth), once(wo.shape), rows(width), rows(width), lines, once(inner.shape)],
        out_specs=[rows(width), lines, rows(width), once((8, width))],
        out_shape=[
            jax.ShapeDtypeStruct((tokens, width), f32),
            jax.ShapeDtypeStruct((chunks, 1, LANES), f32),
            jax.ShapeDtypeStruct((tokens, width), bf16),
            jax.ShapeDtypeStruct((8, width), f32),
        ],
        scratch_shapes=[pltpu.VMEM((8, width), f32)],
        compiler_params=kernel_params(steps, 4),
        cost_estimate=pl.CostEstimate(
            flops=tokens * width * 9000, bytes_accessed=tokens * depth * 16, transcendentals=0
        ),
        name="norm_backward",
    )(e, wo, z, y, q, inner)


def gate_call(place, dn, z, y, q, pull, inner):
    tokens, width = dn.shape
    chunks = tokens // CHUNK
    per_step = min(STEP, chunks)
    steps = chunks // per_step
    rows = lambda lanes: block(steps, (per_step * CHUNK, lanes), lambda i: (i, 0))
    lines = block(steps, (per_step, 1, LANES), lambda i: (i, 0, 0))
    return pl.pallas_call(
        functools.partial(gate_kernel, width, per_step, place.tensors * place.parts * width),
        grid=(steps,),
        in_specs=[rows(width), rows(width), rows(width), lines, lines, once(inner.shape)],
        out_specs=[rows(width), rows(width)],
        out_shape=[jax.ShapeDtypeStruct((tokens, width), f32), jax.ShapeDtypeStruct((tokens, width), bf16)],
        compiler_params=kernel_params(steps, 4),
        cost_estimate=pl.CostEstimate(
            flops=tokens * width * 6000, bytes_accessed=tokens * width * 16, transcendentals=0
        ),
        name="gate_backward",
    )(dn, z, y, q, pull, inner)


def fold(value):
    return jnp.sum(value.reshape(CHUNK // 8, 8, value.shape[1]), axis=0)


def backward_kernel(
    exact,
    width,
    parts,
    per_step,
    steps,
    part_ref,
    dy_ref,
    dz_ref,
    vbd_ref,
    before_ref,
    sin_ref,
    w1_ref,
    wg_ref,
    taps_ref,
    heads_ref,
    inner_ref,
    g0_ref,
    du0_ref,
    own_ref,
    send_ref,
    dvbd_ref,
    gt_ref,
    dut_ref,
    tapg_ref,
    pad,
    dpad,
    sums,
    y_in,
    dxd_out,
    dy_in_all,
    xd_out_all,
    total,
    taps_sum,
    headg_ref,
    skipg_ref,
    back_all,
    sems,
):
    mixed = width + MAPS
    rows = head_rows(width)
    step = steps - 1 - pl.program_id(0)

    @pl.when(pl.program_id(0) == 0)
    def _():
        gt_ref[...] = g0_ref[...]
        dut_ref[...] = du0_ref[...]
        taps_sum[...] = jnp.zeros_like(taps_sum)
        headg_ref[...] = jnp.zeros_like(headg_ref)
        skipg_ref[...] = jnp.zeros_like(skipg_ref)

    row, col = iotas()
    causal = col >= row
    strict = col > row
    onward = (row >= col).astype(bf16)
    head_of = lax.broadcasted_iota(jnp.int32, (rows, width), 1) // HEAD_DIM
    ones = (head_of == lax.broadcasted_iota(jnp.int32, (rows, width), 0)).astype(bf16)

    def conv_back(here, at, lanes, du):
        span = slice(at, at + lanes)
        dpad[0:CHUNK, span] = du
        m = pad[8 : 8 + CHUNK, span]
        taps_sum[CONV * 8 : CONV * 8 + 8, span] += fold(du)
        taps_sum[CONV * 8 - 8 : CONV * 8, span] += fold(m * du)
        dm = taps_ref[CONV - 1 : CONV, span] * du
        for k in range(CONV - 1):
            first = CONV - 1 - k
            moved = dpad[first : first + CHUNK, span]
            dm = dm + taps_ref[k : k + 1, span] * moved
            taps_sum[k * 8 : k * 8 + 8, span] += fold(m * moved)
        dvbd_ref[here, span] = dm.astype(bf16)

    def chunk(reverse, _):
        c = per_step - 1 - reverse
        here = pl.ds(pl.multiple_of(c * CHUNK, CHUNK), CHUNK)
        dpad[CHUNK : CHUNK + 8, :] = dut_ref[...]
        pad[8 : 8 + CHUNK, :] = vbd_ref[here, :mixed]

        @pl.when(c == 0)
        def _():
            pad[0:8, :] = before_ref[0]

        @pl.when(c != 0)
        def _():
            pad[0:8, :] = vbd_ref[pl.ds(pl.multiple_of(jnp.maximum(c * CHUNK - 8, 0), 8), 8), :mixed]

        pre = conv_rows(pad, taps_ref, width, MAPS)
        sig = jax.nn.sigmoid(pre)
        maps = pre * sig
        maps_slope = sig + maps * (1.0 - sig)
        b_maps, c_maps = maps[:, :STATE], maps[:, STATE:]
        b_low, c_low = b_maps.astype(bf16), c_maps.astype(bf16)
        wide, dt, log_row, cols = decay_terms(vbd_ref[here, mixed:], heads_ref, rows, row, col)
        contact = jnp.where(causal, mm_nt(b_low, c_low), 0.0)
        back_low = gt_ref[...].astype(bf16)
        if exact:
            back_all[...] = gt_ref[...]
        c_rows = c_low.T
        y_in[...] = mm(c_low, sin_ref[c])
        dxd_out[...] = mm(b_low, back_low)
        dcontact = jnp.zeros((CHUNK, CHUNK), f32)
        log_rows, through = [], []
        for at, lanes, head, count in groups_of(width):
            span = slice(at, at + lanes)
            pre = conv_rows(pad, taps_ref, at, lanes)
            sig = jax.nn.sigmoid(pre)
            own = pre * sig
            slope = sig + own * (1.0 - sig)
            logs = [column(cols, head + j) for j in range(count)]
            steps_of = [column(cols, rows + head + j) for j in range(count)]
            log_x = choose(logs[0], logs[-1] if count == 2 else None, lanes)
            step_x = choose(steps_of[0], steps_of[-1] if count == 2 else None, lanes)
            last_x = log_x[CHUNK - 1 : CHUNK, :]
            dy = dy_ref[here, span]
            xd = own * step_x
            xd_low = xd.astype(bf16)
            dy_low = dy.astype(bf16)
            to_end = jnp.exp(last_x - log_x)
            dy_in = jnp.exp(log_x) * dy
            dy_in_low = dy_in.astype(bf16)
            if exact:
                dy_in_all[:, span] = dy_in
                xd_out_all[:, span] = to_end * xd
                dmix = mm3_nt(jnp.concatenate([only(xd, j, count) for j in range(count)], axis=0), dy)
            else:
                dy_in_all[:, span] = dy_in_low
                xd_out_all[:, span] = (to_end * xd).astype(bf16)
                dmix = mm_nt(jnp.concatenate([only(xd_low, j, count) for j in range(count)], axis=0), dy_low)
            mixing, products = [], []
            for j in range(count):
                decay = jnp.exp(jnp.minimum(log_row[head + j : head + j + 1, :] - logs[j], 0.0))
                one = decay * contact
                d_one = dmix[j * CHUNK : (j + 1) * CHUNK]
                dcontact = dcontact + decay * d_one
                mixing.append(one.astype(bf16))
                products.append((one * d_one).astype(bf16))
            dxd_in = mm(
                jnp.concatenate(mixing, axis=1),
                jnp.concatenate([only(dy_low, j, count) for j in range(count)], axis=0),
            )
            later = mm(jnp.concatenate(products, axis=0), onward)
            for j in range(count):
                log_rows.append(
                    jnp.sum(jnp.where(strict, later[j * CHUNK : (j + 1) * CHUNK], 0.0), axis=0, keepdims=True)
                )
            from_end = to_end * dxd_out[:, span]
            dxd = dxd_in + from_end
            sums[0:CHUNK, span] = (dy_in * y_in[:, span]).astype(bf16)
            sums[CHUNK : 2 * CHUNK, span] = (xd * from_end).astype(bf16)
            sums[2 * CHUNK : 3 * CHUNK, span] = (own * dxd).astype(bf16)
            carried = jnp.exp(last_x)
            back = gt_ref[:, span]
            through.append(
                jnp.sum(carried * sin_ref[c, :, span].astype(f32) * back, axis=0, keepdims=True)
            )
            skipg_ref[:, span] += fold(dy * own)
            gt_ref[:, span] = carried * back + mm(c_rows, dy_in_low)
            conv_back(here, at, lanes, (step_x * dxd + inner_ref[0:1, span] * dy) * slope)
        dcontact = jnp.where(causal, dcontact, 0.0)
        if exact:
            db = mm3_nt(xd_out_all[...], back_all[...]) + mm3(dcontact, c_maps)
            dc = mm3_nt(dy_in_all[...], sin_ref[c]) + mm3(dcontact.T, b_maps)
        else:
            db = mm_nt(xd_out_all[...], back_low) + mm(dcontact, c_low)
            dc = mm_nt(dy_in_all[...], sin_ref[c]) + mm_tn(dcontact, b_low)
        conv_back(here, width, STATE, db * maps_slope[:, :STATE])
        conv_back(here, width + STATE, STATE, dc * maps_slope[:, STATE:])
        dut_ref[...] = dpad[0:8, :]

        by_token = mm_nt(ones, sums[...])
        entering = by_token[:, :CHUNK]
        leaving = by_token[:, CHUNK : 2 * CHUNK]
        direct = by_token[:, 2 * CHUNK :]
        ends = jnp.broadcast_to(jnp.concatenate(through, axis=1), (CHUNK, width))
        ends = sum(mm_nt(ones, term) for term in pieces_of(ends, 2))
        inside = log_rows
        if rows > len(log_rows):
            inside = log_rows + [jnp.zeros((rows - len(log_rows), CHUNK), f32)]
        dlog = (
            jnp.concatenate(inside, axis=0)
            + sum_dot(entering, onward, 2)
            + sum_dot(leaving, (row < col).astype(bf16), 2)
            + ends
        )
        rate = heads_ref[rows : 2 * rows, :]
        ddt_pre = (direct - rate * dlog) * jax.nn.sigmoid(wide)
        headg_ref[0:rows, :] += ddt_pre
        headg_ref[rows : 2 * rows, :] += -rate * dt * dlog
        ddt_cols = jnp.concatenate([ddt_pre, jnp.zeros((CHUNK - rows, CHUNK), f32)], axis=0).T
        dvbd_ref[here, mixed:] = ddt_cols.astype(bf16)
        return 0

    lax.fori_loop(0, per_step, chunk, 0, unroll=2 if per_step % 2 == 0 else 1)
    nt = (((1,), (1,)), ((), ()))
    total[...] = lax.dot_general(dvbd_ref[...], w1_ref[...], nt, preferred_element_type=f32)
    total[...] += lax.dot_general(dz_ref[...], wg_ref[...], nt, preferred_element_type=f32)

    @pl.when(pl.program_id(0) == steps - 1)
    def _():
        tapg_ref[...] = jnp.zeros_like(tapg_ref)
        for k in range(CONV + 1):
            tapg_ref[k : k + 1, :] = jnp.sum(taps_sum[k * 8 : k * 8 + 8, :], axis=0, keepdims=True)
        skips = jnp.broadcast_to(jnp.sum(skipg_ref[...], axis=0, keepdims=True), (CHUNK, width))
        skips = sum(mm_nt(ones, term) for term in pieces_of(skips, 3))
        by_head = jnp.broadcast_to(jnp.sum(headg_ref[...], axis=1, keepdims=True), (2 * rows, LANES))
        columns = jnp.concatenate([by_head, skips, jnp.zeros((CHUNK - 3 * rows, LANES), f32)], axis=0)
        tapg_ref[HEAD_ROW : HEAD_ROW + 1, 0:LANES] = columns.T[0:1]

    deal(part_ref[0], parts, step * per_step, per_step, total, own_ref, send_ref, sems)


def backward_call(place, exact, dy, dz, vbd, before, states, weights, small, g0, du0):
    w1, wg, _ = weights
    _, taps, heads, inner = small
    tokens, width = dy.shape
    depth = w1.shape[0]
    mixed = width + MAPS
    chunks = tokens // CHUNK
    per_step = min(STEP, chunks)
    steps = chunks // per_step
    count = per_step * CHUNK
    blocks = chunks // place.parts
    rows = lambda lanes: block(steps, (count, lanes), lambda i, _: (steps - 1 - i, 0))
    deep = lambda number, height, lanes: block(
        steps, (number, height, lanes), lambda i, _: (steps - 1 - i, 0, 0)
    )
    shapes = [
        ((STATE, width), f32),
        ((8, mixed), f32),
        ((8, mixed), f32),
    ]
    results = pl.pallas_call(
        functools.partial(backward_kernel, exact, width, place.parts, per_step, steps),
        grid_spec=pltpu.PrefetchScalarGridSpec(
            num_scalar_prefetch=1,
            grid=(steps,),
            in_specs=[
                rows(width),
                rows(width),
                rows(vbd.shape[1]),
                deep(1, 8, mixed),
                deep(per_step, STATE, width),
                once(w1.shape),
                once(wg.shape),
                once(taps.shape),
                once(heads.shape),
                once(inner.shape),
                once(g0.shape),
                once(du0.shape),
            ],
            out_specs=[
                pl.BlockSpec(memory_space=pl.ANY),
                once((place.parts - 1, blocks, CHUNK, depth)),
                rows(vbd.shape[1]),
            ]
            + [once(shape) for shape, _ in shapes],
            scratch_shapes=[
                pltpu.VMEM((CHUNK + 8, mixed), f32),
                pltpu.VMEM((CHUNK + 8, mixed), f32),
                pltpu.VMEM((3 * CHUNK, width), bf16),
                pltpu.VMEM((CHUNK, width), f32),
                pltpu.VMEM((CHUNK, width), f32),
                pltpu.VMEM((CHUNK, width), f32 if exact else bf16),
                pltpu.VMEM((CHUNK, width), f32 if exact else bf16),
                pltpu.VMEM((count, depth), f32),
                pltpu.VMEM((8 * (CONV + 1), mixed), f32),
                pltpu.VMEM((2 * head_rows(width), LANES), f32),
                pltpu.VMEM((8, width), f32),
                pltpu.VMEM((STATE, width), f32),
                pltpu.SemaphoreType.DMA((per_step,)),
            ],
        ),
        out_shape=[
            jax.ShapeDtypeStruct((blocks, CHUNK, depth), f32),
            jax.ShapeDtypeStruct((place.parts - 1, blocks, CHUNK, depth), bf16),
            jax.ShapeDtypeStruct(vbd.shape, bf16),
        ]
        + [jax.ShapeDtypeStruct(*item) for item in shapes],
        compiler_params=kernel_params(steps, 14),
        cost_estimate=pl.CostEstimate(
            flops=tokens * width * 60000, bytes_accessed=tokens * depth * 16, transcendentals=0
        ),
        name="section_backward",
    )(place.part.reshape(1), dy, dz, vbd, before, states, w1, wg, taps, heads, inner, g0, du0)
    own, send, dvbd, gt, dut, sums = results
    return own, send, dvbd, gt, dut, sums


def unpack_kernel(parts, heads, rows, part_ref, both_ref, *refs):
    locals_ref, outs = refs[:parts], refs[parts:]
    wide_ref, bias_ref, gain_ref, maps_ref, maps_bias_ref, norm_ref, heads_ref = outs
    width = wide_ref.shape[1] // parts
    part = part_ref[0]
    lane = lax.broadcasted_iota(jnp.int32, (1, LANES), 1)
    by_head = [jnp.zeros((1, LANES), f32) for _ in range(3)]
    for d in range(parts):
        owner = part ^ d
        here = pl.ds(pl.multiple_of(owner * width, HEAD_DIM), width)
        ref = locals_ref[d]
        if width % LANES == 0:
            wide_ref[:, here] = ref[0:CONV, 0:width]
            bias_ref[:, here] = ref[CONV : CONV + 1, 0:width]
            gain_ref[:, here] = ref[GAIN_ROW : GAIN_ROW + 1, 0:width]
        else:
            for p in range(parts):

                @pl.when(owner == p)
                def _():
                    there = slice(p * width, (p + 1) * width)
                    wide_ref[:, there] = ref[0:CONV, 0:width]
                    bias_ref[:, there] = ref[CONV : CONV + 1, 0:width]
                    gain_ref[:, there] = ref[GAIN_ROW : GAIN_ROW + 1, 0:width]

        for k in range(3):
            values = ref[HEAD_ROW : HEAD_ROW + 1, 0:LANES]
            for p in range(parts):
                moved = pltpu.roll(values, (p * heads - k * rows) % LANES, 1)
                chosen = (owner == p) & (lane >= p * heads) & (lane < (p + 1) * heads)
                by_head[k] = jnp.where(chosen, moved, by_head[k])
    heads_ref[...] = jnp.concatenate(by_head + [jnp.zeros((5, LANES), f32)], axis=0)
    maps_ref[...] = both_ref[0:CONV, width : width + MAPS]
    maps_bias_ref[...] = both_ref[CONV : CONV + 1, width : width + MAPS]
    norm_ref[...] = both_ref[8:9, 0 : norm_ref.shape[1]]


def unpack(place, both, by_part, width, heads, depth):
    total = place.parts * width
    shapes = [(CONV, total), (1, total), (1, total), (CONV, MAPS), (1, MAPS), (1, depth), (8, LANES)]
    return pl.pallas_call(
        functools.partial(unpack_kernel, place.parts, heads, head_rows(width)),
        grid_spec=pltpu.PrefetchScalarGridSpec(
            num_scalar_prefetch=1,
            grid=(1,),
            in_specs=[once(both.shape)] * (1 + place.parts),
            out_specs=[once(shape) for shape in shapes],
        ),
        out_shape=[jax.ShapeDtypeStruct(shape, f32) for shape in shapes],
        compiler_params=pltpu.CompilerParams(vmem_limit_bytes=4 * 1024 * 1024),
        name="unpack_small",
    )(place.part.reshape(1), both, *by_part)


class Place:
    def __init__(self, micro_count):
        self.context = lax.axis_size("context")
        self.micros = micro_count
        self.parts = self.context // micro_count
        self.tensors = lax.axis_size("tensor")
        index = lax.axis_index("context")
        self.micro = index // self.parts
        self.part = index % self.parts
        self.tensor = lax.axis_index("tensor")

    def swap_part(self, block, mask):
        return lax.ppermute(block, "context", [(i, i ^ mask) for i in range(self.context)])

    def swap_micro(self, block, mask):
        return self.swap_part(block, mask * self.parts)

    def swap_tensor(self, block, mask):
        return lax.ppermute(block, "tensor", [(i, i ^ mask) for i in range(self.tensors)])

    def swap_both(self, block):
        count = self.context * self.tensors
        return lax.ppermute(block, ("context", "tensor"), [(i, i ^ self.tensors ^ 1) for i in range(count)])

    def next_section(self, block, step, flip):
        count, tensors = lax.axis_size("section"), self.tensors
        return lax.ppermute(
            block,
            ("section", "tensor"),
            [
                (i * tensors + t, (i + step) * tensors + (t ^ flip))
                for i in range(count)
                if 0 <= i + step < count
                for t in range(tensors)
            ],
        )


def pick(array, index, axis):
    return lax.dynamic_index_in_dim(array, index, axis, False)


def tie(*items):
    return lax.optimization_barrier(items)


def bits_of(count):
    masks = []
    mask = 1
    while mask < count:
        masks.append(mask)
        mask *= 2
    return masks


def order_kernel(count, axis, index_ref, *refs):
    blocks, out, sems = refs[:count], refs[count], refs[count + 1]
    copies = []
    for d, one in enumerate(blocks):
        there = (slice(None),) * axis + (index_ref[0] ^ d,)
        copies.append(pltpu.make_async_copy(one, out.at[there], sems.at[d]))
    for one in copies:
        one.start()
    for one in copies:
        one.wait()


def order(blocks, index, axis, copies=True):
    count = len(blocks)
    shape = list(blocks[0].shape)
    shape.insert(axis, count)
    if count == 1:
        return blocks[0].reshape(shape)
    if copies and axis <= blocks[0].ndim - 2 and shape[-2] % 16 == 0 and shape[-1] >= LANES:
        return pl.pallas_call(
            functools.partial(order_kernel, count, axis),
            grid_spec=pltpu.PrefetchScalarGridSpec(
                num_scalar_prefetch=1,
                grid=(1,),
                in_specs=[pl.BlockSpec(memory_space=pl.ANY)] * count,
                out_specs=pl.BlockSpec(memory_space=pltpu.VMEM),
                scratch_shapes=[pltpu.SemaphoreType.DMA((count,))],
            ),
            out_shape=jax.ShapeDtypeStruct(tuple(shape), blocks[0].dtype),
            compiler_params=pltpu.CompilerParams(vmem_limit_bytes=4 * 1024 * 1024),
            name="order_blocks",
        )(index.reshape(1).astype(jnp.int32), *blocks)
    place = lax.broadcasted_iota(jnp.int32, shape, axis) ^ index
    result = jnp.expand_dims(blocks[0], axis)
    for d in range(1, count):
        result = jnp.where(place == d, jnp.expand_dims(blocks[d], axis), result)
    return jnp.broadcast_to(result, shape)


def beside(blocks, index):
    count = len(blocks)
    if count == 2:
        return jnp.where(
            index == 0, jnp.concatenate(blocks, axis=-1), jnp.concatenate(blocks[::-1], axis=-1)
        )
    return jnp.concatenate(
        [pick(order(blocks, index, 0), i, 0) for i in range(count)], axis=-1
    )


def sum_all(place, block, micro=True, part=True, tensor=True):
    if part and tensor and place.parts == place.tensors == 2:
        block = (block + place.swap_part(block, 1)) + (place.swap_tensor(block, 1) + place.swap_both(block))
    else:
        if part:
            for mask in bits_of(place.parts):
                block = block + place.swap_part(block, mask)
        if tensor:
            for mask in bits_of(place.tensors):
                block = block + place.swap_tensor(block, mask)
    if micro and place.micros == 4:
        block = (block + place.swap_micro(block, 1)) + (place.swap_micro(block, 2) + place.swap_micro(block, 3))
    elif micro:
        for mask in bits_of(place.micros):
            block = block + place.swap_micro(block, mask)
    return block


def lay_kernel(sizes, widths, places_ref, *refs):
    pieces, outs, sems = refs[: len(sizes)], refs[len(sizes) : -1], refs[-1]
    copies, number = [], 0
    for piece, size in zip(pieces, sizes):
        for row in range(size):
            at = 0
            for k, lanes in enumerate(widths):
                copies.append(
                    pltpu.make_async_copy(
                        piece.at[row, :, pl.ds(at, lanes)], outs[k].at[places_ref[number]], sems.at[number, k]
                    )
                )
                at += lanes
            number += 1
    for one in copies:
        one.start()
    for one in copies:
        one.wait()


def lay_rows(pieces, places, widths):
    rows = pieces[0].shape[1]
    sizes = [piece.shape[0] for piece in pieces]
    count = sum(sizes)
    if any(lanes % LANES for lanes in widths):
        whole = jnp.zeros((count,) + pieces[0].shape[1:], pieces[0].dtype)
        for i, row in enumerate(row for piece in pieces for row in piece):
            whole = lax.dynamic_update_index_in_dim(whole, row, places[i], 0)
        whole = whole.reshape(count * rows, -1)
        starts = [sum(widths[:k]) for k in range(len(widths))]
        return [whole[:, at : at + lanes] for at, lanes in zip(starts, widths)]
    results = pl.pallas_call(
        functools.partial(lay_kernel, sizes, widths),
        grid_spec=pltpu.PrefetchScalarGridSpec(
            num_scalar_prefetch=1,
            grid=(1,),
            in_specs=[pl.BlockSpec(memory_space=pl.ANY)] * len(pieces),
            out_specs=[pl.BlockSpec(memory_space=pltpu.VMEM)] * len(widths),
            scratch_shapes=[pltpu.SemaphoreType.DMA((count, len(widths)))],
        ),
        out_shape=[jax.ShapeDtypeStruct((count, rows, lanes), pieces[0].dtype) for lanes in widths],
        compiler_params=pltpu.CompilerParams(vmem_limit_bytes=4 * 1024 * 1024),
        name="lay_rows",
    )(jnp.stack(places).astype(jnp.int32), *pieces)
    return [result.reshape(count * rows, -1) for result in results]


class Collect:
    def __init__(self, place, blocks):
        self.place = place
        self.found = [[block] for block in blocks]
        self.distances = [[0] for _ in blocks]
        self.masks = [bits_of(place.micros)[:: -1 if p % 2 else 1] for p in range(len(blocks))]

    def prepare(self):
        self.out = [found[0] if len(found) == 1 else jnp.concatenate(found, axis=0) for found in self.found]

    def launch(self):
        self.next = [self.place.swap_micro(block, masks[0]) for block, masks in zip(self.out, self.masks)]

    def land(self):
        for p, block in enumerate(self.next):
            mask = self.masks[p].pop(0)
            self.found[p].append(block)
            self.distances[p] += [distance ^ mask for distance in self.distances[p]]

    def finish(self):
        while self.masks[0]:
            self.prepare()
            self.launch()
            self.land()

    def result(self, widths):
        place, pieces, places = self.place, [], []
        for p, found in enumerate(self.found):
            pieces += found
            places += [(place.micro ^ distance) * place.parts + (place.part ^ p) for distance in self.distances[p]]
        return lay_rows(pieces, places, widths)


def gather_weights(place, w_gate, w_value, w_bc, w_dt, w_out):
    parts = place.parts
    width = w_gate.shape[1] // parts
    heads = w_dt.shape[1] // parts

    def cut_of(array, part):
        return lax.dynamic_slice_in_dim(array, part * width, width, 1)

    def columns_of(part):
        steps = lax.dynamic_slice_in_dim(w_dt, part * heads, heads, 1)
        steps = jnp.pad(steps, ((0, 0), (0, LANES - heads)))
        return jnp.concatenate([cut_of(w_value, part), w_bc, steps, cut_of(w_gate, part)], axis=1)[None]

    def collected(make):
        blocks = [make(place.part ^ p) for p in range(parts)]
        return Collect(place, blocks[:1] + [place.swap_part(block, p + 1) for p, block in enumerate(blocks[1:])])

    first = collected(columns_of)
    second = collected(lambda part: cut_of(w_out.T, part)[None])
    return first, second


def whole_tokens(place, rows):
    return [pick(rows, place.micro, 0)] + [
        place.swap_micro(pick(rows, place.micro ^ d, 0), d) for d in range(1, place.micros)
    ]


def lay_tokens(place, blocks):
    held = order(blocks, place.micro, 0, False)
    whole = order([held] + [place.swap_part(held, d) for d in range(1, place.parts)], place.part, 1, False)
    size = place.micros // PIECES
    return [whole[i * size : (i + 1) * size].reshape(-1, held.shape[-1]) for i in range(PIECES)]


class Spread:
    def __init__(self, place, rows):
        self.place, self.rows = place, rows
        micros, count, width = rows.shape
        view = rows.reshape(micros, place.tensors, count // place.tensors, width)
        self.shares = jnp.stack(
            [place.swap_micro(pick(pick(view, place.micro ^ d, 0), place.tensor, 0), d) for d in range(1, micros)]
        )
        self.came = [place.swap_tensor(self.shares, d) for d in range(1, place.tensors)]

    def result(self):
        place = self.place
        both = [self.shares] + self.came
        blocks = [pick(self.rows, place.micro, 0)]
        for d in range(place.micros - 1):
            whole = order([part[d] for part in both], place.tensor, 0, False)
            blocks.append(whole.reshape(-1, self.rows.shape[2]))
        return lay_tokens(place, blocks)


def blocks_of(place, array):
    return array.reshape(place.micros // PIECES, place.parts, place.tensors, -1, array.shape[-1])


def own_share(place, array, flip=0):
    return pick(pick(blocks_of(place, array), place.part, 1), place.tensor ^ flip, 1)


GROUP = 16


def split_kernel(parts, tensors, tensor_ref, own_ref, *refs):
    came, going_ref, kept_ref = refs[: parts - 1], refs[-2], refs[-1]
    rows = kept_ref.shape[1]

    def group(i, _):
        here = pl.ds(pl.multiple_of(i * GROUP, GROUP), GROUP)
        for d in range(tensors):
            start = (tensor_ref[0] ^ d) * rows + i * GROUP
            there = pl.ds(pl.multiple_of(start, GROUP), GROUP)
            total = own_ref[0, there, :]
            for one in came:
                total = total + one[0, there, :].astype(f32)
            if d:
                going_ref[d - 1, 0, here, :] = total.astype(bf16)
            else:
                kept_ref[0, here, :] = total
        return 0

    lax.fori_loop(0, rows // GROUP, group, 0)


def split_call(place, own, came):
    blocks, tokens, depth = own.shape
    rows = tokens // place.tensors
    others = place.tensors - 1
    return pl.pallas_call(
        functools.partial(split_kernel, place.parts, place.tensors),
        grid_spec=pltpu.PrefetchScalarGridSpec(
            num_scalar_prefetch=1,
            grid=(blocks,),
            in_specs=[pl.BlockSpec((1, tokens, depth), lambda b, _: (b, 0, 0))] * place.parts,
            out_specs=[
                pl.BlockSpec((others, 1, rows, depth), lambda b, _: (0, b, 0, 0)),
                pl.BlockSpec((1, rows, depth), lambda b, _: (b, 0, 0)),
            ],
        ),
        out_shape=[
            jax.ShapeDtypeStruct((others, blocks, rows, depth), bf16),
            jax.ShapeDtypeStruct((blocks, rows, depth), f32),
        ],
        compiler_params=pltpu.CompilerParams(vmem_limit_bytes=8 * 1024 * 1024),
        name="split_terms",
    )(place.tensor.reshape(1), own, *came)


def finish_kernel(places_ref, kept_ref, h_ref, e_ref, norm_ref, *refs):
    sent, grad_ref, sum_ref = refs[:-2], refs[-2], refs[-1]
    rows = kept_ref.shape[1]

    @pl.when(pl.program_id(0) == 0)
    def _():
        sum_ref[...] = jnp.zeros_like(sum_ref)

    def group(i, _):
        here = pl.ds(pl.multiple_of(i * GROUP, GROUP), GROUP)
        dxn = kept_ref[0, here, :]
        for one in sent:
            dxn = dxn + one[0, here, :].astype(f32)
        h = h_ref[0, 0, 0, here, :].astype(f32)
        r = lax.rsqrt(jnp.mean(h * h, axis=1, keepdims=True) + epsilon)
        scaled = dxn * norm_ref[...]
        pull = r * r * r * jnp.mean(scaled * h, axis=1, keepdims=True)
        grad_ref[0, here, :] = (e_ref[0, 0, 0, here, :].astype(f32) + r * scaled - h * pull).astype(bf16)
        found = dxn * h * r
        sum_ref[...] += found[0:8] + found[8:16]
        return 0

    lax.fori_loop(0, rows // GROUP, group, 0)


def finish_call(place, kept, sent, h, e, norm_gain):
    blocks, rows, depth = kept.shape
    share = pl.BlockSpec((1, rows, depth), lambda b, _: (b, 0, 0))
    whole = pl.BlockSpec((1, 1, 1, rows, depth), lambda b, places: (b, places[0], places[1], 0, 0))
    return pl.pallas_call(
        finish_kernel,
        grid_spec=pltpu.PrefetchScalarGridSpec(
            num_scalar_prefetch=1,
            grid=(blocks,),
            in_specs=[share, whole, whole, pl.BlockSpec((1, depth), lambda b, _: (0, 0))] + [share] * len(sent),
            out_specs=[share, pl.BlockSpec((8, depth), lambda b, _: (0, 0))],
        ),
        out_shape=[jax.ShapeDtypeStruct(kept.shape, bf16), jax.ShapeDtypeStruct((8, depth), f32)],
        compiler_params=pltpu.CompilerParams(vmem_limit_bytes=8 * 1024 * 1024),
        name="finish_gradient",
    )(jnp.stack([place.part, place.tensor]), kept, blocks_of(place, h), blocks_of(place, e), norm_gain[None], *sent)


def deal_kernel(parts, widths, rounds, part_ref, *refs):
    mine_ref, send_ref = refs[-2], refs[-1]
    each = len(widths) + rounds
    rows = mine_ref.shape[0]

    def group(i, _):
        here = pl.ds(pl.multiple_of(i * GROUP, GROUP), GROUP)
        for p in range(parts):
            arrays = refs[p * each : (p + 1) * each]
            total = jnp.concatenate([one[here, :].astype(f32) for one in arrays[: len(widths)]], axis=1)
            for one in arrays[len(widths) :]:
                total = total + one[here, :].astype(f32)
            distance = part_ref[0] ^ p

            @pl.when(distance == 0)
            def _():
                mine_ref[here, :] = total

            @pl.when(distance != 0)
            def _():
                send_ref[jnp.maximum(distance - 1, 0), here, :] = total.astype(bf16)

        return 0

    lax.fori_loop(0, rows // GROUP, group, 0)


def deal_call(place, groups, came):
    widths = [block.shape[-1] for block in groups[0]]
    rows, total = groups[0][0].shape[0], sum(widths)
    args = [one for held, round_ in zip(groups, came) for one in list(held) + list(round_)]
    others = place.parts - 1
    step = 3 * GROUP
    return pl.pallas_call(
        functools.partial(deal_kernel, place.parts, widths, len(came[0])),
        grid_spec=pltpu.PrefetchScalarGridSpec(
            num_scalar_prefetch=1,
            grid=(rows // step,),
            in_specs=[pl.BlockSpec((step, one.shape[1]), lambda i, _: (i, 0)) for one in args],
            out_specs=[
                pl.BlockSpec((step, total), lambda i, _: (i, 0)),
                pl.BlockSpec((others, step, total), lambda i, _: (0, i, 0)),
            ],
        ),
        out_shape=[jax.ShapeDtypeStruct((rows, total), f32), jax.ShapeDtypeStruct((others, rows, total), bf16)],
        compiler_params=pltpu.CompilerParams(vmem_limit_bytes=8 * 1024 * 1024),
        name="deal_rows",
    )(place.part.reshape(1), *args)


def beside_kernel(parts, at, part_ref, *refs):
    blocks, out_ref = refs[:parts], refs[-1]
    rows, width = out_ref.shape[0], out_ref.shape[1] // parts

    def group(i, _):
        here = pl.ds(pl.multiple_of(i * GROUP, GROUP), GROUP)
        for d, one in enumerate(blocks):
            there = pl.ds(pl.multiple_of((part_ref[0] ^ d) * width, LANES), width)
            out_ref[here, there] = one[here, at : at + width].astype(f32)
        return 0

    lax.fori_loop(0, rows // GROUP, group, 0)


def columns_beside(place, blocks, at, width):
    if width % LANES or at % LANES:
        return beside([block[:, at : at + width].astype(f32) for block in blocks], place.part)
    shape = (blocks[0].shape[0], place.parts * width)
    step = 3 * GROUP
    return pl.pallas_call(
        functools.partial(beside_kernel, place.parts, at),
        grid_spec=pltpu.PrefetchScalarGridSpec(
            num_scalar_prefetch=1,
            grid=(shape[0] // step,),
            in_specs=[pl.BlockSpec((step, block.shape[1]), lambda i, _: (i, 0)) for block in blocks],
            out_specs=pl.BlockSpec((step, shape[1]), lambda i, _: (i, 0)),
        ),
        out_shape=jax.ShapeDtypeStruct(shape, f32),
        compiler_params=pltpu.CompilerParams(vmem_limit_bytes=8 * 1024 * 1024),
        name="columns_beside",
    )(place.part.reshape(1), *blocks)


def cut(place, block):
    return block.reshape(block.shape[:-2] + (place.tensors, -1, block.shape[-1]))


class Reduction:
    def __init__(self, place, own, send, kind=bf16):
        self.place, self.kind, self.going = place, kind, None
        sends = [send.reshape(own.shape)] if place.parts == 2 else [send[d] for d in range(place.parts - 1)]
        self.came = [place.swap_part(block, d + 1) for d, block in enumerate(sends)]
        self.own = own

    def prepare(self):
        place = self.place
        if self.kind == bf16:
            going, self.kept = split_call(place, self.own, self.came)
            self.going = [going.reshape(self.kept.shape)] if place.tensors == 2 else list(going)
        else:
            own, came = cut(place, self.own), [cut(place, block) for block in self.came]

            def side(tensor):
                return pick(own, tensor, 1) + sum(pick(block, tensor, 1).astype(f32) for block in came)

            self.going = [side(place.tensor ^ d).astype(self.kind) for d in range(1, place.tensors)]
            self.kept = side(place.tensor)

    def launch(self, others=None):
        if self.going is None:
            self.prepare()
        self.going, others = tie(self.going, others)
        self.sent = [self.place.swap_tensor(block, d + 1) for d, block in enumerate(self.going)]
        return others

    def land(self, others):
        self.sent, others = tie(self.sent, others)
        return others

    def result(self):
        return self.kept + sum(block.astype(f32) for block in self.sent)


class Gathering:
    def __init__(self, place, shares, flip=0):
        self.place, self.shares, self.flip = place, shares, flip
        self.came = None

    def launch(self):
        place = self.place
        self.came = [[place.swap_tensor(share, d) for share in self.shares] for d in range(1, place.tensors)]

    def result(self):
        place = self.place
        came = tie(self.came)[0]
        held = [order(list(group), place.tensor ^ self.flip, 1) for group in zip(self.shares, *came)]
        came = tie([[place.swap_part(block, d) for block in held] for d in range(1, place.parts)])[0]
        whole = [order(list(group), place.part, 1) for group in zip(held, *came)]
        return [block.reshape((-1,) + share.shape[2:]) for block, share in zip(whole, self.shares)]


def gather_shares(place, shares, flip=0):
    gathering = Gathering(place, shares, flip)
    gathering.launch()
    return gathering.result()


class Homing:
    def __init__(self, place, own):
        self.place = place
        self.rows = None
        self.own = pick(own, place.micro, 0)
        self.sends = [pick(own, place.micro ^ d, 0) for d in range(1, place.micros)]

    def launch(self):
        self.came = [self.place.swap_micro(block, d + 1) for d, block in enumerate(self.sends)]

    def collect(self):
        self.rows = order([self.own] + self.came, self.place.micro, 0)

    def turn(self, others=None):
        place = self.place
        if self.rows is None:
            self.collect()
        self.rows, others = tie(self.rows, others)
        self.swapped = [place.swap_tensor(self.rows, d) for d in range(1, place.tensors)]
        return others

    def result(self):
        return order([self.rows] + self.swapped, self.place.tensor, 1)


def rows_dot(a, b):
    return jnp.dot(a, b, preferred_element_type=f32)


def columns_dot(a, b):
    return lax.dot_general(a, b, (((0,), (0,)), ((), ())), preferred_element_type=f32)


def forward_piece(place, h, weights, small, carry, dn=None):
    results = forward_call(place, h, weights, small, carry[0], carry[1], dn)
    if dn is None:
        return results[:2], (results[2], results[3])
    kept = (h, carry[1]) + tuple(results[5:])
    return results[:3], (results[3], results[4]), kept


def forward_start(place, small):
    width = small[3].shape[1]
    return jnp.zeros((STATE, width), f32), jnp.zeros((8, width + MAPS), f32)


def factor_of(place, small, squares):
    return lax.rsqrt(squares / (place.tensors * place.parts * small[3].shape[1]) + epsilon)


def out_share(place, h, branch):
    return (own_share(place, h).astype(f32) + branch).astype(bf16)


def gates_piece(place, dn, q, pull, kept, small):
    _, _, _, _, z, y, _ = kept
    return gate_call(place, dn, z, y, q[:, None], pull[:, None], small[3])


def normal_piece(e, q, kept, weights, small):
    _, _, _, _, z, y, _ = kept
    dn, pull, n, gain = normal_call(e, weights, z, y, q[:, None], small[3])
    return dn, pull[:, 0], n, gain


def backward_piece(place, exact, gates, kept, weights, small, carry):
    _, before, _, vbd, _, _, states = kept
    mixed = small[3].shape[1] + MAPS
    count = min(STEP * CHUNK, vbd.shape[0])
    tails = vbd.reshape(-1, count, vbd.shape[1])[:-1, count - 8 :, :mixed]
    before = jnp.concatenate([before[None], tails], axis=0)
    own, send, dvbd, adjoint, du, sums = backward_call(
        place, exact, gates[0], gates[1], vbd, before, states, weights, small, carry[0], carry[1]
    )
    return (own, send), (adjoint, du), dvbd, sums


def input_grad(place, e, h, norm_gain, item):
    return finish_call(place, item.kept, item.sent, h, e, norm_gain)


class Scatter:
    def __init__(self, place, arrays):
        self.place = place
        parts = place.parts
        shape = [2] * len(bits_of(place.micros))
        views = [array.reshape(place.micros, parts, -1, array.shape[1]) for array in arrays]
        self.held = [[view[:, p].reshape(shape + list(view.shape[2:])) for view in views] for p in range(parts)]
        self.came = [[] for _ in range(parts)]
        self.left = [sorted(bits_of(place.micros), reverse=True) for _ in range(parts)]

    def prepare(self):
        place = self.place
        self.out, self.masks = [], []
        for p, left in enumerate(self.left):
            mask = left[0] if p % 2 else left[-1]
            axis = left.index(mask)
            mine = (place.micro // mask) % 2

            def side(bit):
                total = jnp.concatenate([pick(block, bit, axis) for block in self.held[p]], axis=-1)
                for block in self.came[p]:
                    total = total.astype(f32) + pick(block, bit, axis).astype(f32)
                return total.astype(bf16)

            self.out.append(side(1 - mine))
            self.masks.append(mask)
            self.held[p] = [pick(block, mine, axis) for block in self.held[p]]
            self.came[p] = [pick(block, mine, axis) for block in self.came[p]]
            left.remove(mask)

    def launch(self):
        self.next = [self.place.swap_micro(block, mask) for block, mask in zip(self.out, self.masks)]

    def land(self):
        for p, block in enumerate(self.next):
            self.came[p].append(block)

    def trade(self):
        place = self.place
        mine, send = deal_call(place, self.held, self.came)
        sends = [send.reshape(mine.shape)] if place.parts == 2 else list(send)
        return [mine] + [place.swap_part(block, d + 1) for d, block in enumerate(sends)]


def body(
    block_input,
    norm_gain,
    w_gate,
    w_value,
    w_bc,
    w_dt,
    conv_value,
    conv_bc,
    conv_value_bias,
    conv_bc_bias,
    dt_bias,
    decay_log,
    skip,
    gate_gain,
    w_out,
    cotangent,
):
    sections = lax.axis_size("section")
    section = lax.axis_index("section")
    place = Place(block_input.shape[0])
    parts, part = place.parts, place.part
    width = w_gate.shape[2] // parts
    heads_here = w_dt.shape[2] // parts
    mixed = width + MAPS

    def share(vector, size):
        return lax.dynamic_slice_in_dim(vector, part * size, size, vector.ndim - 1)

    def padded(vector):
        return jnp.pad(vector, (0, head_rows(width) - heads_here))

    spread = Spread(place, block_input)
    collected, second = gather_weights(place, w_gate[0], w_value[0], w_bc[0], w_dt[0], w_out[0])
    collected.prepare()
    collected.launch()
    spread.came, collected.next = tie(spread.came, collected.next)
    collected.land()
    h0 = spread.result()
    while collected.masks[0]:
        collected.prepare()
        collected.launch()
        h0, collected.next = tie(h0, collected.next)
        collected.land()
    weights = tuple(collected.result([mixed + LANES, width]))
    taps = jnp.concatenate(
        [
            jnp.concatenate([share(conv_value[0], width), conv_bc[0]], axis=1),
            jnp.concatenate([share(conv_value_bias[0], width), conv_bc_bias[0]])[None],
            jnp.zeros((8 - CONV - 1, mixed), f32),
        ],
        axis=0,
    )
    own_skip = share(skip[0], heads_here)
    rate = jnp.exp(share(decay_log[0], heads_here))
    heads = jnp.concatenate([padded(share(dt_bias[0], heads_here)), padded(rate)])
    heads = jnp.broadcast_to(heads[:, None], (heads.size, LANES))
    inner = jnp.stack([jnp.repeat(own_skip, HEAD_DIM), share(gate_gain[0], width)])
    inner = jnp.concatenate([inner, jnp.zeros((6, width), f32)], axis=0)
    small = (norm_gain[0], taps, heads, inner)

    span = range(PIECES)
    first, last = section == 0, section == sections - 1
    flip = 1 if place.tensors > 1 else 0

    def leave(place_of, block, came, step, others):
        if came:
            newest = list(came)[-1]
            block, came[newest], others = tie(block, came[newest], others)
        else:
            block, others = tie(block, others)
        came[place_of] = place.next_section(block, step, flip if step > 0 else 0)
        return others

    def arrive(i, came, stays, originals, others, flip):
        block, others = tie(came[i], others)
        return jnp.where(stays, own_share(place, originals[i], flip), block), others

    came = None
    for turn in range(sections - 1):
        carry = forward_start(place, small)
        shares_in, came = came, {}
        pieces, halves, terms, crossing = list(h0), [], None, []
        for i in span:
            if shares_in is not None:
                share, terms = arrive(i, shares_in, first, h0, terms, flip)
                pieces[i] = gather_shares(place, [share], flip)[0]
            if i:
                pieces[i], halves[-1][1] = tie(pieces[i], halves[-1][1])
                crossing = [place.swap_tensor(halves[-1][1], mask) for mask in bits_of(place.tensors)]
            if second.masks[0]:
                second.prepare()
                pieces[i], second.out = tie(pieces[i], second.out)
                second.launch()
                terms, carry = forward_piece(place, pieces[i], weights, small, carry)
                terms, crossing, second.next = tie(terms, crossing, second.next)
                second.land()
            else:
                terms, carry = forward_piece(place, pieces[i], weights, small, carry)
                terms, crossing = tie(terms, crossing)
            if i:
                halves[-1][1] = halves[-1][1] + sum(crossing)
            halves.append([terms[0], sum_all(place, terms[1][0, :, 0], micro=False, tensor=False)])
        halves[-1][1] = sum_all(place, halves[-1][1], micro=False, part=False)
        second.finish()
        if len(weights) == 2:
            weights += tuple(second.result([width]))
        red = []
        for g, squares in halves:
            if red:
                g = red[-1].launch(g)
            elif turn == 0:
                g, cotangent = tie(g, cotangent)
                e_blocks = whole_tokens(place, cotangent)
            own, send = out_call(place, g, factor_of(place, small, squares), weights, small[3])
            red.append(Reduction(place, own, send, jnp.float16))
        red[-1].launch()
        if turn == 0:
            e_blocks = red[0].land(e_blocks)
            e0 = lay_tokens(place, e_blocks)
            e0, dn0 = red[-1].land((e0, [rows_dot(e, weights[2]) for e in e0]))
        for i, item in enumerate(red):
            leave(i, out_share(place, pieces[i], item.result()), came, 1, None)
    second.finish()
    if len(weights) == 2:
        weights += tuple(second.result([width]))
    if sections == 1:
        e0 = lay_tokens(place, whole_tokens(place, cotangent))
        dn0 = [rows_dot(e, weights[2]) for e in e0]

    carry = forward_start(place, small)
    kept, sums, lines, terms, ahead = [], [], [], None, None
    for i in span:
        h = h0[i]
        if came is not None:
            if ahead is None:
                share, terms = arrive(i, came, first, h0, terms, flip)
                ahead = Gathering(place, [share], flip)
                ahead.launch()
                if i + 1 < PIECES:
                    ahead.came, came[i + 1] = tie(ahead.came, came[i + 1])
            h = ahead.result()[0]
            ahead = None
            if i + 1 < PIECES:
                share, h = arrive(i + 1, came, first, h0, h, flip)
                h, share = tie(h, share)
                ahead = Gathering(place, [share], flip)
                ahead.launch()
        terms, carry, keep = forward_piece(place, h, weights, small, carry, dn0[i])
        if ahead is not None:
            terms, ahead.came = tie(terms, ahead.came)
        kept.append(keep)
        lines.append(terms[2][:, :, 0])
        sums.append(Reduction(place, terms[0], terms[1]))
    lines = sum_all(place, jnp.stack(lines), micro=False)
    qs = [factor_of(place, small, lines[i, 0]) for i in span]
    dots = [lines[i, 1] for i in span]

    def gradient_of(i, came, others):
        share, others = arrive(i, came, last, e0, others, 0)
        gathering = Gathering(place, [share])
        gathering.launch()
        return gathering, others

    def outputs_of():
        outs = []
        for k in span:
            branch = sums[k].result() * own_share(place, qs[k].reshape(-1, 1))
            outs.append(out_share(place, kept[k][0], branch))
        return Homing(place, jnp.concatenate(outs, axis=0))

    came, homing, ready = None, None, None
    es = list(e0)
    for turn in range(sections - 1):
        carry = forward_start(place, small)
        shares_in, came = came, {}
        es, terms = list(e0), None
        for i in reversed(span):
            dn, pull = dn0[i], dots[i]
            if shares_in is not None:
                ready, terms = gradient_of(i, shares_in, terms)
                es[i] = ready.result()[0]
                dn, pull, _, _ = normal_piece(es[i], qs[i], kept[i], weights, small)
                pull = sum_all(place, pull, micro=False)
            elif homing is None:
                for item in sums:
                    dn = item.launch(dn)
            gates = gates_piece(place, dn, qs[i], pull, kept[i], small)
            if i + 1 < PIECES:
                gates = leave(i + 1, share, came, -1, gates)
            terms, carry, _, _ = backward_piece(place, False, gates, kept[i], weights, small, carry)
            if i + 1 < PIECES:
                terms, came[i + 1] = tie(terms, came[i + 1])
            if homing is None:
                for item in sums:
                    terms = item.land(terms)
            red = Reduction(place, terms[0], terms[1])
            red.launch()
            if homing is None:
                homing = outputs_of()
            if not i and turn == sections - 2 and PIECES > 1:
                ready, _ = gradient_of(PIECES - 1, came, None)
                ready.came = red.land(ready.came)
            share, _ = input_grad(place, es[i], kept[i][0], norm_gain[0], red)
        leave(0, share, came, -1, None)
    if homing is None:
        for item in sums:
            item.launch()
        homing = outputs_of()

    carry = forward_start(place, small)
    red, matrix, small_sums, terms = [], [None] * 3, None, None

    def add(old, a, b):
        now = columns_dot(a, b)
        return now if old is None else old + now

    for i in reversed(span):
        if came is not None:
            if red or ready is None:
                ready, terms = gradient_of(i, came, terms)
            if red:
                red[-1].prepare()
                homing.collect()
                ready.came, red[-1].going, homing.rows = tie(ready.came, red[-1].going, homing.rows)
            es[i] = ready.result()[0]
        dn, pull, n, gain_grad = normal_piece(es[i], qs[i], kept[i], weights, small)
        pull = sum_all(place, pull, micro=False)
        matrix[0] = add(matrix[0], es[i], n)
        pull, matrix[0] = tie(pull, matrix[0])
        if red:
            pull = homing.turn(red[-1].launch(pull))
        else:
            pull, homing.sends = tie(pull, homing.sends)
            homing.launch()
        gates = gates_piece(place, dn, qs[i], pull, kept[i], small)
        if not i:
            scatter = Scatter(place, [matrix[0].astype(bf16), add(matrix[1], kept[i][2], gates[1]).astype(bf16)])
            scatter.prepare()
            gates, scatter.out = tie(gates, scatter.out)
            scatter.launch()
        terms, carry, dvbd, now = backward_piece(place, True, gates, kept[i], weights, small, carry)
        if red:
            terms = red[-1].land(terms)
        else:
            homing.came, terms, gates, dvbd, now = tie(homing.came, terms, gates, dvbd, now)
            if PIECES == 1:
                homing.turn()
        now = [now, gain_grad]
        if i:
            red.append(Reduction(place, terms[0], terms[1]))
            for k, b in ((1, gates[1]), (2, dvbd)):
                matrix[k] = add(matrix[k], kept[i][2], b)
        else:
            ahead = Reduction(place, terms[0], terms[1])
            ahead.own, dvbd, now, scatter.next, homing.swapped = tie(
                ahead.own, dvbd, now, scatter.next, homing.swapped
            )
            scatter.land()
            red.append(ahead)
        small_sums = now if small_sums is None else [a + b for a, b in zip(small_sums, now)]
    outputs = homing.result().reshape(block_input.shape)
    scatter.prepare()
    scatter.launch()
    red[-1].prepare()
    red[-1].going, dvbd = tie(red[-1].going, dvbd)
    red[-1].launch()
    mixes = Scatter(place, [add(matrix[2], kept[0][2], dvbd).astype(bf16)])
    mixes.prepare()
    mixes.launch()
    grads, norm_grad = [], jnp.zeros((8, norm_gain.shape[1]), f32)
    for i, item in zip(reversed(span), red[:-1]):
        block, now = input_grad(place, es[i], kept[i][0], norm_gain[0], item)
        grads.insert(0, block)
        norm_grad = norm_grad + now
    scatter.next = red[-1].land(scatter.next)
    scatter.land()
    while scatter.left[0]:
        scatter.prepare()
        scatter.launch()
        scatter.land()
    block, now = input_grad(place, es[0], kept[0][0], norm_gain[0], red[-1])
    norm_grad = norm_grad + now
    homing = Homing(place, jnp.concatenate([block] + grads, axis=0))
    homing.launch()
    scatter = scatter.trade()
    gate_grad = columns_beside(place, scatter, width, width)
    out_grad = order([block[:, :width].astype(f32).T for block in scatter], part, 0).reshape(-1, w_out.shape[2])
    homing.came, mixes.next, gate_grad, out_grad, outputs = tie(
        homing.came, mixes.next, gate_grad, out_grad, outputs
    )
    mixes.land()
    mixes.prepare()
    homing.collect()
    mixes.out, homing.rows = tie(mixes.out, homing.rows)
    homing.turn()
    mixes.launch()
    packed, gain_grad = small_sums
    norm_grad = jnp.sum(norm_grad, axis=0)
    row = lax.broadcasted_iota(jnp.int32, (8, mixed), 0)
    packed = jnp.where(row == GAIN_ROW, jnp.pad(gain_grad, ((0, 0), (0, MAPS))), packed)
    lanes = max(mixed, norm_grad.size)
    packed = jnp.concatenate(
        [jnp.pad(packed, ((0, 0), (0, lanes - mixed))), jnp.pad(norm_grad[None], ((0, 7), (0, lanes - norm_grad.size)))],
        axis=0,
    )
    mixes.land()
    while mixes.left[0]:
        mixes.prepare()
        mixes.launch()
        mixes.land()
    mixes = mixes.trade()
    packed, mixes = tie(packed, mixes)
    packed = sum_all(place, packed, part=False, tensor=False)
    by_part = [packed] + [place.swap_part(packed, d) for d in range(1, parts)]
    input_grads = homing.result().reshape(block_input.shape).astype(f32)
    value_grad = columns_beside(place, mixes, 0, width)
    step_grad = beside([block[:, mixed : mixed + heads_here].astype(f32) for block in mixes], part)
    maps_grad = sum(block[:, width:mixed].astype(f32) for block in mixes).astype(bf16)
    maps_sum = maps_grad.astype(f32)
    for mask in bits_of(place.tensors):
        maps_sum = maps_sum + place.swap_tensor(maps_sum, mask)

    both = sum_all(place, packed, micro=False)
    wide, bias_grad, gain_grad, maps_small, maps_bias, norm_sum, by_head = unpack(
        place, both, by_part, width, heads_here, norm_grad.size
    )
    total_heads = parts * heads_here
    return (
        outputs[None],
        input_grads[None],
        norm_sum,
        gate_grad[None],
        value_grad[None],
        maps_sum[None],
        step_grad[None],
        wide[None],
        maps_small[None],
        bias_grad,
        maps_bias,
        by_head[0:1, :total_heads],
        by_head[1:2, :total_heads],
        by_head[2:3, :total_heads],
        gain_grad,
        out_grad[None],
    )


def solution(mesh):
    placed = (
        P(None, "context", None),
        P("section", None),
        P("section", "context", "tensor"),
        P("section", "context", "tensor"),
        P("section", "context", None),
        P("section", "context", "tensor"),
        P("section", None, "tensor"),
        P("section", None, None),
        P("section", "tensor"),
        P("section", None),
        P("section", "tensor"),
        P("section", "tensor"),
        P("section", "tensor"),
        P("section", "tensor"),
        P("section", "tensor", "context"),
        P(None, "context", None),
    )
    return jax.shard_map(
        body,
        mesh=mesh,
        in_specs=placed,
        out_specs=(
            P("section", None, "context", None),
            P("section", None, "context", None),
            P("section", None),
            P("section", "context", "tensor"),
            P("section", "context", "tensor"),
            P("section", "context", None),
            P("section", "context", "tensor"),
            P("section", None, "tensor"),
            P("section", None, None),
            P("section", "tensor"),
            P("section", None),
            P("section", "tensor"),
            P("section", "tensor"),
            P("section", "tensor"),
            P("section", "tensor"),
            P("section", "tensor", "context"),
        ),
        check_vma=False,
    )
```
